32 devices in a mesh: dp: 16 (over z, y, x), mp: 2 (over core).
Axes of the slice: x: 2, y: 2, z: 4, core: 2. Of those that a mesh axis runs over, the one named last changes fastest.
Arguments:
- inputs: bfloat16 [16384, 1024], P(('dp', 'mp')), may hold values from -6 to 6
- first_gain: float32 [1024], replicated, may hold values from 0.25 to 1.75
- first_shift: float32 [1024], replicated, may hold values from -2 to 2
- query_weight: bfloat16 [1024, 1024], P(None, 'mp'), may hold values from -0.1875 to 0.1875
- key_weight: bfloat16 [1024, 1024], P(None, 'mp'), may hold values from -0.1875 to 0.1875
- value_weight: bfloat16 [1024, 1024], P(None, 'mp'), may hold values from -0.1875 to 0.1875
- output_weight: bfloat16 [1024, 1024], P('mp'), may hold values from -4 to 4
- second_gain: float32 [1024], replicated, may hold values from 0.25 to 1.75
- second_shift: float32 [1024], replicated, may hold values from -2 to 2
- gate_weight: bfloat16 [1024, 4096], P(None, 'mp'), may hold values from -0.1875 to 0.1875
- up_weight: bfloat16 [1024, 4096], P(None, 'mp'), may hold values from -0.1875 to 0.1875
- down_weight: bfloat16 [4096, 1024], P('mp'), may hold values from -0.09375 to 0.09375
- cotangent: bfloat16 [16384, 1024], P(('dp', 'mp')), may hold values from -6 to 6
- species_weight: float32 [850], replicated, may hold values from 0.25 to 4
- species_ids: int32 [16], P('dp'), may hold values from 0 to 849, as said below
- slot_bucket: int32 [16], P('dp'), may hold values from 0 to 1, as said below
- slot_length: int32 [16], P('dp'), may hold values from 768 to 1024, as said below
Outputs:
- output: bfloat16 [16384, 1024], P(('dp', 'mp'))
- input_grad: float32 [16384, 1024], P(('dp', 'mp'))
- first_gain_grad: float32 [1024], P(('dp', 'mp'))
- first_shift_grad: float32 [1024], P(('dp', 'mp'))
- query_grad: float32 [1024, 1024], P('dp', 'mp')
- key_grad: float32 [1024, 1024], P('dp', 'mp')
- value_grad: float32 [1024, 1024], P('dp', 'mp')
- project_grad: float32 [1024, 1024], P('mp', 'dp')
- second_gain_grad: float32 [1024], P(('dp', 'mp'))
- second_shift_grad: float32 [1024], P(('dp', 'mp'))
- gate_grad: float32 [1024, 4096], P('dp', 'mp')
- up_grad: float32 [1024, 4096], P('dp', 'mp')
- down_grad: float32 [4096, 1024], P('mp', 'dp')
The draws below stay inside these ranges and needn't reach their ends.
Inputs may be any that keep to these rules, and one draw needn't show every extreme that they name: `slot_bucket`: slots 2p and 2p + 1 always have the same bucket; exactly half of these pairs (rounded down) are long windows. `slot_length`: every slot of a long window has length 1024; a short window's length is below 1024. `species_ids`: both slots of a long window carry the same species.
All inputs are finite; a program needn't handle non-finite values.
Results may differ from the reference program's by a relative error of at most 0.014.
Values may be sent and summed in bfloat16 or wider, within the bound.
No kernel may reach another device: no remote copies, remote signals or barrier semaphores. Data moves between devices by JAX's collectives and lax.ppermute only.
A program may use at most 384 MiB of HBM per device.

```python
import math
import jax
import jax.numpy as jnp
from jax import lax

D = 1024
HEADS = 16
HEAD_DIM = 64
FF = 4096
SLOT_LEN = 1024
SPECIES = 850
SLOTS = 16
TOKENS = 16384


def window_layout(key):
    base_key = jax.random.fold_in(key, 11)
    pair_count = SLOTS // 2
    ranking = jax.random.permutation(jax.random.fold_in(base_key, 1), pair_count)
    joined_pairs = (ranking < pair_count // 2).astype(jnp.int32)
    bucket = jnp.repeat(joined_pairs, 2)
    short_length = jax.random.randint(jax.random.fold_in(base_key, 2), (SLOTS,), SLOT_LEN - SLOT_LEN // 4, SLOT_LEN)
    length = jnp.where(bucket == 1, SLOT_LEN, short_length).astype(jnp.int32)
    pair_species = jax.random.randint(jax.random.fold_in(base_key, 3), (pair_count,), 0, SPECIES)
    slot_species = jax.random.randint(jax.random.fold_in(base_key, 4), (SLOTS,), 0, SPECIES)
    species = jnp.where(bucket == 1, jnp.repeat(pair_species, 2), slot_species).astype(jnp.int32)
    return (bucket.astype(jnp.int32), length, species)


def draw_slot_bucket(key, part):
    return window_layout(key)[0]


def draw_slot_length(key, part):
    return window_layout(key)[1]


def draw_species_ids(key, part):
    return window_layout(key)[2]


def with_spikes(drawn, own_key, source, target, parts, factor):
    owner, partner = [(jnp.arange(drawn.shape[position]) // (drawn.shape[position] // parts)).reshape([-1 if axis == position else 1 for axis in range(drawn.ndim)]) for position in (source, target)]
    chosen = jax.random.permutation(own_key, parts)[partner]
    strong = (owner == chosen) | (owner == (partner + parts // 2) % parts)
    return jnp.where(strong, factor * drawn, drawn)


def level_of(own_key, shape, cuts, low, high):
    def one(dim, blocks):
        heights = jax.random.uniform(jax.random.fold_in(jax.random.fold_in(own_key, 6), dim), (blocks,), jnp.float32, low / len(cuts), high / len(cuts))
        return jnp.repeat(jnp.exp(heights), shape[dim] // blocks).reshape((-1,) + (1,) * (len(shape) - dim - 1))

    gain = one(*cuts[0])
    for cut in cuts[1:]:
        gain = gain * one(*cut)
    return gain


def noise(key, shape, deviation, limit, cuts=(), kind=jnp.bfloat16):
    loudness = level_of(key, shape, cuts, -0.22, 0.18) if cuts else 1.0
    drawn = jax.random.normal(key, shape, jnp.float32) * deviation * loudness
    return jnp.minimum(jnp.maximum(drawn, -limit), limit).astype(kind)


def gaussian_with(key, shape, spread, bound, shards, heavy, kind=jnp.bfloat16):
    drawn = spread * jax.random.normal(key, shape, jnp.float32)
    if shards:
        drawn = drawn * level_of(key, shape, shards, -0.22, 0.18)
    return jnp.clip(with_spikes(drawn, jax.random.fold_in(key, 3), *heavy), -bound, bound).astype(kind)


def setup_inputs(seed: int = 0) -> dict:
    arg_keys = jax.random.split(jax.random.key(seed), 18)
    inputs = gaussian_with(arg_keys[0], (TOKENS, D), 1.0, 6.0, ((0, 32),), (0, 1, 32, 2.75))
    first_gain = jnp.clip(1.0 + 0.15 * jax.random.normal(arg_keys[1], (D,), jnp.float32), 0.25, 1.75)
    first_shift = noise(arg_keys[2], (D,), 0.5, 2.0, (), jnp.float32)
    query_weight = noise(arg_keys[3], (D, D), D ** -0.5, 0.1875, ((1, 2),))
    key_weight = noise(arg_keys[4], (D, D), D ** -0.5, 0.1875, ((1, 2),))
    value_weight = noise(arg_keys[5], (D, D), D ** -0.5, 0.1875, ((1, 2),))
    output_weight = noise(arg_keys[6], (D, D), (max(1, 2 * D // SLOT_LEN)) ** -0.5, 4.0, ((0, 2),))
    second_gain = jnp.clip(1.0 + 0.15 * jax.random.normal(arg_keys[7], (D,), jnp.float32), 0.25, 1.75)
    second_shift = noise(arg_keys[8], (D,), 0.5, 2.0, (), jnp.float32)
    gate_weight = noise(arg_keys[9], (D, FF), D ** -0.5, 0.1875, ((1, 2),))
    up_weight = noise(arg_keys[10], (D, FF), D ** -0.5, 0.1875, ((1, 2),))
    down_weight = noise(arg_keys[11], (FF, D), FF ** -0.5, 0.09375, ((0, 2),))
    cotangent = gaussian_with(arg_keys[12], (TOKENS, D), 1.0, 6.0, ((0, 32),), (0, 1, 32, 2.75))
    species_weight = jnp.clip(jnp.exp(jax.random.uniform(arg_keys[13], (SPECIES,), jnp.float32, math.log(0.25), math.log(4.0))), 0.25, 4.0)
    species_ids = draw_species_ids(jax.random.fold_in(arg_keys[17], 71), 0)
    slot_bucket = draw_slot_bucket(jax.random.fold_in(arg_keys[17], 71), 0)
    slot_length = draw_slot_length(jax.random.fold_in(arg_keys[17], 71), 0)
    return {"inputs": inputs, "first_gain": first_gain, "first_shift": first_shift, "query_weight": query_weight, "key_weight": key_weight, "value_weight": value_weight, "output_weight": output_weight, "second_gain": second_gain, "second_shift": second_shift, "gate_weight": gate_weight, "up_weight": up_weight, "down_weight": down_weight, "cotangent": cotangent, "species_weight": species_weight, "species_ids": species_ids, "slot_bucket": slot_bucket, "slot_length": slot_length}


@jax.custom_vjp
def low(v):
    return lax.optimization_barrier(v.astype(jnp.bfloat16)).astype(jnp.float32)

@jax.custom_vjp
def low_back(v):
    return v

def low_keep(v):
    return (low(v), None)

def low_pass(kept, grad):
    return (grad,)

def back_keep(v):
    return (v, None)

def back_low(kept, grad):
    return (low(grad),)
low.defvjp(low_keep, low_pass)
low_back.defvjp(back_keep, back_low)
EPS = 1e-05
NEG = -1e+30
HIGHEST = lax.Precision.HIGHEST

def rotate_half(values):
    half_dim = values.shape[-1] // 2
    return jnp.concatenate([-values[..., half_dim:], values[..., :half_dim]], -1)

def rotary_tables(positions):
    half_dim = HEAD_DIM // 2
    frequency = 10000.0 ** (-(jnp.arange(half_dim, dtype=jnp.float32) * 2.0 / HEAD_DIM))
    angles = positions[:, None] * frequency[None, :]
    angles = jnp.concatenate([angles, angles], -1)
    return (jnp.cos(angles), jnp.sin(angles))

def layer_norm(values, norm_gain, norm_shift):
    average = lax.optimization_barrier(jnp.mean(values, -1, keepdims=True))
    centred = values - average
    variance = lax.optimization_barrier(jnp.mean(centred * centred, -1, keepdims=True))
    return centred * lax.rsqrt(variance + EPS) * norm_gain + norm_shift

def pair_layer(params, inputs_pair, bucket_pair, length_pair):
    first_gain, first_shift, query_weight, key_weight, value_weight, output_weight, second_gain, second_shift, gate_weight, up_weight, down_weight = params
    window_rows = 2 * SLOT_LEN
    score_scale = HEAD_DIM ** (-0.5)
    token_index = jnp.arange(window_rows, dtype=jnp.int32)
    slot_of = token_index // SLOT_LEN
    within = token_index - slot_of * SLOT_LEN
    joined = bucket_pair[0]
    positions = within + SLOT_LEN * slot_of * joined
    key_valid = within < length_pair[slot_of]
    allowed = key_valid[None, :] & ((slot_of[:, None] == slot_of[None, :]) | (joined == 1))
    cosine_table, sine_table = rotary_tables(positions.astype(jnp.float32))

    def split_heads(values):
        return values.reshape(window_rows, HEADS, HEAD_DIM)

    def apply_rotary(values):
        return values * cosine_table[:, None, :] + rotate_half(values) * sine_table[:, None, :]
    normed = low(layer_norm(inputs_pair, first_gain, first_shift))
    query_rot = low(apply_rotary(split_heads(low_back(jnp.dot(normed, query_weight, precision=HIGHEST)))))
    key_rot = low(apply_rotary(split_heads(low_back(jnp.dot(normed, key_weight, precision=HIGHEST)))))
    value_low = low(low_back(split_heads(jnp.dot(normed, value_weight, precision=HIGHEST))))
    scores = low_back(score_scale * jnp.einsum('qhd,khd->hqk', query_rot, key_rot, precision=HIGHEST))
    scores = jnp.where(allowed[None], scores, NEG)
    probs_low = low(jax.nn.softmax(scores, axis=-1))
    context = low(low_back(jnp.einsum('hqk,khd->qhd', probs_low, value_low, precision=HIGHEST)))
    context = context.reshape(window_rows, D)
    attended = low_back(jnp.dot(context, output_weight, precision=HIGHEST))
    middle = inputs_pair + attended
    normed_two = low(layer_norm(middle, second_gain, second_shift))
    gate_value = low_back(jnp.dot(normed_two, gate_weight, precision=HIGHEST))
    up_value = low_back(jnp.dot(normed_two, up_weight, precision=HIGHEST))
    hidden = low(jax.nn.silu(gate_value) * up_value)
    branch = low_back(jnp.dot(hidden, down_weight, precision=HIGHEST))
    return middle + branch

def reference(inputs, first_gain, first_shift, query_weight, key_weight, value_weight, output_weight, second_gain, second_shift, gate_weight, up_weight, down_weight, cotangent, species_weight, species_ids, slot_bucket, slot_length):
    params = (first_gain.astype(jnp.float32), first_shift.astype(jnp.float32), query_weight.astype(jnp.float32), key_weight.astype(jnp.float32), value_weight.astype(jnp.float32), output_weight.astype(jnp.float32), second_gain.astype(jnp.float32), second_shift.astype(jnp.float32), gate_weight.astype(jnp.float32), up_weight.astype(jnp.float32), down_weight.astype(jnp.float32))
    inputs_float = inputs.astype(jnp.float32)
    bucket_pairs = slot_bucket.reshape(SLOTS // 2, 2)
    length_pairs = slot_length.reshape(SLOTS // 2, 2)

    def forward(inputs_all, weights):
        pairs = inputs_all.reshape(SLOTS // 2, 2 * SLOT_LEN, D)

        def per_pair(pair_items):
            return jax.checkpoint(pair_layer)(weights, pair_items[0], pair_items[1], pair_items[2])
        results = lax.map(per_pair, (pairs, bucket_pairs, length_pairs))
        return results.reshape(TOKENS, D)
    result, pullback = jax.vjp(forward, inputs_float, params)
    token_index = jnp.arange(SLOT_LEN, dtype=jnp.int32)
    token_valid = (token_index[None, :] < slot_length[:, None]).astype(jnp.float32)
    slot_weight = species_weight[species_ids].astype(jnp.float32)
    token_weight = (token_valid * slot_weight[:, None]).reshape(TOKENS)
    cot_full = cotangent.astype(jnp.float32) * token_weight[:, None]
    input_grad, param_grads = pullback(cot_full)
    return (result.astype(jnp.bfloat16), input_grad, param_grads[0], param_grads[1], param_grads[2], param_grads[3], param_grads[4], param_grads[5], param_grads[6], param_grads[7], param_grads[8], param_grads[9], param_grads[10])
```

```python
import functools

import jax
import jax.numpy as jnp
import numpy as np
from jax import lax
from jax.experimental import pallas as pl
from jax.experimental.pallas import tpu as pltpu
from jax.sharding import PartitionSpec as P

HEAD_DIM = 64
EPS = 1e-05
NEG = -1e30
F32 = jnp.float32
BF16 = jnp.bfloat16
NT = (((1,), (1,)), ((), ()))
NN = (((1,), (0,)), ((), ()))
MIB = 1024 * 1024
ONES = 16
VMEM = 60
WIDTH = 512


def product(a, b, dims=NN):
    return lax.dot_general(a, b, dims, preferred_element_type=F32)


def lanes_of(shape):
    return lax.broadcasted_iota(jnp.int32, shape, 1)


def limits():
    return pltpu.CompilerParams(vmem_limit_bytes=VMEM * MIB)


def cost(flops):
    return pl.CostEstimate(flops=flops, bytes_accessed=4 * MIB, transcendentals=0)


def shape_of(dims, kind):
    return jax.ShapeDtypeStruct(dims, kind)


ONCE = pl.Buffered(1)
SMALL = pl.BlockSpec(memory_space=pltpu.SMEM)


def fixed(dims, at=None):
    place = (0,) * len(dims) if at is None else at
    return pl.BlockSpec(dims, lambda *_: place, pipeline_mode=ONCE)


def normalize(v):
    centred = v - jnp.mean(v, -1, keepdims=True)
    inv_std = lax.rsqrt(jnp.mean(centred * centred, -1, keepdims=True) + EPS)
    return centred * inv_std, inv_std


def norm_back(upstream, x_hat, inv_std, gain):
    scaled = upstream * gain
    return inv_std * (
        scaled - jnp.mean(scaled, -1, keepdims=True) - x_hat * jnp.mean(scaled * x_hat, -1, keepdims=True)
    )


def norm_kernel(x_ref, gain_ref, shift_ref, n_ref):
    x_hat, _ = normalize(x_ref[...].astype(F32))
    n_ref[...] = (x_hat * gain_ref[...] + shift_ref[...]).astype(BF16)


def norm_rows(x, gain, shift, block=128):
    rows, dim = x.shape
    spec = pl.BlockSpec((block, dim), lambda i: (i, 0))
    return pl.pallas_call(
        norm_kernel,
        out_shape=shape_of((rows, dim), BF16),
        grid=(rows // block,),
        in_specs=[spec, fixed((1, dim)), fixed((1, dim))],
        out_specs=spec,
        compiler_params=limits(),
        cost_estimate=cost(0),
        name="norm_rows",
    )(x, gain[None], shift[None])


def rotate(u, cos, sin, sign):
    lane = lanes_of(u.shape)
    half = HEAD_DIM // 2
    turned = jnp.where(lane % HEAD_DIM < half, -pltpu.roll(u, 128 - half, 1), pltpu.roll(u, half, 1))
    return u * cos + sign * turned * sin


def project_kernel(with_query, sel, own_ref, other_ref, *rest):
    if with_query:
        wq_ref, wk_ref, wv_ref, cos_ref, sin_ref, q_ref, k_ref, v_ref = rest
        todo = ((wq_ref, q_ref, HEAD_DIM**-0.5), (wk_ref, k_ref, 1.0))
    else:
        wk_ref, wv_ref, cos_ref, sin_ref, k_ref, v_ref = rest
        todo = ((wk_ref, k_ref, 1.0),)

    def work(n):
        cos, sin = cos_ref[...], sin_ref[...]
        for w_ref, out_ref, scale in todo:
            u = product(n, w_ref[...])
            for g in range(u.shape[1] // 128):
                cols = slice(g * 128, (g + 1) * 128)
                turned = rotate(u[:, cols], cos, sin, 1.0).astype(BF16)
                out_ref[:, cols] = (turned.astype(F32) * scale).astype(BF16)
        v_ref[...] = product(n, wv_ref[...]).astype(BF16)

    first = pl.program_id(0) < pl.num_programs(0) // 2
    work(jnp.where(first, own_ref[...], other_ref[...]))


def project(sel, own, other, weights, cos, sin, block=256):
    half, dim = own.shape
    cols = weights[0].shape[1]
    steps = 2 * half // block
    middle = steps // 2
    table = pl.BlockSpec((block, 128), lambda i, s: (s[0] * steps + i, 0))
    count = len(weights)
    return pl.pallas_call(
        functools.partial(project_kernel, count == 3),
        out_shape=(shape_of((2 * half, cols), BF16),) * count,
        grid_spec=pltpu.PrefetchScalarGridSpec(
            num_scalar_prefetch=1,
            grid=(steps,),
            in_specs=[
                pl.BlockSpec((block, dim), lambda i, s: (jnp.minimum(i, middle - 1), 0)),
                pl.BlockSpec((block, dim), lambda i, s: (jnp.maximum(i - middle, 0), 0)),
            ]
            + [fixed((dim, cols))] * count
            + [table, table],
            out_specs=[pl.BlockSpec((block, cols), lambda i, s: (i, 0))] * count,
        ),
        compiler_params=limits(),
        cost_estimate=cost(half * dim * cols * count),
        name="project_rows",
    )(sel, own, other, *weights, cos, sin)


def middle_kernel(c_ref, co_ref, w_ref, wo_ref, x_ref, gain_ref, shift_ref, middle_ref, n_ref):
    middle = x_ref[...].astype(F32) + (product(c_ref[...], w_ref[...]) + product(co_ref[...], wo_ref[...]))
    middle_ref[...] = middle
    x_hat, _ = normalize(middle)
    n_ref[...] = (x_hat * gain_ref[...] + shift_ref[...]).astype(BF16)


def middle_rows(context, other, weight, weight_other, x, gain, shift, block=256):
    rows, dim = x.shape
    cols = context.shape[1]
    narrow = pl.BlockSpec((block, cols), lambda i: (i, 0))
    wide = pl.BlockSpec((block, dim), lambda i: (i, 0))
    return pl.pallas_call(
        middle_kernel,
        out_shape=(shape_of((rows, dim), F32), shape_of((rows, dim), BF16)),
        grid=(rows // block,),
        in_specs=[narrow, narrow, fixed((cols, dim)), fixed((cols, dim)), wide, fixed((1, dim)), fixed((1, dim))],
        out_specs=[wide, wide],
        compiler_params=limits(),
        cost_estimate=cost(rows * dim * cols),
        name="middle_rows",
    )(context, other, weight, weight_other, x, gain[None], shift[None])


def add_sums(sums_ref, upstream, x_hat):
    row = lax.broadcasted_iota(jnp.int32, sums_ref.shape, 0)
    new = jnp.where(
        row == 0,
        jnp.sum(upstream * x_hat, 0, keepdims=True),
        jnp.where(row == 1, jnp.sum(upstream, 0, keepdims=True), 0.0),
    )
    first = pl.program_id(0) == 0

    @pl.when(first)
    def _():
        sums_ref[...] = new

    @pl.when(jnp.logical_not(first))
    def _():
        sums_ref[...] += new


def middle_back_kernel(d_ref, got_ref, middle_ref, cot_ref, weight_ref, gain_ref, dm_ref, da_ref, sums_ref):
    upstream = d_ref[...] + got_ref[...].astype(F32)
    x_hat, inv_std = normalize(middle_ref[...])
    d_middle = cot_ref[...].astype(F32) * weight_ref[...] + norm_back(upstream, x_hat, inv_std, gain_ref[...])
    dm_ref[...] = d_middle
    da_ref[...] = d_middle.astype(BF16)
    add_sums(sums_ref, upstream, x_hat)


def middle_back(d_n2, got, middle, cotangent, token_weight, gain, block=128):
    rows, dim = middle.shape
    wide = pl.BlockSpec((block, dim), lambda i: (i, 0))
    return pl.pallas_call(
        middle_back_kernel,
        out_shape=(shape_of((rows, dim), F32), shape_of((rows, dim), BF16), shape_of((8, dim), F32)),
        grid=(rows // block,),
        in_specs=[wide] * 4 + [pl.BlockSpec((block, 1), lambda i: (i, 0)), fixed((1, dim))],
        out_specs=[wide, wide, pl.BlockSpec((8, dim), lambda i: (0, 0))],
        compiler_params=limits(),
        cost_estimate=cost(0),
        name="middle_back",
    )(d_n2, got, middle, cotangent, token_weight, gain[None])


def first_back_kernel(d_ref, got_ref, far_ref, x_ref, dm_ref, gain_ref, out_ref, sums_ref):
    upstream = d_ref[...] + got_ref[...].astype(F32) + far_ref[...].astype(F32)
    x_hat, inv_std = normalize(x_ref[...].astype(F32))
    out_ref[...] = dm_ref[...] + norm_back(upstream, x_hat, inv_std, gain_ref[...])
    add_sums(sums_ref, upstream, x_hat)


def first_back(d_n1, got, far, x, d_middle, gain, block=128):
    rows, dim = x.shape
    wide = pl.BlockSpec((block, dim), lambda i: (i, 0))
    return pl.pallas_call(
        first_back_kernel,
        out_shape=(shape_of((rows, dim), F32), shape_of((8, dim), F32)),
        grid=(rows // block,),
        in_specs=[wide] * 5 + [fixed((1, dim))],
        out_specs=[wide, pl.BlockSpec((8, dim), lambda i: (0, 0))],
        compiler_params=limits(),
        cost_estimate=cost(0),
        name="first_back",
    )(d_n1, got, far, x, d_middle, gain[None])


def rows_times_kernel(count, dims, mark, *refs):
    lefts, rights = refs[:count], refs[count : 2 * count]
    give_ref, own_ref = refs[2 * count :]
    total = None
    for left, right in zip(lefts, rights):
        x = product(left[...], right[...], dims)
        total = x if total is None else total + x
    giving = pl.program_id(0) < pl.num_programs(0) // 2

    @pl.when(giving)
    def _():
        give_ref[...] = total.astype(BF16)

    @pl.when(jnp.logical_not(giving))
    def _():
        own_ref[...] = total


def rows_times(mark, terms, dims, block=256):
    rows = terms[0][0].shape[0]
    dim = terms[0][1].shape[0 if dims is NT else 1]
    steps = rows // block
    middle = steps // 2
    specs, rights = [], []
    for left, right, which in terms:
        depth = left.shape[1]
        specs.append(fixed((dim, depth), (0, which)) if dims is NT else fixed((depth, dim), (which, 0)))
    return pl.pallas_call(
        functools.partial(rows_times_kernel, len(terms), dims),
        out_shape=(shape_of((rows // 2, dim), BF16), shape_of((rows // 2, dim), F32)),
        grid=(steps,),
        in_specs=[SMALL]
        + [
            pl.BlockSpec((block, left.shape[1]), lambda i: ((i + middle) % steps, 0))
            for left, _, _ in terms
        ]
        + specs,
        out_specs=[
            pl.BlockSpec((block, dim), lambda i: (jnp.minimum(i, middle - 1), 0)),
            pl.BlockSpec((block, dim), lambda i: (jnp.maximum(i - middle, 0), 0)),
        ],
        compiler_params=limits(),
        cost_estimate=cost(rows * dim * sum(left.shape[1] for left, _, _ in terms) // 2),
        name="rows_times",
    )(mark, *[t[0] for t in terms], *[t[1] for t in terms])


def key_side(k, h, bias):
    lane = lanes_of(k.shape)
    pos = lane % HEAD_DIM
    extra = jnp.where(pos < 3, 1.0, jnp.where(pos == 3, bias, 0.0))
    return jnp.where(lane // HEAD_DIM == h, k.astype(F32), extra).astype(BF16)


def row_side(q, h, stat):
    lane = lanes_of(q.shape)
    pos = lane % HEAD_DIM
    high = stat.astype(BF16).astype(F32)
    left = stat - high
    mid = left.astype(BF16).astype(F32)
    low = left - mid
    extra = jnp.where(
        pos == 0, high, jnp.where(pos == 1, mid, jnp.where(pos == 2, low, jnp.where(pos == 3, 1.0, 0.0)))
    )
    return jnp.where(lane // HEAD_DIM == h, q.astype(F32), extra).astype(BF16)


def only_head(q, h):
    return jnp.where(lanes_of(q.shape) // HEAD_DIM == h, q, jnp.zeros_like(q))


def key_bias(info, rows):
    row = lax.broadcasted_iota(jnp.int32, (rows, 128), 0)
    return jnp.where(lax.rem(row + info[2], rows) < info[1], 0.0, NEG)


def attend_kernel(own, sub, kb, info, q_ref, k_ref, v_ref, *rest):
    if own:
        o_ref, l_ref, m_ref, keys, values_t = rest
    else:
        o1_ref, l1_ref, m1_ref, c_ref, give_ref, lse_ref, keys, values_t = rest
    count = k_ref.shape[0]
    rows = q_ref.shape[0]

    def scores(unit):
        h, r = unit
        q = q_ref[r * sub : (r + 1) * sub, :]
        qa = row_side(q, h, jnp.zeros(q.shape, F32))
        parts = [product(keys[h, b * kb : (b + 1) * kb], qa, NT) for b in range(count // kb)]
        top = jnp.max(parts[0], 0, keepdims=True)
        for s in parts[1:]:
            top = jnp.maximum(top, jnp.max(s, 0, keepdims=True))
        return parts, top

    def combine(unit, parts, top):
        h, _ = unit
        total = None
        for b, s in enumerate(parts):
            p = jnp.exp(s - top).astype(BF16)
            x = product(values_t[h, :, b * kb : (b + 1) * kb], p)
            total = x if total is None else total + x
        return total[:HEAD_DIM], total[HEAD_DIM : HEAD_DIM + 1], top

    def work():
        bias = key_bias(info, count) if own else 0.0
        for h in range(2):
            keys[h] = key_side(k_ref[...], h, bias)
        flipped = v_ref[...].T
        for h in range(2):
            values_t[h, :HEAD_DIM] = flipped[h * HEAD_DIM : (h + 1) * HEAD_DIM]
            values_t[h, HEAD_DIM:] = jnp.ones((ONES, count), BF16)
        units = [(h, r) for r in range(rows // sub) for h in range(2)]
        ready = scores(units[0])
        done = {}
        for i, unit in enumerate(units):
            following = scores(units[i + 1]) if i + 1 < len(units) else None
            done[unit] = combine(unit, *ready)
            ready = following
        gathered = []
        for part in range(3):
            strips = []
            for r in range(rows // sub):
                strips.append(
                    jnp.concatenate(
                        [jnp.broadcast_to(done[(h, r)][part], (HEAD_DIM, sub)) for h in range(2)], 0
                    )
                )
            gathered.append(jnp.concatenate(strips, 1))
        return gathered

    def finish(o, l, m):
        context = (o / l).T.astype(BF16)
        c_ref[...] = context
        give_ref[...] = context[rows // 2 :]
        lse_ref[...] = pltpu.roll((m + jnp.log(l)).T, HEAD_DIM, 1)

    if own:
        o, l, m = work()
        o_ref[...] = o
        l_ref[...] = l
        m_ref[...] = m
    else:

        @pl.when(info[0] == 1)
        def _():
            o, l, m = work()
            m1 = m1_ref[...]
            top = jnp.maximum(m, m1)
            a1 = jnp.exp(m1 - top)
            a2 = jnp.exp(m - top)
            finish(o1_ref[...] * a1 + o * a2, l1_ref[...] * a1 + l * a2, top)

        @pl.when(info[0] != 1)
        def _():
            finish(o1_ref[...], l1_ref[...], m1_ref[...])


def attend(own, info, q, k, v, earlier=(), sub=256, kb=256):
    rows, cols = q.shape
    count = k.shape[0]
    wide = pl.BlockSpec((rows, 128), lambda p, s: (0, p))
    tall = pl.BlockSpec((128, rows), lambda p, s: (p, 0))
    upright = jax.ShapeDtypeStruct((cols, rows), F32)
    if own:
        outs = (upright,) * 3
    else:
        outs = (
            jax.ShapeDtypeStruct((rows, cols), BF16),
            jax.ShapeDtypeStruct((rows // 2, cols), BF16),
            jax.ShapeDtypeStruct((rows, cols), F32),
        )
    return pl.pallas_call(
        functools.partial(attend_kernel, own, sub, kb),
        out_shape=outs,
        grid_spec=pltpu.PrefetchScalarGridSpec(
            num_scalar_prefetch=1,
            grid=(cols // 128,),
            in_specs=[wide, pl.BlockSpec((count, 128), lambda p, s: (0, p)), pl.BlockSpec((count, 128), lambda p, s: (0, p))]
            + [tall] * len(earlier),
            out_specs=[tall] * 3 if own else [wide, pl.BlockSpec((rows // 2, 128), lambda p, s: (0, p)), wide],
            scratch_shapes=[
                pltpu.VMEM((2, count, 128), BF16),
                pltpu.VMEM((2, HEAD_DIM + ONES, count), BF16),
            ],
        ),
        compiler_params=limits(),
        cost_estimate=cost(4 * rows * count * cols),
        name="attend_own" if own else "attend_far",
    )(info, q, k, v, *earlier)


def attend_back_kernel(own, kb, info, q_ref, k_ref, v_ref, c_ref, lse_ref, cos_ref, sin_ref, *rest):
    if own:
        g_ref, qcos_ref, qsin_ref, before_ref, dq_ref, dk_ref, dv_ref, *rest = rest
    else:
        d_ref, do_ref, w_ref, g_ref, dq_ref, dk_ref, dv_ref, *rest = rest
    keys, values, keys_t, dk_sum, dv_sum = rest
    count = k_ref.shape[0]
    if not own:
        half = d_ref.shape[0]
        g_ref[:half] = product(d_ref[...], w_ref[...], NT).astype(BF16)
        g_ref[half:] = product(do_ref[...], w_ref[...], NT).astype(BF16)

    def work():
        bias = key_bias(info, count) if own else 0.0
        for h in range(2):
            keys[h] = key_side(k_ref[...], h, bias)
            values[h] = key_side(v_ref[...], h, 0.0)
            keys_t[h] = only_head(k_ref[...], h).T
        q = q_ref[...]
        g = g_ref[...]
        lane = lanes_of(q.shape)
        overlap = g.astype(F32) * c_ref[...].astype(F32)
        lse = lse_ref[...]
        dq = None
        for h in range(2):
            qa = row_side(q, h, -lse)
            delta = jnp.sum(jnp.where(lane // HEAD_DIM == h, overlap, 0.0), -1, keepdims=True)
            ga = row_side(g, h, jnp.broadcast_to(-delta, q.shape))
            qm = only_head(q, h)
            gm = only_head(g, h)
            for b in range(count // kb):
                rows = slice(b * kb, (b + 1) * kb)
                p = jnp.exp(product(keys[h, rows], qa, NT))
                ds = (p * product(values[h, rows], ga, NT)).astype(BF16)
                dv = product(p.astype(BF16), gm)
                dk = product(ds, qm)
                if h == 0:
                    dv_sum[rows] = dv
                    dk_sum[rows] = dk
                else:
                    dv_sum[rows] += dv
                    dk_sum[rows] += dk
                part = product(keys_t[h, :, rows], ds)
                dq = part if dq is None else dq + part
        dk_ref[...] = rotate(dk_sum[...], cos_ref[...], sin_ref[...], -1.0).astype(BF16)
        dv_ref[...] = dv_sum[...].astype(BF16)
        return dq.T * (HEAD_DIM**-0.5)

    if own:
        dq = work() + before_ref[...]
        dq_ref[...] = rotate(dq, qcos_ref[...], qsin_ref[...], -1.0).astype(BF16)
    else:

        @pl.when(info[0] == 1)
        def _():
            dq_ref[...] = work()

        @pl.when(info[0] != 1)
        def _():
            dq_ref[...] = jnp.zeros_like(dq_ref)
            dk_ref[...] = jnp.zeros_like(dk_ref)
            dv_ref[...] = jnp.zeros_like(dv_ref)


def attend_back(own, info, q, k, v, c, lse, tables, extra, kb=256, at=0, pairs=None):
    rows = q.shape[0]
    cols = 128 * pairs
    count = k.shape[0]
    wide = pl.BlockSpec((rows, 128), lambda p, s: (0, p + at))
    side = pl.BlockSpec((count, 128), lambda p, s: (0, p + at))
    wide_out = pl.BlockSpec((rows, 128), lambda p, s: (0, p))
    side_out = pl.BlockSpec((count, 128), lambda p, s: (0, p))
    own_table = pl.BlockSpec((rows, 128), lambda p, s: (s[3], 0))
    far_table = pl.BlockSpec((count, 128), lambda p, s: (s[4], 0))
    ins = [q, k, v, c, lse, *tables]
    specs = [wide, side, side, wide, wide] + [own_table if own else far_table] * 2
    shapes = (
        shape_of((rows, cols), BF16 if own else F32),
        shape_of((count, cols), BF16),
        shape_of((count, cols), BF16),
    )
    outs = [wide_out, side_out, side_out]
    if own:
        g, before = extra
        ins += [g, *tables, before]
        specs += [wide, own_table, own_table, wide]
    else:
        d, d_other, weight = extra
        ins += [d, d_other, weight]
        specs += [fixed(d.shape), fixed(d.shape), pl.BlockSpec((128, weight.shape[1]), lambda p, s: (p + at, 0))]
        shapes = (shape_of((rows, cols), BF16),) + shapes
        outs = [wide_out] + outs
    return pl.pallas_call(
        functools.partial(attend_back_kernel, own, kb),
        out_shape=shapes,
        grid_spec=pltpu.PrefetchScalarGridSpec(
            num_scalar_prefetch=1,
            grid=(pairs,),
            in_specs=specs,
            out_specs=outs,
            scratch_shapes=[
                pltpu.VMEM((2, count, 128), BF16),
                pltpu.VMEM((2, count, 128), BF16),
                pltpu.VMEM((2, 128, count), BF16),
                pltpu.VMEM((count, 128), F32),
                pltpu.VMEM((count, 128), F32),
            ],
        ),
        compiler_params=limits(),
        cost_estimate=cost(8 * rows * count * cols),
        name="attend_back_own" if own else "attend_back_far",
    )(info, *ins)


def turn(out, parts):
    each = out.shape[1]
    size = 256
    unit = (lax.broadcasted_iota(jnp.int32, (size, size), 0) == lax.broadcasted_iota(jnp.int32, (size, size), 1)).astype(
        F32
    ).astype(BF16)
    at = 0
    for n_ref in parts:
        rows, dim = n_ref.shape
        for j in range(dim // size):
            flipped = product(unit, n_ref[:, j * size : (j + 1) * size], NT).astype(BF16)
            out[j * size // each : (j + 1) * size // each, :, at : at + rows] = flipped.reshape(
                size // each, each, rows
            )
        at += rows


def place(grads, flow, j, count, gb):
    out = grads[2 * flow + j // (count // 2)]
    j = j % (count // 2)
    return out, slice(j * gb, (j + 1) * gb)


def rows_in_order(turned, order, flow, j, gb):
    blocks, each, _ = turned.shape
    per = gb // each
    return jnp.concatenate([turned[order[flow * blocks + j * per + i]] for i in range(per)], 0)


def gated_kernel(gb, again, order, n_ref, no_ref, b_ref, bo_ref, wg_ref, wu_ref, wd_ref, *rest):
    if again:
        before_ref, hid_ref, own_ref, give_ref, *grads, dg, du, acc, nt, bt = rest
    else:
        hid_ref, out_ref, *grads, dg, du, acc, nt, bt = rest
    step = pl.program_id(0)
    last = pl.num_programs(0) - 1
    half_rows, dim = n_ref.shape
    width = wg_ref.shape[1]

    @pl.when(step == 0)
    def _():
        turn(nt, (n_ref, no_ref))
        turn(bt, (b_ref, bo_ref))

    for r, (rows_ref, d_ref) in enumerate(((n_ref, b_ref), (no_ref, bo_ref))):
        part = slice(r * half_rows, (r + 1) * half_rows)
        n = rows_ref[...]
        gate = product(n, wg_ref[...])
        up = product(n, wu_ref[...])
        d_hidden = product(d_ref[...], wd_ref[...], NT)
        s = 0.5 * jnp.tanh(0.5 * gate) + 0.5
        silu = gate * s
        hid_ref[part] = (silu * up).astype(BF16)
        d_gate = (d_hidden * up * (s * (1.0 + gate * (1.0 - s)))).astype(BF16)
        d_up = (d_hidden * silu).astype(BF16)
        dg[part] = d_gate
        du[part] = d_up
        back = product(d_gate, wg_ref[...], NT) + product(d_up, wu_ref[...], NT)

        @pl.when(step == 0)
        def _():
            acc[part] = back + before_ref[part] if again else back

        @pl.when(step != 0)
        def _():
            acc[part] += back

    @pl.when(step == last)
    def _():
        if again:
            own_ref[...] = acc[:half_rows]
            give_ref[...] = acc[half_rows:].astype(BF16)
        else:
            out_ref[...] = acc[...]

    half = width // 2
    for flow in range(2):
        cols = slice(flow * half, (flow + 1) * half)
        for j in range(dim // gb):
            left = rows_in_order(nt, order, flow, j, gb)
            left_down = rows_in_order(bt, order, flow, j, gb)
            out, part = place(grads, flow, j, dim // gb, gb)
            out[part, :half] = product(left, dg[:, cols]).astype(BF16)
            out[part, half : 2 * half] = product(left, du[:, cols]).astype(BF16)
            out[part, 2 * half :] = product(left_down, hid_ref[:, cols]).astype(BF16)


def gated_units(order, rows_in, wg, wu, wd, blocks, first, last, before=(), width=WIDTH, gb=256):
    half, dim = rows_in[0].shape
    rows = 2 * half
    steps = (last - first) // width
    at = first // width
    again = bool(before)
    columns = pl.BlockSpec((dim, width), lambda s, o: (0, s + at))
    grads = shape_of((dim // 2, 3 * (last - first) // 2), BF16)
    grad_spec = pl.BlockSpec((dim // 2, 3 * width // 2), lambda s, o: (0, s))
    split = pl.BlockSpec((half, dim), lambda s, o: (0, 0))
    if again:
        shapes = (shape_of((half, dim), F32), shape_of((half, dim), BF16))
        specs = [split, split]
    else:
        shapes = (shape_of((rows, dim), F32),)
        specs = [pl.BlockSpec((rows, dim), lambda s, o: (0, 0))]
    return pl.pallas_call(
        functools.partial(gated_kernel, gb, again),
        out_shape=(shape_of((rows, last - first), BF16),) + shapes + (grads,) * 4,
        grid_spec=pltpu.PrefetchScalarGridSpec(
            num_scalar_prefetch=1,
            grid=(steps,),
            in_specs=[fixed((half, dim))] * 4
            + [columns, columns, pl.BlockSpec((width, dim), lambda s, o: (s + at, 0))]
            + [fixed((rows, dim))] * len(before),
            out_specs=[pl.BlockSpec((rows, width), lambda s, o: (0, s))] + specs + [grad_spec] * 4,
            scratch_shapes=[
                pltpu.VMEM((rows, width), BF16),
                pltpu.VMEM((rows, width), BF16),
                pltpu.VMEM((rows, dim), F32),
                pltpu.VMEM((blocks, dim // blocks, rows), BF16),
                pltpu.VMEM((blocks, dim // blocks, rows), BF16),
            ],
        ),
        compiler_params=limits(),
        cost_estimate=cost(4 * rows * dim * (last - first)),
        name="gated_units",
    )(order, *rows_in, wg, wu, wd, *before)


def weight_grad_kernel(gb, with_context, order, *refs):
    n_ref, no_ref, f_ref, fo_ref, q_ref, k_ref, v_ref, kf_ref, vf_ref, *refs = refs
    if with_context:
        d_ref, do_ref, c_ref, *grads, nt, ft, dt = refs
        turn(dt, (d_ref, do_ref))
    else:
        *grads, nt, ft = refs
    turn(nt, (n_ref, no_ref))
    turn(ft, (f_ref, fo_ref))
    blocks, each, _ = nt.shape
    dim = blocks * each
    cols = q_ref.shape[1]
    for flow in range(2):
        half = slice(flow * cols // 2, (flow + 1) * cols // 2)
        for j in range(dim // gb):
            out, part = place(grads, flow, j, dim // gb, gb)
            left = rows_in_order(nt, order, flow, j, gb)
            far = rows_in_order(ft, order, flow, j, gb)
            if flow == 0:
                whole = product(left, q_ref[...])
            else:
                whole = product(left, v_ref[...]) + product(far, vf_ref[...])
            out[part, :cols] = whole.astype(BF16)
            out[part, cols : cols + cols // 2] = (
                product(left, k_ref[:, half]) + product(far, kf_ref[:, half])
            ).astype(BF16)
            if with_context:
                wide = c_ref.shape[1] // 2
                out[part, cols + cols // 2 :] = product(
                    rows_in_order(dt, order, flow, j, gb), c_ref[:, flow * wide : (flow + 1) * wide]
                ).astype(BF16)


def weight_grads(order, lefts, own, far, which, blocks, context=(), gb=256):
    half, dim = lefts[0].shape
    rows, cols = own[0].shape
    extra = context[2].shape[1] // 2 if context else 0
    grads = shape_of((dim // 2, 3 * cols // 2 + extra), BF16)
    ins = [*lefts, *own, *far, *context]
    specs = (
        [SMALL]
        + [fixed(a.shape) for a in (*lefts, *own)]
        + [fixed((rows, cols), (0, which))] * len(far)
        + [fixed(a.shape) for a in context]
    )
    return pl.pallas_call(
        functools.partial(weight_grad_kernel, gb, bool(context)),
        out_shape=(grads,) * 4,
        grid=(1,),
        in_specs=specs,
        out_specs=[fixed(grads.shape)] * 4,
        scratch_shapes=[pltpu.VMEM((blocks, dim // blocks, rows), BF16)] * (3 if context else 2),
        compiler_params=limits(),
        cost_estimate=cost(rows * dim * (5 * cols + 2 * extra) // 2),
        name="weight_grads",
    )(order, *ins)


def unpack_gated_kernel(first_ref, second_ref, gate_ref, up_ref, down_ref):
    half = WIDTH // 2
    at = 0
    for ref in (first_ref, second_ref):
        flow = ref.shape[1] // 2
        for step in range(flow // (3 * half)):
            for f in range(2):
                base = f * flow + 3 * step * half
                cols = slice(at, at + half)
                gate_ref[:, cols] = ref[:, base : base + half].astype(F32)
                up_ref[:, cols] = ref[:, base + half : base + 2 * half].astype(F32)
                down_ref[cols, :] = ref[:, base + 2 * half : base + 3 * half].astype(F32).T
                at += half


def unpack_gated(first, second):
    rows = first.shape[0]
    units = 2 * first.shape[1] // 3
    whole = pl.BlockSpec(memory_space=pltpu.VMEM)
    return pl.pallas_call(
        unpack_gated_kernel,
        out_shape=(shape_of((rows, units), F32), shape_of((rows, units), F32), shape_of((units, rows), F32)),
        in_specs=[whole] * 2,
        out_specs=[whole] * 3,
        compiler_params=limits(),
        cost_estimate=cost(0),
        name="unpack_gated",
    )(first, second)


def unpack_rest_kernel(first_ref, second_ref, q_ref, k_ref, v_ref, p_ref):
    cols = q_ref.shape[1] // 2
    half = cols // 2
    for i, ref in enumerate((first_ref, second_ref)):
        flow = ref.shape[1] // 2
        part = slice(i * cols, (i + 1) * cols)
        q_ref[:, part] = ref[:, :cols].astype(F32)
        v_ref[:, part] = ref[:, flow : flow + cols].astype(F32)
        for f in range(2):
            base = f * flow + cols
            k_ref[:, i * cols + f * half : i * cols + (f + 1) * half] = ref[:, base : base + half].astype(F32)
        if i == 0:
            wide = flow - cols - half
            for f in range(2):
                base = f * flow + cols + half
                p_ref[f * wide : (f + 1) * wide, :] = ref[:, base : base + wide].astype(F32).T


def unpack_rest(first, second, cols):
    rows = first.shape[0]
    whole = pl.BlockSpec(memory_space=pltpu.VMEM)
    return pl.pallas_call(
        unpack_rest_kernel,
        out_shape=(shape_of((rows, cols), F32),) * 3 + (shape_of((cols, rows), F32),),
        in_specs=[whole] * 2,
        out_specs=[whole] * 4,
        compiler_params=limits(),
        cost_estimate=cost(0),
        name="unpack_rest",
    )(first, second)


def swap(value):
    return lax.ppermute(value, "mp", [(0, 1), (1, 0)])


def across(value, bit):
    return lax.ppermute(value, "dp", [(i, i ^ (1 << bit)) for i in range(lax.axis_size("dp"))])


def send_first(grads):
    return across(grads[0], 0), across(grads[2], 1)


def onward(grads, got):
    half = got[0].shape[0] // 2
    return [(keep[:half].astype(F32) + g[:half].astype(F32)).astype(BF16) for keep, g in zip(grads[1::2], got)]


def send_second(quarters):
    return across(quarters[0], 1), across(quarters[1], 0)


def kept(grads, got, got_again):
    half = got[0].shape[0] // 2
    quarters = [
        keep[half:].astype(F32) + g[half:].astype(F32) + h.astype(F32)
        for keep, g, h in zip(grads[1::2], got, got_again)
    ]
    return jnp.concatenate([q.astype(BF16) for q in quarters], 1)


def scatter_rest(quarters):
    size = lax.axis_size("dp")
    groups = [[b + 4 * k for k in range(size // 4)] for b in range(4)]
    return lax.psum_scatter(quarters, "dp", scatter_dimension=0, axis_index_groups=groups, tiled=True)


def later_bits():
    return range(2, lax.axis_size("dp").bit_length() - 1)


def halve(total, bit):
    half = total.shape[0] // 2
    return (total[half:].astype(F32) + across(total[:half], bit).astype(F32)).astype(BF16)


def sum_all(value):
    value = value + swap(value)
    for bit in range(lax.axis_size("dp").bit_length() - 1):
        value = value + across(value, bit)
    return value


def after(value, done):
    return lax.optimization_barrier((value, done))[0]


def block_orders():
    size = lax.axis_size("dp")
    me = lax.axis_index("dp")
    count = size.bit_length() - 1
    places = np.arange(size)
    results = []
    for halved in (2, count):
        flows = []
        for outer, inner in ((0, 1), (1, 0)):
            flipped = np.zeros(size, np.int32)
            plain = np.zeros(size, np.int32)
            for position, bit in enumerate((outer, inner, *range(2, halved))):
                flipped |= (1 - ((places >> (count - 1 - position)) & 1)).astype(np.int32) << bit
            if halved == 2:
                plain = (places % (size // 4)).astype(np.int32) * 4
                flows.append((jnp.asarray(flipped) ^ (me & 3)) | jnp.asarray(plain))
            else:
                flows.append(jnp.asarray(flipped) ^ me)
        results.append(jnp.concatenate(flows).astype(jnp.int32))
    return results


def rotary_tables(slot_rows):
    half_dim = HEAD_DIM // 2
    frequency = (10000.0 ** (-(np.arange(half_dim) * 2.0 / HEAD_DIM))).astype(np.float32)
    within = np.arange(slot_rows)
    tables = []
    for window_half in range(2):
        for shift in (0, slot_rows // 2):
            tables.append((within + shift) % slot_rows + window_half * slot_rows)
    angles = np.concatenate(tables).astype(np.float32)[:, None] * frequency[None, :]
    angles = np.tile(angles.astype(np.float64), (1, 4))
    return np.cos(angles).astype(np.float32), np.sin(angles).astype(np.float32)


def local(
    inputs,
    first_gain,
    first_shift,
    query_weight,
    key_weight,
    value_weight,
    output_weight,
    second_gain,
    second_shift,
    gate_weight,
    up_weight,
    down_weight,
    cotangent,
    species_weight,
    species_ids,
    slot_bucket,
    slot_length,
):
    half_rows = inputs.shape[0]
    slot_rows = 2 * half_rows
    blocks = lax.axis_size("dp")
    core = lax.axis_index("mp")
    parity = lax.axis_index("dp") % 2
    joined = slot_bucket[0]
    length = slot_length[0]
    start = core * half_rows
    own_table = 2 * parity * joined + core
    far_table = 2 * (1 - parity) * joined + core
    info = jnp.stack([joined, length, start, own_table, far_table]).astype(jnp.int32)
    order, order_all = block_orders()
    tables = rotary_tables(slot_rows)
    units = gate_weight.shape[1]
    pairs = query_weight.shape[1] // 128
    few = pairs // 2

    cot_other = swap(cotangent)
    output_weight_other = swap(output_weight)
    n1_own = norm_rows(inputs, first_gain, first_shift)
    n1_far_own = across(n1_own, 0)
    n1_other = swap(n1_own)
    q, k, v = project(info[3:4], n1_own, n1_other, (query_weight, key_weight, value_weight), *tables)
    earlier = attend(True, info, q, k, v)

    n1_far_own = after(n1_far_own, earlier[2])
    n1_far_other = swap(n1_far_own)
    token_index = (jnp.arange(slot_rows, dtype=jnp.int32) + start) % slot_rows
    table_index = jnp.arange(species_weight.shape[0], dtype=jnp.int32)
    slot_weight = jnp.sum(jnp.where(table_index == species_ids[0], species_weight, 0.0))
    token_weight = jnp.where(token_index < length, slot_weight, 0.0)[:, None]
    late_cot, late_other = after((cotangent, cot_other), earlier[2])
    d_branch = [
        (c.astype(F32) * w).astype(BF16)
        for c, w in ((late_cot, token_weight[:half_rows]), (late_other, token_weight[half_rows:]))
    ]
    k_far, v_far = project(info[4:5], n1_far_own, n1_far_other, (key_weight, value_weight), *tables)
    context, context_give, log_total = attend(False, info, q, k_far, v_far, tuple(earlier))
    middle, n2_own = middle_rows(
        context, swap(context_give), output_weight, output_weight_other, inputs, second_gain, second_shift
    )
    rows_in = (n2_own, swap(n2_own), *d_branch)

    gated = functools.partial(gated_units, order, rows_in, gate_weight, up_weight, down_weight, blocks)
    hidden_1, d_n2, *grads_1 = gated(0, units // 2)
    got_1 = send_first(grads_1)
    hidden_2, d_n2_own, d_n2_give, *grads_2 = gated(units // 2, units, (d_n2,))
    got_2 = send_first(grads_2)
    d_middle, d_attended, second_sums = middle_back(
        d_n2_own, swap(d_n2_give), middle, cotangent, token_weight[:half_rows], second_gain
    )
    d_attended_other = swap(d_attended)
    got_1 = after(got_1, d_attended)
    onward_1 = onward(grads_1, got_1)
    again_1 = send_second(onward_1)

    back = functools.partial(attend_back, q=q, c=context, lse=log_total, tables=tables)
    d_context, dq_far, *far = back(
        False,
        after(info, onward_1),
        k=k_far,
        v=v_far,
        extra=(d_attended, d_attended_other, output_weight),
        pairs=pairs,
    )
    got_2, again_1 = after((got_2, again_1), dq_far)
    onward_2 = onward(grads_2, got_2)
    again_2 = send_second(onward_2)
    d_far_give, d_far = rows_times(order, ((far[0], key_weight, 0), (far[1], value_weight, 0)), NT)
    d_far_got = swap(d_far_give)
    kept_1 = kept(grads_1, got_1, again_1)
    gated_1 = scatter_rest(kept_1)

    own_1 = back(
        True, after(info, (kept_1, onward_2, d_far_give)), k=k, v=v, extra=(d_context, dq_far), pairs=few
    )
    d_far_got, again_2 = after((d_far_got, again_2), own_1[0])
    d_far = (d_far + d_far_got.astype(F32)).astype(BF16)
    d_far_back = across(d_far, 0)
    kept_2 = kept(grads_2, got_2, again_2)
    gated_2 = scatter_rest(kept_2)
    lefts = (n1_own, n1_other, n1_far_own, n1_far_other)
    grads_3 = weight_grads(order_all, lefts, own_1, far, 0, blocks, (d_attended, d_attended_other, context))
    got_3 = send_first(grads_3)
    own_2 = back(
        True, after(info, (kept_2, d_far, grads_3[0])), k=k, v=v, extra=(d_context, dq_far), at=few, pairs=few
    )
    grads_4 = weight_grads(order_all, lefts, own_2, far, 1, blocks)
    got_4 = send_first(grads_4)
    got_3 = after(got_3, grads_4[0])
    onward_3 = onward(grads_3, got_3)
    again_3 = send_second(onward_3)

    terms = [
        (d, w, i)
        for i, own in enumerate((own_1, own_2))
        for d, w in zip(own, (query_weight, key_weight, value_weight))
    ]
    d_n1_give, d_n1 = rows_times(after(order, onward_3), terms, NT)
    d_n1_got = swap(d_n1_give)
    got_4 = after(got_4, d_n1_give)
    onward_4 = onward(grads_4, got_4)
    again_4 = send_second(onward_4)
    input_grad, first_sums = first_back(d_n1, d_n1_got, d_far_back, inputs, d_middle, first_gain)
    rest_1 = kept(grads_3, got_3, again_3)
    branch_give, branch = rows_times(
        after(order, (onward_4, rest_1)), ((hidden_1, down_weight, 0), (hidden_2, down_weight, 1)), NN
    )
    output = (middle + branch + swap(branch_give).astype(F32)).astype(BF16)
    rest_2 = kept(grads_4, got_4, again_4)
    for bit in later_bits():
        rest_1 = halve(rest_1, bit)
        rest_2 = halve(rest_2, bit)

    norm_sums = sum_all(jnp.concatenate([first_sums[:2], second_sums[:2]], 0))
    share = norm_sums.shape[1] // (2 * blocks)
    norm_sums = lax.dynamic_slice_in_dim(norm_sums, (2 * lax.axis_index("dp") + core) * share, share, 1)
    gate_grad, up_grad, down_grad = unpack_gated(gated_1, gated_2)
    query_grad, key_grad, value_grad, project_grad = unpack_rest(rest_1, rest_2, query_weight.shape[1])
    return (
        output,
        input_grad,
        norm_sums[0],
        norm_sums[1],
        query_grad,
        key_grad,
        value_grad,
        project_grad,
        norm_sums[2],
        norm_sums[3],
        gate_grad,
        up_grad,
        down_grad,
    )


def solution(mesh):
    rows = P(("dp", "mp"), None)
    in_specs = (
        rows,
        P(),
        P(),
        P(None, "mp"),
        P(None, "mp"),
        P(None, "mp"),
        P("mp", None),
        P(),
        P(),
        P(None, "mp"),
        P(None, "mp"),
        P("mp", None),
        rows,
        P(),
        P("dp"),
        P("dp"),
        P("dp"),
    )
    out_specs = (
        rows,
        rows,
        P(("dp", "mp")),
        P(("dp", "mp")),
        P("dp", "mp"),
        P("dp", "mp"),
        P("dp", "mp"),
        P("mp", "dp"),
        P(("dp", "mp")),
        P(("dp", "mp")),
        P("dp", "mp"),
        P("dp", "mp"),
        P("mp", "dp"),
    )
    return jax.shard_map(local, mesh=mesh, in_specs=in_specs, out_specs=out_specs, check_vma=False)
```

```python
import functools

import jax
import jax.numpy as jnp
import numpy as np
from jax import lax
from jax.experimental import pallas as pl
from jax.experimental.pallas import tpu as pltpu
from jax.sharding import PartitionSpec as P

HEAD_DIM = 64
EPS = 1e-05
NEG = -1e30
F32 = jnp.float32
BF16 = jnp.bfloat16
NT = (((1,), (1,)), ((), ()))
NN = (((1,), (0,)), ((), ()))
MIB = 1024 * 1024
ONES = 16
WIDTH = 512


def product(a, b, dims=NN):
    return lax.dot_general(a, b, dims, preferred_element_type=F32)


def lanes_of(shape):
    return lax.broadcasted_iota(jnp.int32, shape, 1)


def limits(mebibytes):
    return pltpu.CompilerParams(vmem_limit_bytes=mebibytes * MIB)


def cost(flops):
    return pl.CostEstimate(flops=flops // MIB, bytes_accessed=0, transcendentals=0)


def shape_of(dims, kind):
    return jax.ShapeDtypeStruct(dims, kind)


ONCE = pl.Buffered(1)
SMALL = pl.BlockSpec(memory_space=pltpu.SMEM)


def fixed(dims, at=None):
    place = (0,) * len(dims) if at is None else at
    return pl.BlockSpec(dims, lambda *_: place, pipeline_mode=ONCE)


def normalize(v):
    centred = v - jnp.mean(v, -1, keepdims=True)
    inv_std = lax.rsqrt(jnp.mean(centred * centred, -1, keepdims=True) + EPS)
    return centred * inv_std, inv_std


def norm_back(upstream, x_hat, inv_std, gain):
    scaled = upstream * gain
    return inv_std * (
        scaled - jnp.mean(scaled, -1, keepdims=True) - x_hat * jnp.mean(scaled * x_hat, -1, keepdims=True)
    )


def norm_kernel(x_ref, gain_ref, shift_ref, n_ref):
    x_hat, _ = normalize(x_ref[...].astype(F32))
    n_ref[...] = (x_hat * gain_ref[...] + shift_ref[...]).astype(BF16)


def norm_rows(x, gain, shift, block=256):
    rows, dim = x.shape
    spec = pl.BlockSpec((block, dim), lambda i: (i, 0))
    return pl.pallas_call(
        norm_kernel,
        out_shape=shape_of((rows, dim), BF16),
        grid=(rows // block,),
        in_specs=[spec, fixed((1, dim)), fixed((1, dim))],
        out_specs=spec,
        compiler_params=limits(60),
        cost_estimate=cost(0),
        name="norm_rows",
    )(x, gain[None], shift[None])


def rotate(u, cos, sin, sign):
    lane = lanes_of(u.shape)
    half = HEAD_DIM // 2
    turned = jnp.where(lane % HEAD_DIM < half, -pltpu.roll(u, 128 - half, 1), pltpu.roll(u, half, 1))
    return u * cos + sign * turned * sin


def project_kernel(with_query, sel, own_ref, other_ref, *rest):
    if with_query:
        wq_ref, wk_ref, wv_ref, cos_ref, sin_ref, q_ref, k_ref, v_ref = rest
        todo = ((wq_ref, q_ref, HEAD_DIM**-0.5), (wk_ref, k_ref, 1.0))
    else:
        wk_ref, wv_ref, cos_ref, sin_ref, k_ref, v_ref = rest
        todo = ((wk_ref, k_ref, 1.0),)

    def work(n):
        cos, sin = cos_ref[...], sin_ref[...]
        for w_ref, out_ref, scale in todo:
            u = product(n, w_ref[...])
            for g in range(u.shape[1] // 128):
                cols = slice(g * 128, (g + 1) * 128)
                turned = rotate(u[:, cols], cos, sin, 1.0).astype(BF16)
                out_ref[:, cols] = (turned.astype(F32) * scale).astype(BF16)
        v_ref[...] = product(n, wv_ref[...]).astype(BF16)

    first = pl.program_id(0) < pl.num_programs(0) // 2
    work(jnp.where(first, own_ref[...], other_ref[...]))


def project(sel, own, other, weights, cos, sin, block=256):
    half, dim = own.shape
    cols = weights[0].shape[1]
    steps = 2 * half // block
    middle = steps // 2
    table = pl.BlockSpec((block, 128), lambda i, s: (s[0] * steps + i, 0))
    count = len(weights)
    return pl.pallas_call(
        functools.partial(project_kernel, count == 3),
        out_shape=(shape_of((2 * half, cols), BF16),) * count,
        grid_spec=pltpu.PrefetchScalarGridSpec(
            num_scalar_prefetch=1,
            grid=(steps,),
            in_specs=[
                pl.BlockSpec((block, dim), lambda i, s: (jnp.minimum(i, middle - 1), 0)),
                pl.BlockSpec((block, dim), lambda i, s: (jnp.maximum(i - middle, 0), 0)),
            ]
            + [fixed((dim, cols))] * count
            + [table, table],
            out_specs=[pl.BlockSpec((block, cols), lambda i, s: (i, 0))] * count,
        ),
        compiler_params=limits(60),
        cost_estimate=cost(half * dim * cols * count),
        name="project_rows",
    )(sel, own, other, *weights, cos, sin)


def middle_kernel(c_ref, co_ref, w_ref, wo_ref, x_ref, gain_ref, shift_ref, middle_ref, n_ref):
    middle = x_ref[...].astype(F32) + (product(c_ref[...], w_ref[...]) + product(co_ref[...], wo_ref[...]))
    middle_ref[...] = middle
    x_hat, _ = normalize(middle)
    n_ref[...] = (x_hat * gain_ref[...] + shift_ref[...]).astype(BF16)


def middle_rows(context, other, weight, weight_other, x, gain, shift, block=256):
    rows, dim = x.shape
    cols = context.shape[1]
    narrow = pl.BlockSpec((block, cols), lambda i: (i, 0))
    wide = pl.BlockSpec((block, dim), lambda i: (i, 0))
    return pl.pallas_call(
        middle_kernel,
        out_shape=(shape_of((rows, dim), F32), shape_of((rows, dim), BF16)),
        grid=(rows // block,),
        in_specs=[narrow, narrow, fixed((cols, dim)), fixed((cols, dim)), wide, fixed((1, dim)), fixed((1, dim))],
        out_specs=[wide, wide],
        compiler_params=limits(60),
        cost_estimate=cost(rows * dim * cols),
        name="middle_rows",
    )(context, other, weight, weight_other, x, gain[None], shift[None])


def add_sums(sums_ref, upstream, x_hat):
    row = lax.broadcasted_iota(jnp.int32, sums_ref.shape, 0)
    new = jnp.where(
        row == 0,
        jnp.sum(upstream * x_hat, 0, keepdims=True),
        jnp.where(row == 1, jnp.sum(upstream, 0, keepdims=True), 0.0),
    )
    first = pl.program_id(0) == 0

    @pl.when(first)
    def _():
        sums_ref[...] = new

    @pl.when(jnp.logical_not(first))
    def _():
        sums_ref[...] += new


def middle_back_kernel(d_ref, got1_ref, got2_ref, middle_ref, cot_ref, weight_ref, gain_ref, dm_ref, da_ref, sums_ref):
    upstream = d_ref[...] + (got1_ref[...].astype(F32) + got2_ref[...].astype(F32))
    x_hat, inv_std = normalize(middle_ref[...])
    d_middle = cot_ref[...].astype(F32) * weight_ref[...] + norm_back(upstream, x_hat, inv_std, gain_ref[...])
    dm_ref[...] = d_middle
    da_ref[...] = d_middle.astype(BF16)
    add_sums(sums_ref, upstream, x_hat)


def middle_back(parts, middle, cotangent, token_weight, gain, block=128):
    rows, dim = middle.shape
    wide = pl.BlockSpec((block, dim), lambda i: (i, 0))
    return pl.pallas_call(
        middle_back_kernel,
        out_shape=(shape_of((rows, dim), F32), shape_of((rows, dim), BF16), shape_of((8, dim), F32)),
        grid=(rows // block,),
        in_specs=[wide] * 5 + [pl.BlockSpec((block, 1), lambda i: (i, 0)), fixed((1, dim))],
        out_specs=[wide, wide, pl.BlockSpec((8, dim), lambda i: (0, 0))],
        compiler_params=limits(60),
        cost_estimate=cost(0),
        name="middle_back",
    )(*parts, middle, cotangent, token_weight, gain[None])


def first_back_kernel(d_ref, got_ref, far_ref, x_ref, dm_ref, gain_ref, out_ref, sums_ref):
    upstream = d_ref[...] + got_ref[...].astype(F32) + far_ref[...].astype(F32)
    x_hat, inv_std = normalize(x_ref[...].astype(F32))
    out_ref[...] = dm_ref[...] + norm_back(upstream, x_hat, inv_std, gain_ref[...])
    add_sums(sums_ref, upstream, x_hat)


def first_back(d_n1, got, far, x, d_middle, gain, block=128):
    rows, dim = x.shape
    wide = pl.BlockSpec((block, dim), lambda i: (i, 0))
    return pl.pallas_call(
        first_back_kernel,
        out_shape=(shape_of((rows, dim), F32), shape_of((8, dim), F32)),
        grid=(rows // block,),
        in_specs=[wide] * 5 + [fixed((1, dim))],
        out_specs=[wide, pl.BlockSpec((8, dim), lambda i: (0, 0))],
        compiler_params=limits(60),
        cost_estimate=cost(0),
        name="first_back",
    )(d_n1, got, far, x, d_middle, gain[None])


def rows_times_kernel(count, dims, mark, *refs):
    lefts, rights = refs[:count], refs[count : 2 * count]
    give_ref, own_ref = refs[2 * count :]
    total = product(
        jnp.concatenate([a[...] for a in lefts], 1),
        jnp.concatenate([a[...] for a in rights], 1 if dims is NT else 0),
        dims,
    )
    giving = pl.program_id(0) < pl.num_programs(0) // 2

    @pl.when(giving)
    def _():
        give_ref[...] = total.astype(BF16)

    @pl.when(jnp.logical_not(giving))
    def _():
        own_ref[...] = total


def rows_times(mark, terms, dims, block=256):
    rows = terms[0][0].shape[0]
    dim = terms[0][1].shape[0 if dims is NT else 1]
    steps = rows // block
    middle = steps // 2
    specs, rights = [], []
    for left, right, which in terms:
        depth = left.shape[1]
        specs.append(fixed((dim, depth), (0, which)) if dims is NT else fixed((depth, dim), (which, 0)))
    return pl.pallas_call(
        functools.partial(rows_times_kernel, len(terms), dims),
        out_shape=(shape_of((rows // 2, dim), BF16), shape_of((rows // 2, dim), F32)),
        grid=(steps,),
        in_specs=[SMALL]
        + [
            pl.BlockSpec((block, left.shape[1]), lambda i: ((i + middle) % steps, 0))
            for left, _, _ in terms
        ]
        + specs,
        out_specs=[
            pl.BlockSpec((block, dim), lambda i: (jnp.minimum(i, middle - 1), 0)),
            pl.BlockSpec((block, dim), lambda i: (jnp.maximum(i - middle, 0), 0)),
        ],
        compiler_params=limits(60),
        cost_estimate=cost(rows * dim * sum(left.shape[1] for left, _, _ in terms) // 2),
        name="rows_times",
    )(mark, *[t[0] for t in terms], *[t[1] for t in terms])


def key_side(k, h, bias):
    lane = lanes_of(k.shape)
    pos = lane % HEAD_DIM
    extra = jnp.where(pos < 3, 1.0, jnp.where(pos == 3, bias, 0.0))
    return jnp.where(lane // HEAD_DIM == h, k.astype(F32), extra).astype(BF16)


def row_side(q, h, stat):
    lane = lanes_of(q.shape)
    pos = lane % HEAD_DIM
    high = stat.astype(BF16).astype(F32)
    left = stat - high
    mid = left.astype(BF16).astype(F32)
    low = left - mid
    extra = jnp.where(
        pos == 0, high, jnp.where(pos == 1, mid, jnp.where(pos == 2, low, jnp.where(pos == 3, 1.0, 0.0)))
    )
    return jnp.where(lane // HEAD_DIM == h, q.astype(F32), extra).astype(BF16)


def only_head(q, h):
    return jnp.where(lanes_of(q.shape) // HEAD_DIM == h, q, jnp.zeros_like(q))


def key_bias(info, rows):
    row = lax.broadcasted_iota(jnp.int32, (rows, 128), 0)
    return jnp.where(lax.rem(row + info[2], rows) < info[1], 0.0, NEG)


def attend_kernel(own, sub, kb, info, q_ref, k_ref, v_ref, *rest):
    if own:
        o_ref, l_ref, m_ref, keys, values_t = rest
    else:
        o1_ref, l1_ref, m1_ref, c_ref, give_ref, lse_ref, keys, values_t = rest
    count = k_ref.shape[0]
    rows = q_ref.shape[0]

    def scores(unit):
        h, r = unit
        q = q_ref[r * sub : (r + 1) * sub, :]
        qa = row_side(q, h, jnp.zeros(q.shape, F32))
        parts = [product(keys[h, b * kb : (b + 1) * kb], qa, NT) for b in range(count // kb)]
        top = jnp.max(parts[0], 0, keepdims=True)
        for s in parts[1:]:
            top = jnp.maximum(top, jnp.max(s, 0, keepdims=True))
        return parts, top

    def combine(unit, parts, top):
        h, _ = unit
        total = None
        for b, s in enumerate(parts):
            p = jnp.exp(s - top).astype(BF16)
            x = product(values_t[h, :, b * kb : (b + 1) * kb], p)
            total = x if total is None else total + x
        return total[:HEAD_DIM], total[HEAD_DIM : HEAD_DIM + 1], top

    def work():
        bias = key_bias(info, count) if own else 0.0
        for h in range(2):
            keys[h] = key_side(k_ref[...], h, bias)
        flipped = v_ref[...].T
        for h in range(2):
            values_t[h, :HEAD_DIM] = flipped[h * HEAD_DIM : (h + 1) * HEAD_DIM]
            values_t[h, HEAD_DIM:] = jnp.ones((ONES, count), BF16)
        units = [(h, r) for r in range(rows // sub) for h in range(2)]
        ready = scores(units[0])
        done = {}
        for i, unit in enumerate(units):
            following = scores(units[i + 1]) if i + 1 < len(units) else None
            done[unit] = combine(unit, *ready)
            ready = following
        gathered = []
        for part in range(3):
            strips = []
            for r in range(rows // sub):
                strips.append(
                    jnp.concatenate(
                        [jnp.broadcast_to(done[(h, r)][part], (HEAD_DIM, sub)) for h in range(2)], 0
                    )
                )
            gathered.append(jnp.concatenate(strips, 1))
        return gathered

    def finish(o, l, m):
        context = (o / l).T.astype(BF16)
        c_ref[...] = context
        give_ref[...] = context[rows // 2 :]
        lse_ref[...] = pltpu.roll((m + jnp.log(l)).T, HEAD_DIM, 1)

    if own:
        o, l, m = work()
        o_ref[...] = o
        l_ref[...] = l
        m_ref[...] = m
    else:

        @pl.when(info[0] == 1)
        def _():
            o, l, m = work()
            m1 = m1_ref[...]
            top = jnp.maximum(m, m1)
            a1 = jnp.exp(m1 - top)
            a2 = jnp.exp(m - top)
            finish(o1_ref[...] * a1 + o * a2, l1_ref[...] * a1 + l * a2, top)

        @pl.when(info[0] != 1)
        def _():
            finish(o1_ref[...], l1_ref[...], m1_ref[...])


def attend(own, info, q, k, v, earlier=(), sub=256, kb=256):
    rows, cols = q.shape
    count = k.shape[0]
    wide = pl.BlockSpec((rows, 128), lambda p, s: (0, p))
    tall = pl.BlockSpec((128, rows), lambda p, s: (p, 0))
    upright = jax.ShapeDtypeStruct((cols, rows), F32)
    if own:
        outs = (upright,) * 3
    else:
        outs = (
            jax.ShapeDtypeStruct((rows, cols), BF16),
            jax.ShapeDtypeStruct((rows // 2, cols), BF16),
            jax.ShapeDtypeStruct((rows, cols), F32),
        )
    return pl.pallas_call(
        functools.partial(attend_kernel, own, sub, kb),
        out_shape=outs,
        grid_spec=pltpu.PrefetchScalarGridSpec(
            num_scalar_prefetch=1,
            grid=(cols // 128,),
            in_specs=[wide, pl.BlockSpec((count, 128), lambda p, s: (0, p)), pl.BlockSpec((count, 128), lambda p, s: (0, p))]
            + [tall] * len(earlier),
            out_specs=[tall] * 3 if own else [wide, pl.BlockSpec((rows // 2, 128), lambda p, s: (0, p)), wide],
            scratch_shapes=[
                pltpu.VMEM((2, count, 128), BF16),
                pltpu.VMEM((2, HEAD_DIM + ONES, count), BF16),
            ],
        ),
        compiler_params=limits(60),
        cost_estimate=cost(4 * rows * count * cols),
        name="attend_own" if own else "attend_far",
    )(info, q, k, v, *earlier)


def turn(out, parts):
    each = out.shape[1]
    size = 256
    unit = (lax.broadcasted_iota(jnp.int32, (size, size), 0) == lax.broadcasted_iota(jnp.int32, (size, size), 1)).astype(
        F32
    ).astype(BF16)
    at = 0
    for n_ref in parts:
        rows, dim = n_ref.shape
        for j in range(dim // size):
            flipped = product(unit, n_ref[:, j * size : (j + 1) * size], NT).astype(BF16)
            out[j * size // each : (j + 1) * size // each, :, at : at + rows] = flipped.reshape(
                size // each, each, rows
            )
        at += rows


def place(grads, j, count, gb):
    j, out = j % (count // 2), grads[j // (count // 2)]
    return out, slice(j * gb, (j + 1) * gb)


def rows_in_order(turned, order, j, gb, first=0):
    per = gb // turned.shape[1]
    return jnp.concatenate([turned[order[first + j * per + i]] for i in range(per)], 0)


def heads_back(q, g, k_ref, v_ref, c, lse, bias, scratch, kb):
    keys, values, keys_t, dk_sum, dv_sum = scratch
    count = k_ref.shape[0]
    for h in range(2):
        keys[h] = key_side(k_ref[...], h, bias)
        values[h] = key_side(v_ref[...], h, 0.0)
        keys_t[h] = only_head(k_ref[...], h).T
    lane = lanes_of(q.shape)
    overlap = g.astype(F32) * c.astype(F32)
    dq = None
    for h in range(2):
        qa = row_side(q, h, -lse)
        delta = jnp.sum(jnp.where(lane // HEAD_DIM == h, overlap, 0.0), -1, keepdims=True)
        ga = row_side(g, h, jnp.broadcast_to(-delta, q.shape))
        qm = only_head(q, h)
        gm = only_head(g, h)
        for b in range(count // kb):
            rows = slice(b * kb, (b + 1) * kb)
            p = jnp.exp(product(keys[h, rows], qa, NT))
            ds = (p * product(values[h, rows], ga, NT)).astype(BF16)
            dv = product(p.astype(BF16), gm)
            dk = product(ds, qm)
            if h == 0:
                dv_sum[rows] = dv
                dk_sum[rows] = dk
            else:
                dv_sum[rows] += dv
                dk_sum[rows] += dk
            part = product(keys_t[h, :, rows], ds)
            dq = part if dq is None else dq + part
    return dq.T * (HEAD_DIM**-0.5)


def heads_scratch(count):
    return [
        pltpu.VMEM((2, count, 128), BF16),
        pltpu.VMEM((2, count, 128), BF16),
        pltpu.VMEM((2, 128, count), BF16),
        pltpu.VMEM((count, 128), F32),
        pltpu.VMEM((count, 128), F32),
    ]


def pair_lanes(pair, first=0):
    return pl.ds(pl.multiple_of(first + pair * 128, 128), 128)


def copies(sources, targets, sems):
    return [pltpu.make_async_copy(a, b, sems.at[i]) for i, (a, b) in enumerate(zip(sources, targets))]


def far_kernel(kb, info, q_ref, k_ref, v_ref, c_ref, lse_ref, cos_ref, sin_ref, d_ref, do_ref, wo_ref, *rest):
    wk_hbm, wv_hbm, g_ref, dq_ref, dk_ref, dv_ref, give_ref, own_ref, kv, wk, wv, sems, *scratch = rest
    pair = pl.program_id(0)
    last = pl.num_programs(0) - 1
    half = d_ref.shape[0]
    cols = wk.shape[1]
    joined = info[0] == 1

    @pl.when(pair == 0)
    def _():
        for c in copies((wk_hbm, wv_hbm), (wk, wv), sems):
            c.start()
        g_ref[:half] = product(d_ref[...], wo_ref[...], NT).astype(BF16)
        g_ref[half:] = product(do_ref[...], wo_ref[...], NT).astype(BF16)

    @pl.when(joined)
    def _():
        g = g_ref[:, pair_lanes(pair)]
        dq_ref[...] = heads_back(q_ref[...], g, k_ref, v_ref, c_ref[...], lse_ref[...], 0.0, scratch, kb)
        dk = rotate(scratch[3][...], cos_ref[...], sin_ref[...], -1.0).astype(BF16)
        dv = scratch[4][...].astype(BF16)
        dk_ref[...] = dk
        dv_ref[...] = dv
        kv[:, pair_lanes(pair)] = dk
        kv[:, pair_lanes(pair, cols)] = dv

    @pl.when(jnp.logical_not(joined))
    def _():
        dq_ref[...] = jnp.zeros_like(dq_ref)
        dk_ref[...] = jnp.zeros_like(dk_ref)
        dv_ref[...] = jnp.zeros_like(dv_ref)

    @pl.when(pair == last)
    def _():
        for c in copies((wk_hbm, wv_hbm), (wk, wv), sems):
            c.wait()

    @pl.when(jnp.logical_and(pair == last, joined))
    def _():
        w = jnp.concatenate([wk[...], wv[...]], 1)
        give_ref[...] = product(kv[half:], w, NT).astype(BF16)
        own_ref[...] = product(kv[:half], w, NT)

    @pl.when(jnp.logical_and(pair == last, jnp.logical_not(joined)))
    def _():
        give_ref[...] = jnp.zeros_like(give_ref)
        own_ref[...] = jnp.zeros_like(own_ref)


def attend_back_far(info, q, k, v, c, lse, tables, d, d_other, wo, wk, wv, kb=1024):
    rows, cols = q.shape
    count = k.shape[0]
    dim = wk.shape[0]
    half = d.shape[0]
    wide = pl.BlockSpec((rows, 128), lambda p, s: (0, p))
    table = pl.BlockSpec((count, 128), lambda p, s: (s[4], 0), pipeline_mode=ONCE)
    anywhere = pl.BlockSpec(memory_space=pl.ANY)
    out = shape_of((rows, cols), BF16)
    return pl.pallas_call(
        functools.partial(far_kernel, kb),
        out_shape=(
            out,
            shape_of((rows, cols), F32),
            out,
            out,
            shape_of((half, dim), BF16),
            shape_of((half, dim), F32),
        ),
        grid_spec=pltpu.PrefetchScalarGridSpec(
            num_scalar_prefetch=1,
            grid=(cols // 128,),
            in_specs=[wide] * 5
            + [table, table, fixed(d.shape), fixed(d.shape), fixed(wo.shape), anywhere, anywhere],
            out_specs=[fixed((rows, cols)), wide, wide, wide, fixed((half, dim)), fixed((half, dim))],
            scratch_shapes=[
                pltpu.VMEM((count, 2 * cols), BF16),
                pltpu.VMEM(wk.shape, BF16),
                pltpu.VMEM(wv.shape, BF16),
                pltpu.SemaphoreType.DMA((2,)),
            ]
            + heads_scratch(count),
        ),
        compiler_params=limits(60),
        cost_estimate=cost(8 * rows * count * cols),
        name="attend_back_far",
    )(info, q, k, v, c, lse, *tables, d, d_other, wo, wk, wv)


def own_kernel(kb, gb, at, pairs, with_context, info, order, q_ref, k_ref, v_ref, c_ref, lse_ref, g_ref, before_ref, *rest):
    cos_ref, sin_ref, *rest = rest
    late = 12 if with_context else 11
    hbm, rest = rest[:late], rest[late:]
    give_ref, own_ref, *rest = rest
    grads, rest = rest[:2], rest[2:]
    vmem, (qkv, sems, *rest) = rest[:late], rest[late:]
    scratch, turned = rest[:5], rest[5:]
    n_ref, no_ref, f_ref, fo_ref, kf_ref, vf_ref, wq, wk, wv = vmem[:9]
    pair = pl.program_id(0)
    half = n_ref.shape[0]
    cols = 128 * pairs
    part = pl.ds(at * 128, cols)
    sources = list(hbm)
    for i in range(4, 9):
        sources[i] = hbm[i].at[:, part]

    @pl.when(pair == 0)
    def _():
        for c in copies(sources, vmem, sems):
            c.start()

    bias = key_bias(info, k_ref.shape[0])
    dq = heads_back(q_ref[...], g_ref[...], k_ref, v_ref, c_ref[...], lse_ref[...], bias, scratch, kb)
    cos, sin = cos_ref[...], sin_ref[...]
    qkv[:, pair_lanes(pair)] = rotate(dq + before_ref[...], cos, sin, -1.0).astype(BF16)
    qkv[:, pair_lanes(pair, cols)] = rotate(scratch[3][...], cos, sin, -1.0).astype(BF16)
    qkv[:, pair_lanes(pair, 2 * cols)] = scratch[4][...].astype(BF16)

    @pl.when(pair == pl.num_programs(0) - 1)
    def _():
        for c in copies(sources, vmem, sems):
            c.wait()
        w = jnp.concatenate([wq[...], wk[...], wv[...]], 1)
        if with_context:
            give_ref[...] = product(qkv[half:], w, NT)
            own_ref[...] = product(qkv[:half], w, NT)
        else:
            give_ref[...] = (product(qkv[half:], w, NT) + vmem[9][...]).astype(BF16)
            own_ref[...] = product(qkv[:half], w, NT) + vmem[10][...]
        nt, ft, *dt = turned
        turn(nt, (n_ref, no_ref))
        turn(ft, (f_ref, fo_ref))
        if with_context:
            turn(dt[0], vmem[9:11])
        blocks, each, _ = nt.shape
        dim = blocks * each
        for j in range(dim // gb):
            out, rows = place(grads, j, dim // gb, gb)
            left = rows_in_order(nt, order, j, gb)
            far = rows_in_order(ft, order, j, gb)
            both = product(left, qkv[...])
            out[rows, :cols] = both[:, :cols].astype(BF16)
            for i, other in ((1, kf_ref), (2, vf_ref)):
                columns = slice(i * cols, (i + 1) * cols)
                out[rows, columns] = (both[:, columns] + product(far, other[...])).astype(BF16)
            if with_context:
                out[rows, 3 * cols :] = product(rows_in_order(dt[0], order, j, gb), vmem[11][...]).astype(BF16)


def attend_back_own(info, order, q, k, v, c, lse, tables, g, before, lefts, far, weights, blocks, at, pairs, context=(), before_rows=(), gb=256, kb=1024):
    rows = q.shape[0]
    cols = 128 * pairs
    count = k.shape[0]
    half, dim = lefts[0].shape
    wide = pl.BlockSpec((rows, 128), lambda p, s, o: (0, p + at))
    table = pl.BlockSpec((rows, 128), lambda p, s, o: (s[3], 0), pipeline_mode=ONCE)
    anywhere = pl.BlockSpec(memory_space=pl.ANY)
    extra = context[2].shape[1] if context else 0
    grads = shape_of((dim // 2, 3 * cols + extra), BF16)
    turned = pltpu.VMEM((blocks, dim // blocks, rows), BF16)
    late = [*lefts, *far, *weights, *context, *before_rows]
    shapes = [a.shape for a in lefts] + [(count, cols)] * 2 + [(dim, cols)] * 3 + [a.shape for a in context]
    landing = [pltpu.VMEM(dims, BF16) for dims in shapes] + [pltpu.VMEM(a.shape, F32) for a in before_rows]
    return pl.pallas_call(
        functools.partial(own_kernel, kb, gb, at, pairs, bool(context)),
        out_shape=(shape_of((half, dim), F32 if context else BF16), shape_of((half, dim), F32), grads, grads),
        grid_spec=pltpu.PrefetchScalarGridSpec(
            num_scalar_prefetch=2,
            grid=(pairs,),
            in_specs=[wide] * 7 + [table, table] + [anywhere] * len(late),
            out_specs=[fixed((half, dim)), fixed((half, dim)), fixed(grads.shape), fixed(grads.shape)],
            scratch_shapes=landing
            + [pltpu.VMEM((rows, 3 * cols), BF16), pltpu.SemaphoreType.DMA((len(late),))]
            + heads_scratch(count)
            + [turned] * (3 if context else 2),
        ),
        compiler_params=limits(60),
        cost_estimate=cost(8 * rows * count * cols),
        name="attend_back_own",
    )(info, order, q, k, v, c, lse, g, before, *tables, *late)


def gated_kernel(gb, rb, again, order, n_ref, no_ref, b_ref, bo_ref, wg_ref, wu_ref, wd_ref, *rest):
    if again:
        before_hbm, *rest, before, sem = rest
    hid_ref, own_ref, give_ref, *grads, down_ref, dg, du, acc, nt, bt = rest
    step = pl.program_id(0)
    half_rows, dim = n_ref.shape
    width = wg_ref.shape[1]

    @pl.when(step == 0)
    def _():
        if again:
            pltpu.make_async_copy(before_hbm, before, sem).start()
        turn(nt, (n_ref, no_ref))
        turn(bt, (b_ref, bo_ref))
        acc[...] = jnp.zeros_like(acc)

    for r in range(2 * half_rows // rb):
        rows_ref, d_ref = ((n_ref, b_ref), (no_ref, bo_ref))[r * rb // half_rows]
        inner = slice(r * rb % half_rows, r * rb % half_rows + rb)
        part = slice(r * rb, (r + 1) * rb)
        n = rows_ref[inner]
        gate = product(n, wg_ref[...])
        up = product(n, wu_ref[...])
        d_hidden = product(d_ref[inner], wd_ref[...], NT)
        s = 0.5 * jnp.tanh(0.5 * gate) + 0.5
        silu = gate * s
        hid_ref[part] = (silu * up).astype(BF16)
        d_gate = (d_hidden * up * (s * (1.0 + gate * (1.0 - s)))).astype(BF16)
        d_up = (d_hidden * silu).astype(BF16)
        dg[part] = d_gate
        du[part] = d_up
        acc[part] += product(
            jnp.concatenate([d_gate, d_up], 1), jnp.concatenate([wg_ref[...], wu_ref[...]], 1), NT
        )

    for j in range(dim // gb):
        left = rows_in_order(nt, order, j, gb)
        out, part = place(grads, j, dim // gb, gb)
        out[part, :width] = product(left, dg[...]).astype(BF16)
        out[part, width:] = product(left, du[...]).astype(BF16)
        left = rows_in_order(bt, order, j, gb, nt.shape[0])
        down_ref[j * gb : (j + 1) * gb] = product(left, hid_ref[...]).astype(BF16)

    @pl.when(step == pl.num_programs(0) - 1)
    def _():
        if again:
            pltpu.make_async_copy(before_hbm, before, sem).wait()
            own_ref[...] = acc[:half_rows] + before[...]
        else:
            own_ref[...] = acc[:half_rows]
        give_ref[...] = acc[half_rows:].astype(BF16)


def gated_units(order, rows_in, wg, wu, wd, blocks, first, last, before=(), width=WIDTH, gb=256, rb=512):
    half, dim = rows_in[0].shape
    rows = 2 * half
    steps = (last - first) // width
    at = first // width
    columns = pl.BlockSpec((dim, width), lambda s, o: (0, s + at))
    grads = shape_of((dim // 2, 2 * (last - first)), BF16)
    grad_spec = pl.BlockSpec((dim // 2, 2 * width), lambda s, o: (0, s))
    split = pl.BlockSpec((half, dim), lambda s, o: (0, 0))
    return pl.pallas_call(
        functools.partial(gated_kernel, gb, rb, bool(before)),
        out_shape=(shape_of((rows, last - first), BF16), shape_of((half, dim), F32), shape_of((half, dim), BF16))
        + (grads, grads, shape_of((dim, last - first), BF16)),
        grid_spec=pltpu.PrefetchScalarGridSpec(
            num_scalar_prefetch=1,
            grid=(steps,),
            in_specs=[fixed((half, dim))] * 4
            + [columns, columns, pl.BlockSpec((width, dim), lambda s, o: (s + at, 0))]
            + [pl.BlockSpec(memory_space=pl.ANY)] * len(before),
            out_specs=[pl.BlockSpec((rows, width), lambda s, o: (0, s)), split, split]
            + [grad_spec, grad_spec, pl.BlockSpec((dim, width), lambda s, o: (0, s))],
            scratch_shapes=[
                pltpu.VMEM((rows, width), BF16),
                pltpu.VMEM((rows, width), BF16),
                pltpu.VMEM((rows, dim), F32),
                pltpu.VMEM((blocks, dim // blocks, rows), BF16),
                pltpu.VMEM((blocks, dim // blocks, rows), BF16),
            ]
            + [pltpu.VMEM(a.shape, F32) for a in before]
            + [pltpu.SemaphoreType.DMA] * len(before),
        ),
        compiler_params=limits(60),
        cost_estimate=cost(4 * rows * dim * (last - first)),
        name="gated_units",
    )(order, *rows_in, wg, wu, wd, *before)


def unpack_gated_kernel(first_ref, second_ref, down12_ref, gate_ref, up_ref, down_ref):
    at = 0
    for ref in (first_ref, second_ref):
        for step in range(ref.shape[1] // (2 * WIDTH)):
            base = 2 * step * WIDTH
            cols = slice(at, at + WIDTH)
            gate_ref[:, cols] = ref[:, base : base + WIDTH].astype(F32)
            up_ref[:, cols] = ref[:, base + WIDTH : base + 2 * WIDTH].astype(F32)
            at += WIDTH
    down_ref[...] = down12_ref[...].astype(F32)


def unpack_gated(first, second, down):
    rows, units = first.shape
    whole = pl.BlockSpec(memory_space=pltpu.VMEM)
    return pl.pallas_call(
        unpack_gated_kernel,
        out_shape=(shape_of((rows, units), F32), shape_of((rows, units), F32), shape_of((rows, units), F32)),
        in_specs=[whole] * 3,
        out_specs=[whole] * 3,
        compiler_params=limits(60),
        cost_estimate=cost(0),
        name="unpack_gated",
    )(first, second, down)


def unpack_rest_kernel(first_ref, second_ref, q_ref, k_ref, v_ref, p_ref):
    at = 0
    for ref in (first_ref, second_ref):
        cols = (ref.shape[1] - (p_ref.shape[1] if ref is first_ref else 0)) // 3
        for i, out in enumerate((q_ref, k_ref, v_ref)):
            out[:, at : at + cols] = ref[:, i * cols : (i + 1) * cols].astype(F32)
        if ref is first_ref:
            p_ref[...] = ref[:, 3 * cols :].astype(F32)
        at += cols


def unpack_rest(first, second, cols):
    rows = first.shape[0]
    whole = pl.BlockSpec(memory_space=pltpu.VMEM)
    return pl.pallas_call(
        unpack_rest_kernel,
        out_shape=(shape_of((rows, cols), F32),) * 4,
        in_specs=[whole] * 2,
        out_specs=[whole] * 4,
        compiler_params=limits(60),
        cost_estimate=cost(0),
        name="unpack_rest",
    )(first, second)


def swap(value):
    return lax.ppermute(value, "mp", [(0, 1), (1, 0)])


def across(value, bit):
    return lax.ppermute(value, "dp", [(i, i ^ (1 << bit)) for i in range(lax.axis_size("dp"))])


def exchange(value, bits):
    size = lax.axis_size("dp")
    pairs = [(2 * i + c, 2 * (i ^ (1 << bit)) + c) for i in range(size) for c, bit in enumerate(bits)]
    return lax.ppermute(value, ("dp", "mp"), pairs)


def rounded_sum(parts):
    total = parts[0].astype(F32)
    for part in parts[1:]:
        total += part.astype(F32)
    return total.astype(BF16)


def first_half(parts):
    half = parts[0].shape[0] // 2
    return rounded_sum([p[:half] for p in parts])


def second_halves(parts):
    half = parts[0].shape[0] // 2
    return [p[half:] for p in parts]


def scatter_rest(quarters):
    size = lax.axis_size("dp")
    groups = [[b + 4 * k for k in range(size // 4)] for b in range(4)]
    return lax.psum_scatter(quarters, "dp", scatter_dimension=0, axis_index_groups=groups, tiled=True)


def later_bits():
    return range(2, lax.axis_size("dp").bit_length() - 1)


def sum_all(value):
    value = value + swap(value)
    for bit in range(lax.axis_size("dp").bit_length() - 1):
        value = value + across(value, bit)
    return value


def after(value, done):
    return lax.optimization_barrier((value, done))[0]


def block_orders():
    size = lax.axis_size("dp")
    me = lax.axis_index("dp")
    first_core = lax.axis_index("mp") == 0
    count = size.bit_length() - 1
    places = np.arange(size)
    results = []
    for halved in (2, count):
        flows = []
        for outer, inner in ((0, 1), (1, 0)):
            flipped = np.zeros(size, np.int32)
            for position, bit in enumerate((outer, inner, *range(2, halved))):
                flipped |= (1 - ((places >> (count - 1 - position)) & 1)).astype(np.int32) << bit
            if halved == 2:
                plain = (places % (size // 4)).astype(np.int32) * 4
                flows.append((jnp.asarray(flipped) ^ (me & 3)) | jnp.asarray(plain))
            else:
                flows.append(jnp.asarray(flipped) ^ me)
        results.append(jnp.where(first_core, flows[0], flows[1]).astype(jnp.int32))
    within = places % 4
    swapped = (within % 2) * 2 + within // 2
    flipped = jnp.where(first_core, jnp.asarray(3 - swapped), jnp.asarray(3 - within)) ^ (me & 3)
    last = ((places // 4) * 4 + flipped).astype(jnp.int32)
    return jnp.concatenate([results[0], last]), results[1]


def rotary_tables(slot_rows):
    half_dim = HEAD_DIM // 2
    frequency = (10000.0 ** (-(np.arange(half_dim) * 2.0 / HEAD_DIM))).astype(np.float32)
    within = np.arange(slot_rows)
    tables = []
    for window_half in range(2):
        for shift in (0, slot_rows // 2):
            tables.append((within + shift) % slot_rows + window_half * slot_rows)
    angles = np.concatenate(tables).astype(np.float32)[:, None] * frequency[None, :]
    angles = np.tile(angles.astype(np.float64), (1, 4))
    return np.cos(angles).astype(np.float32), np.sin(angles).astype(np.float32)


def local(
    inputs,
    first_gain,
    first_shift,
    query_weight,
    key_weight,
    value_weight,
    output_weight,
    second_gain,
    second_shift,
    gate_weight,
    up_weight,
    down_weight,
    cotangent,
    species_weight,
    species_ids,
    slot_bucket,
    slot_length,
):
    half_rows = inputs.shape[0]
    slot_rows = 2 * half_rows
    blocks = lax.axis_size("dp")
    core = lax.axis_index("mp")
    parity = lax.axis_index("dp") % 2
    joined = slot_bucket[0]
    length = slot_length[0]
    start = core * half_rows
    own_table = 2 * parity * joined + core
    far_table = 2 * (1 - parity) * joined + core
    info = jnp.stack([joined, length, start, own_table, far_table]).astype(jnp.int32)
    order, order_all = block_orders()
    tables = rotary_tables(slot_rows)
    units = gate_weight.shape[1]
    pairs = query_weight.shape[1] // 128
    few = pairs // 2

    cot_other = swap(cotangent)
    output_weight_other = swap(output_weight)
    n1_own = norm_rows(inputs, first_gain, first_shift)
    n1_far_own = across(n1_own, 0)
    n1_other = swap(n1_own)
    q, k, v = project(info[3:4], n1_own, n1_other, (query_weight, key_weight, value_weight), *tables)
    earlier = attend(True, info, q, k, v)

    n1_far_own = after(n1_far_own, earlier[2])
    n1_far_other = swap(n1_far_own)
    token_index = (jnp.arange(slot_rows, dtype=jnp.int32) + start) % slot_rows
    table_index = jnp.arange(species_weight.shape[0], dtype=jnp.int32)
    slot_weight = jnp.sum(jnp.where(table_index == species_ids[0], species_weight, 0.0))
    token_weight = jnp.where(token_index < length, slot_weight, 0.0)[:, None]
    late_cot, late_other = after((cotangent, cot_other), earlier[2])
    d_branch = [
        (c.astype(F32) * w).astype(BF16)
        for c, w in ((late_cot, token_weight[:half_rows]), (late_other, token_weight[half_rows:]))
    ]
    k_far, v_far = project(
        after(info[4:5], d_branch), n1_far_own, n1_far_other, (key_weight, value_weight), *tables
    )
    context, context_give, log_total = attend(False, info, q, k_far, v_far, tuple(earlier))
    middle, n2_own = middle_rows(
        context, swap(context_give), output_weight, output_weight_other, inputs, second_gain, second_shift
    )
    rows_in = (n2_own, swap(n2_own), *d_branch)

    gated = functools.partial(gated_units, order, rows_in, gate_weight, up_weight, down_weight, blocks)
    near, off = (0, 1), (1, 0)
    hidden_1, d_n2_1, give_1, sent, parts_1, down_1 = gated(0, units // 2)
    got_1 = exchange(sent, near)
    down_1 = scatter_rest(down_1)
    hidden_2, d_n2, give_2, sent, parts_2, down_2 = gated(units // 2, units, (d_n2_1,))
    got_2 = exchange(sent, near)
    down_2 = scatter_rest(down_2)
    d_middle, d_attended, second_sums = middle_back(
        (d_n2, swap(give_1), swap(give_2)), middle, cotangent, token_weight, second_gain
    )
    d_attended_other = swap(d_attended)
    parts_1 = [parts_1, after(got_1, d_attended)]
    onward_1 = first_half(parts_1)
    again_1 = exchange(onward_1, off)

    d_context, dq_far, dk_far, dv_far, d_far_give, d_far = attend_back_far(
        after(info, onward_1),
        q,
        k_far,
        v_far,
        context,
        log_total,
        tables,
        d_attended,
        d_attended_other,
        output_weight,
        key_weight,
        value_weight,
    )
    got_2, again_1 = after((got_2, again_1), dq_far)
    parts_2 = [parts_2, got_2]
    onward_2 = first_half(parts_2)
    again_2 = exchange(onward_2, off)
    kept_1 = rounded_sum([*second_halves(parts_1), again_1])
    gated_1 = scatter_rest(kept_1)
    d_far_got = after(swap(d_far_give), (kept_1, onward_2))
    d_far = rounded_sum([d_far, d_far_got])
    d_far_back = across(d_far, 0)

    own_back = functools.partial(
        attend_back_own,
        q=q,
        k=k,
        v=v,
        c=context,
        lse=log_total,
        tables=tables,
        g=d_context,
        before=dq_far,
        lefts=(n1_own, n1_other, n1_far_own, n1_far_other),
        far=(dk_far, dv_far),
        weights=(query_weight, key_weight, value_weight),
        blocks=blocks,
        pairs=few,
    )
    d_n1_give, d_n1, sent, parts_3 = own_back(
        after(info, (kept_1, onward_2, d_far)), order_all, at=0, context=(d_attended, d_attended_other, context)
    )
    got_3 = exchange(sent, near)
    again_2, down_1, down_2 = after((again_2, down_1, down_2), parts_3)
    kept_2 = rounded_sum([*second_halves(parts_2), again_2])
    gated_2 = scatter_rest(kept_2)
    downs = [jnp.concatenate([down_1, down_2], 1)]
    down_send = first_half(downs)
    down_got = exchange(down_send, near)
    branch_give, branch = rows_times(
        after(order, (kept_2, down_send)), ((hidden_1, down_weight, 0), (hidden_2, down_weight, 1)), NN
    )
    d_n1_give, d_n1, sent, parts_4 = own_back(
        after(info, (branch_give, gated_1, d_far_back)), order_all, at=few, before_rows=(d_n1_give, d_n1)
    )
    got_4 = exchange(sent, near)
    got_3, down_got = after((got_3, down_got), parts_4)
    parts_3 = [parts_3, got_3]
    onward_3 = first_half(parts_3)
    again_3 = exchange(onward_3, off)
    downs = [*second_halves(downs), down_got]
    down_again = exchange(first_half(downs), off)
    d_n1_got = after(swap(d_n1_give), (onward_3, gated_2))
    input_grad, first_sums = first_back(d_n1, d_n1_got, d_far_back, inputs, d_middle, first_gain)
    parts_4 = [parts_4, after(got_4, first_sums)]
    again_4 = exchange(first_half(parts_4), off)
    parts_3 = [*second_halves(parts_3), after(again_3, first_sums)]
    parts_4 = [*second_halves(parts_4), again_4]
    for bit in later_bits():
        from_3 = across(first_half(parts_3), bit)
        from_4 = across(first_half(parts_4), bit)
        parts_3 = [*second_halves(parts_3), from_3]
        parts_4 = [*second_halves(parts_4), from_4]
    rest_1 = rounded_sum(parts_3)
    rest_2 = rounded_sum(parts_4)
    down = rounded_sum([*second_halves(downs), down_again])
    output = (middle + branch + swap(branch_give).astype(F32)).astype(BF16)

    norm_sums = sum_all(jnp.concatenate([first_sums[:2], second_sums[:2]], 0))
    share = norm_sums.shape[1] // (2 * blocks)
    norm_sums = lax.dynamic_slice_in_dim(norm_sums, (2 * lax.axis_index("dp") + core) * share, share, 1)
    gate_grad, up_grad, down_grad = unpack_gated(gated_1, gated_2, down)
    query_grad, key_grad, value_grad, project_grad = unpack_rest(rest_1, rest_2, query_weight.shape[1])
    return (
        output,
        input_grad,
        norm_sums[0],
        norm_sums[1],
        query_grad,
        key_grad,
        value_grad,
        project_grad.T,
        norm_sums[2],
        norm_sums[3],
        gate_grad,
        up_grad,
        down_grad.T,
    )


def solution(mesh):
    rows = P(("dp", "mp"), None)
    in_specs = (
        rows,
        P(),
        P(),
        P(None, "mp"),
        P(None, "mp"),
        P(None, "mp"),
        P("mp", None),
        P(),
        P(),
        P(None, "mp"),
        P(None, "mp"),
        P("mp", None),
        rows,
        P(),
        P("dp"),
        P("dp"),
        P("dp"),
    )
    out_specs = (
        rows,
        rows,
        P(("dp", "mp")),
        P(("dp", "mp")),
        P("dp", "mp"),
        P("dp", "mp"),
        P("dp", "mp"),
        P("mp", "dp"),
        P(("dp", "mp")),
        P(("dp", "mp")),
        P("dp", "mp"),
        P("dp", "mp"),
        P("mp", "dp"),
    )
    return jax.shard_map(local, mesh=mesh, in_specs=in_specs, out_specs=out_specs, check_vma=False)
```

```python
import functools

import jax
import jax.numpy as jnp
import numpy as np
from jax import lax
from jax.experimental import pallas as pl
from jax.experimental.pallas import tpu as pltpu
from jax.sharding import PartitionSpec as P

HEAD_DIM = 64
EPS = 1e-05
NEG = -1e30
F32 = jnp.float32
BF16 = jnp.bfloat16
NT = (((1,), (1,)), ((), ()))
NN = (((1,), (0,)), ((), ()))
MIB = 1024 * 1024
ONES = 16
WIDTH = 512


def product(a, b, dims=NN):
    return lax.dot_general(a, b, dims, preferred_element_type=F32)


def lanes_of(shape):
    return lax.broadcasted_iota(jnp.int32, shape, 1)


def limits(mebibytes):
    return pltpu.CompilerParams(vmem_limit_bytes=mebibytes * MIB)


def cost(us):
    return pl.CostEstimate(flops=0, bytes_accessed=us * 3500000, transcendentals=0)


def shape_of(dims, kind):
    return jax.ShapeDtypeStruct(dims, kind)


ONCE = pl.Buffered(1)
SMALL = pl.BlockSpec(memory_space=pltpu.SMEM)


def fixed(dims, at=None):
    place = (0,) * len(dims) if at is None else at
    return pl.BlockSpec(dims, lambda *_: place, pipeline_mode=ONCE)


def normalize(v):
    centred = v - jnp.mean(v, -1, keepdims=True)
    inv_std = lax.rsqrt(jnp.mean(centred * centred, -1, keepdims=True) + EPS)
    return centred * inv_std, inv_std


def norm_back(upstream, x_hat, inv_std, gain):
    scaled = upstream * gain
    return inv_std * (
        scaled - jnp.mean(scaled, -1, keepdims=True) - x_hat * jnp.mean(scaled * x_hat, -1, keepdims=True)
    )


def norm_kernel(x_ref, gain_ref, shift_ref, n_ref):
    x_hat, _ = normalize(x_ref[...].astype(F32))
    n_ref[...] = (x_hat * gain_ref[...] + shift_ref[...]).astype(BF16)


def norm_rows(x, gain, shift, block=256):
    rows, dim = x.shape
    spec = pl.BlockSpec((block, dim), lambda i: (i, 0))
    return pl.pallas_call(
        norm_kernel,
        out_shape=shape_of((rows, dim), BF16),
        grid=(rows // block,),
        in_specs=[spec, fixed((1, dim)), fixed((1, dim))],
        out_specs=spec,
        compiler_params=limits(60),
        cost_estimate=cost(2),
        name="norm_rows",
    )(x, gain[None], shift[None])


def rotate(u, cos, sin, sign):
    lane = lanes_of(u.shape)
    half = HEAD_DIM // 2
    turned = jnp.where(lane % HEAD_DIM < half, -pltpu.roll(u, 128 - half, 1), pltpu.roll(u, half, 1))
    return u * cos + sign * turned * sin


def project_kernel(with_query, sel, own_ref, other_ref, *rest):
    if with_query:
        wq_ref, wk_ref, wv_ref, cos_ref, sin_ref, q_ref, k_ref, v_ref = rest
        todo = ((wq_ref, q_ref, HEAD_DIM**-0.5), (wk_ref, k_ref, 1.0))
    else:
        wk_ref, wv_ref, cos_ref, sin_ref, k_ref, v_ref = rest
        todo = ((wk_ref, k_ref, 1.0),)

    def work(n):
        cos, sin = cos_ref[...], sin_ref[...]
        for w_ref, out_ref, scale in todo:
            u = product(n, w_ref[...])
            for g in range(u.shape[1] // 128):
                cols = slice(g * 128, (g + 1) * 128)
                turned = rotate(u[:, cols], cos, sin, 1.0).astype(BF16)
                out_ref[:, cols] = (turned.astype(F32) * scale).astype(BF16)
        v_ref[...] = product(n, wv_ref[...]).astype(BF16)

    first = pl.program_id(0) < pl.num_programs(0) // 2
    work(jnp.where(first, own_ref[...], other_ref[...]))


def project(sel, own, other, weights, cos, sin, block=256):
    half, dim = own.shape
    cols = weights[0].shape[1]
    steps = 2 * half // block
    middle = steps // 2
    table = pl.BlockSpec((block, 128), lambda i, s: (s[0] * steps + i, 0))
    count = len(weights)
    return pl.pallas_call(
        functools.partial(project_kernel, count == 3),
        out_shape=(shape_of((2 * half, cols), BF16),) * count,
        grid_spec=pltpu.PrefetchScalarGridSpec(
            num_scalar_prefetch=1,
            grid=(steps,),
            in_specs=[
                pl.BlockSpec((block, dim), lambda i, s: (jnp.minimum(i, middle - 1), 0)),
                pl.BlockSpec((block, dim), lambda i, s: (jnp.maximum(i - middle, 0), 0)),
            ]
            + [fixed((dim, cols))] * count
            + [table, table],
            out_specs=[pl.BlockSpec((block, cols), lambda i, s: (i, 0))] * count,
        ),
        compiler_params=limits(60),
        cost_estimate=cost(0),
        name="project_rows",
    )(sel, own, other, *weights, cos, sin)


def middle_kernel(c_ref, co_ref, w_ref, wo_ref, x_ref, gain_ref, shift_ref, middle_ref, n_ref):
    middle = x_ref[...].astype(F32) + (product(c_ref[...], w_ref[...]) + product(co_ref[...], wo_ref[...]))
    middle_ref[...] = middle
    x_hat, _ = normalize(middle)
    n_ref[...] = (x_hat * gain_ref[...] + shift_ref[...]).astype(BF16)


def middle_rows(context, other, weight, weight_other, x, gain, shift, block=256):
    rows, dim = x.shape
    cols = context.shape[1]
    narrow = pl.BlockSpec((block, cols), lambda i: (i, 0))
    wide = pl.BlockSpec((block, dim), lambda i: (i, 0))
    return pl.pallas_call(
        middle_kernel,
        out_shape=(shape_of((rows, dim), F32), shape_of((rows, dim), BF16)),
        grid=(rows // block,),
        in_specs=[narrow, narrow, fixed((cols, dim)), fixed((cols, dim)), wide, fixed((1, dim)), fixed((1, dim))],
        out_specs=[wide, wide],
        compiler_params=limits(60),
        cost_estimate=cost(5),
        name="middle_rows",
    )(context, other, weight, weight_other, x, gain[None], shift[None])


def add_sums(sums_ref, upstream, x_hat):
    row = lax.broadcasted_iota(jnp.int32, sums_ref.shape, 0)
    new = jnp.where(
        row == 0,
        jnp.sum(upstream * x_hat, 0, keepdims=True),
        jnp.where(row == 1, jnp.sum(upstream, 0, keepdims=True), 0.0),
    )
    first = pl.program_id(0) == 0

    @pl.when(first)
    def _():
        sums_ref[...] = new

    @pl.when(jnp.logical_not(first))
    def _():
        sums_ref[...] += new


def middle_back_kernel(info, weight, d_ref, got1_ref, got2_ref, middle_ref, cot_ref, gain_ref, dm_ref, da_ref, sums_ref):
    upstream = d_ref[...] + (got1_ref[...].astype(F32) + got2_ref[...].astype(F32))
    x_hat, inv_std = normalize(middle_ref[...])
    block, dim = cot_ref.shape
    row = lax.broadcasted_iota(jnp.int32, (block, dim), 0) + (info[2] + pl.program_id(0) * block)
    cot = cot_ref[...].astype(F32) * jnp.where(row < info[1], weight[0], 0.0)
    d_middle = cot + norm_back(upstream, x_hat, inv_std, gain_ref[...])
    dm_ref[...] = d_middle
    da_ref[...] = d_middle.astype(BF16)
    add_sums(sums_ref, upstream, x_hat)


def middle_back(info, weight, parts, middle, cotangent, gain, block=128):
    rows, dim = middle.shape
    wide = pl.BlockSpec((block, dim), lambda i: (i, 0))
    return pl.pallas_call(
        middle_back_kernel,
        out_shape=(shape_of((rows, dim), F32), shape_of((rows, dim), BF16), shape_of((8, dim), F32)),
        grid=(rows // block,),
        in_specs=[SMALL, SMALL] + [wide] * 5 + [fixed((1, dim))],
        out_specs=[wide, wide, pl.BlockSpec((8, dim), lambda i: (0, 0))],
        compiler_params=limits(60),
        cost_estimate=cost(0),
        name="middle_back",
    )(info, weight, *parts, middle, cotangent, gain[None])


def first_back_kernel(d_ref, got_ref, far_ref, x_ref, dm_ref, gain_ref, out_ref, sums_ref):
    upstream = d_ref[...] + got_ref[...].astype(F32) + far_ref[...].astype(F32)
    x_hat, inv_std = normalize(x_ref[...].astype(F32))
    out_ref[...] = dm_ref[...] + norm_back(upstream, x_hat, inv_std, gain_ref[...])
    add_sums(sums_ref, upstream, x_hat)


def first_back(d_n1, got, far, x, d_middle, gain, block=128):
    rows, dim = x.shape
    wide = pl.BlockSpec((block, dim), lambda i: (i, 0))
    return pl.pallas_call(
        first_back_kernel,
        out_shape=(shape_of((rows, dim), F32), shape_of((8, dim), F32)),
        grid=(rows // block,),
        in_specs=[wide] * 5 + [fixed((1, dim))],
        out_specs=[wide, pl.BlockSpec((8, dim), lambda i: (0, 0))],
        compiler_params=limits(60),
        cost_estimate=cost(6),
        name="first_back",
    )(d_n1, got, far, x, d_middle, gain[None])


def rows_times_kernel(count, dims, mark, *refs):
    lefts, rights = refs[:count], refs[count : 2 * count]
    give_ref, own_ref = refs[2 * count :]
    total = product(
        jnp.concatenate([a[...] for a in lefts], 1),
        jnp.concatenate([a[...] for a in rights], 1 if dims is NT else 0),
        dims,
    )
    giving = pl.program_id(0) < pl.num_programs(0) // 2

    @pl.when(giving)
    def _():
        give_ref[...] = total.astype(BF16)

    @pl.when(jnp.logical_not(giving))
    def _():
        own_ref[...] = total


def rows_times(mark, terms, dims, block=256):
    rows = terms[0][0].shape[0]
    dim = terms[0][1].shape[0 if dims is NT else 1]
    steps = rows // block
    middle = steps // 2
    specs, rights = [], []
    for left, right, which in terms:
        depth = left.shape[1]
        specs.append(fixed((dim, depth), (0, which)) if dims is NT else fixed((depth, dim), (which, 0)))
    return pl.pallas_call(
        functools.partial(rows_times_kernel, len(terms), dims),
        out_shape=(shape_of((rows // 2, dim), BF16), shape_of((rows // 2, dim), F32)),
        grid=(steps,),
        in_specs=[SMALL]
        + [
            pl.BlockSpec((block, left.shape[1]), lambda i: ((i + middle) % steps, 0))
            for left, _, _ in terms
        ]
        + specs,
        out_specs=[
            pl.BlockSpec((block, dim), lambda i: (jnp.minimum(i, middle - 1), 0)),
            pl.BlockSpec((block, dim), lambda i: (jnp.maximum(i - middle, 0), 0)),
        ],
        compiler_params=limits(60),
        cost_estimate=cost(9),
        name="rows_times",
    )(mark, *[t[0] for t in terms], *[t[1] for t in terms])


def key_side(k, h, bias):
    lane = lanes_of(k.shape)
    pos = lane % HEAD_DIM
    extra = jnp.where(pos < 3, 1.0, jnp.where(pos == 3, bias, 0.0))
    return jnp.where(lane // HEAD_DIM == h, k.astype(F32), extra).astype(BF16)


def row_side(q, h, stat):
    lane = lanes_of(q.shape)
    pos = lane % HEAD_DIM
    high = stat.astype(BF16).astype(F32)
    left = stat - high
    mid = left.astype(BF16).astype(F32)
    low = left - mid
    extra = jnp.where(
        pos == 0, high, jnp.where(pos == 1, mid, jnp.where(pos == 2, low, jnp.where(pos == 3, 1.0, 0.0)))
    )
    return jnp.where(lane // HEAD_DIM == h, q.astype(F32), extra).astype(BF16)


def only_head(q, h):
    return jnp.where(lanes_of(q.shape) // HEAD_DIM == h, q, jnp.zeros_like(q))


def key_bias(info, rows):
    row = lax.broadcasted_iota(jnp.int32, (rows, 128), 0)
    return jnp.where(lax.rem(row + info[2], rows) < info[1], 0.0, NEG)


def attend_kernel(own, sub, kb, info, q_ref, k_ref, v_ref, *rest):
    if own:
        o_ref, l_ref, m_ref, keys, values_t = rest
    else:
        o1_ref, l1_ref, m1_ref, c_ref, give_ref, lse_ref, keys, values_t = rest
    count = k_ref.shape[0]
    rows = q_ref.shape[0]

    def scores(unit):
        h, r = unit
        q = q_ref[r * sub : (r + 1) * sub, :]
        qa = row_side(q, h, jnp.zeros(q.shape, F32))
        parts = [product(keys[h, b * kb : (b + 1) * kb], qa, NT) for b in range(count // kb)]
        top = jnp.max(parts[0], 0, keepdims=True)
        for s in parts[1:]:
            top = jnp.maximum(top, jnp.max(s, 0, keepdims=True))
        return parts, top

    def combine(unit, parts, top):
        h, _ = unit
        total = None
        for b, s in enumerate(parts):
            p = jnp.exp(s - top).astype(BF16)
            x = product(values_t[h, :, b * kb : (b + 1) * kb], p)
            total = x if total is None else total + x
        return total[:HEAD_DIM], total[HEAD_DIM : HEAD_DIM + 1], top

    def work():
        bias = key_bias(info, count) if own else 0.0
        for h in range(2):
            keys[h] = key_side(k_ref[...], h, bias)
        flipped = v_ref[...].T
        for h in range(2):
            values_t[h, :HEAD_DIM] = flipped[h * HEAD_DIM : (h + 1) * HEAD_DIM]
            values_t[h, HEAD_DIM:] = jnp.ones((ONES, count), BF16)
        units = [(h, r) for r in range(rows // sub) for h in range(2)]
        ready = scores(units[0])
        done = {}
        for i, unit in enumerate(units):
            following = scores(units[i + 1]) if i + 1 < len(units) else None
            done[unit] = combine(unit, *ready)
            ready = following
        gathered = []
        for part in range(3):
            strips = []
            for r in range(rows // sub):
                strips.append(
                    jnp.concatenate(
                        [jnp.broadcast_to(done[(h, r)][part], (HEAD_DIM, sub)) for h in range(2)], 0
                    )
                )
            gathered.append(jnp.concatenate(strips, 1))
        return gathered

    def finish(o, l, m):
        context = (o / l).T.astype(BF16)
        c_ref[...] = context
        give_ref[...] = context[rows // 2 :]
        lse_ref[...] = pltpu.roll((m + jnp.log(l)).T, HEAD_DIM, 1)

    if own:
        o, l, m = work()
        o_ref[...] = o
        l_ref[...] = l
        m_ref[...] = m
    else:

        @pl.when(info[0] == 1)
        def _():
            o, l, m = work()
            m1 = m1_ref[...]
            top = jnp.maximum(m, m1)
            a1 = jnp.exp(m1 - top)
            a2 = jnp.exp(m - top)
            finish(o1_ref[...] * a1 + o * a2, l1_ref[...] * a1 + l * a2, top)

        @pl.when(info[0] != 1)
        def _():
            finish(o1_ref[...], l1_ref[...], m1_ref[...])


def attend(own, info, q, k, v, earlier=(), sub=256, kb=256):
    rows, cols = q.shape
    count = k.shape[0]
    wide = pl.BlockSpec((rows, 128), lambda p, s: (0, p))
    tall = pl.BlockSpec((128, rows), lambda p, s: (p, 0))
    upright = jax.ShapeDtypeStruct((cols, rows), F32)
    if own:
        outs = (upright,) * 3
    else:
        outs = (
            jax.ShapeDtypeStruct((rows, cols), BF16),
            jax.ShapeDtypeStruct((rows // 2, cols), BF16),
            jax.ShapeDtypeStruct((rows, cols), F32),
        )
    return pl.pallas_call(
        functools.partial(attend_kernel, own, sub, kb),
        out_shape=outs,
        grid_spec=pltpu.PrefetchScalarGridSpec(
            num_scalar_prefetch=1,
            grid=(cols // 128,),
            in_specs=[wide, pl.BlockSpec((count, 128), lambda p, s: (0, p)), pl.BlockSpec((count, 128), lambda p, s: (0, p))]
            + [tall] * len(earlier),
            out_specs=[tall] * 3 if own else [wide, pl.BlockSpec((rows // 2, 128), lambda p, s: (0, p)), wide],
            scratch_shapes=[
                pltpu.VMEM((2, count, 128), BF16),
                pltpu.VMEM((2, HEAD_DIM + ONES, count), BF16),
            ],
        ),
        compiler_params=limits(60),
        cost_estimate=cost(0),
        name="attend_own" if own else "attend_far",
    )(info, q, k, v, *earlier)


def turn(out, parts):
    each = out.shape[1]
    size = 256
    unit = (lax.broadcasted_iota(jnp.int32, (size, size), 0) == lax.broadcasted_iota(jnp.int32, (size, size), 1)).astype(
        F32
    ).astype(BF16)
    at = 0
    for n_ref in parts:
        rows, dim = n_ref.shape
        for j in range(dim // size):
            flipped = product(unit, n_ref[:, j * size : (j + 1) * size], NT).astype(BF16)
            out[j * size // each : (j + 1) * size // each, :, at : at + rows] = flipped.reshape(
                size // each, each, rows
            )
        at += rows


def place(grads, j, count, gb):
    j, out = j % (count // 2), grads[j // (count // 2)]
    return out, slice(j * gb, (j + 1) * gb)


def rows_in_order(turned, order, j, gb, first=0):
    per = gb // turned.shape[1]
    return jnp.concatenate([turned[order[first + j * per + i]] for i in range(per)], 0)


def heads_back(q, g, k_ref, v_ref, c, lse, bias, scratch, kb):
    keys, values, keys_t, dk_sum, dv_sum = scratch
    count = k_ref.shape[0]
    for h in range(2):
        keys[h] = key_side(k_ref[...], h, bias)
        values[h] = key_side(v_ref[...], h, 0.0)
        keys_t[h] = only_head(k_ref[...], h).T
    lane = lanes_of(q.shape)
    overlap = g.astype(F32) * c.astype(F32)
    dq = None
    for h in range(2):
        qa = row_side(q, h, -lse)
        delta = jnp.sum(jnp.where(lane // HEAD_DIM == h, overlap, 0.0), -1, keepdims=True)
        ga = row_side(g, h, jnp.broadcast_to(-delta, q.shape))
        qm = only_head(q, h)
        gm = only_head(g, h)
        for b in range(count // kb):
            rows = slice(b * kb, (b + 1) * kb)
            p = jnp.exp(product(keys[h, rows], qa, NT))
            ds = (p * product(values[h, rows], ga, NT)).astype(BF16)
            dv = product(p.astype(BF16), gm)
            dk = product(ds, qm)
            if h == 0:
                dv_sum[rows] = dv
                dk_sum[rows] = dk
            else:
                dv_sum[rows] += dv
                dk_sum[rows] += dk
            part = product(keys_t[h, :, rows], ds)
            dq = part if dq is None else dq + part
    return dq.T * (HEAD_DIM**-0.5)


def heads_scratch(count):
    return [
        pltpu.VMEM((2, count, 128), BF16),
        pltpu.VMEM((2, count, 128), BF16),
        pltpu.VMEM((2, 128, count), BF16),
        pltpu.VMEM((count, 128), F32),
        pltpu.VMEM((count, 128), F32),
    ]


def pair_lanes(pair, first=0):
    return pl.ds(pl.multiple_of(first + pair * 128, 128), 128)


def copies(sources, targets, sems):
    return [pltpu.make_async_copy(a, b, sems.at[i]) for i, (a, b) in enumerate(zip(sources, targets))]


def far_kernel(kb, gb, info, order, q_ref, k_ref, v_ref, c_ref, lse_ref, cos_ref, sin_ref, d_ref, do_ref, *rest):
    wo_ref, wk_hbm, wv_hbm, g_ref, dq_ref, dk_ref, dv_ref, give_ref, own_ref, grad_ref, *rest = rest
    kv, context, wk, wv, dt, sems, *scratch = rest
    pair = pl.program_id(0)
    last = pl.num_programs(0) - 1
    half = d_ref.shape[0]
    cols = wk.shape[1]
    joined = info[0] == 1

    @pl.when(pair == 0)
    def _():
        for c in copies((wk_hbm, wv_hbm), (wk, wv), sems):
            c.start()
        g_ref[:half] = product(d_ref[...], wo_ref[...], NT).astype(BF16)
        g_ref[half:] = product(do_ref[...], wo_ref[...], NT).astype(BF16)

    context[:, pair_lanes(pair)] = c_ref[...]

    @pl.when(joined)
    def _():
        g = g_ref[:, pair_lanes(pair)]
        dq_ref[...] = heads_back(q_ref[...], g, k_ref, v_ref, c_ref[...], lse_ref[...], 0.0, scratch, kb)
        dk = rotate(scratch[3][...], cos_ref[...], sin_ref[...], -1.0).astype(BF16)
        dv = scratch[4][...].astype(BF16)
        dk_ref[...] = dk
        dv_ref[...] = dv
        kv[:, pair_lanes(pair)] = dk
        kv[:, pair_lanes(pair, cols)] = dv

    @pl.when(jnp.logical_not(joined))
    def _():
        dq_ref[...] = jnp.zeros_like(dq_ref)
        dk_ref[...] = jnp.zeros_like(dk_ref)
        dv_ref[...] = jnp.zeros_like(dv_ref)

    @pl.when(pair == last)
    def _():
        for c in copies((wk_hbm, wv_hbm), (wk, wv), sems):
            c.wait()
        turn(dt, (d_ref, do_ref))
        for j in range(grad_ref.shape[0] // gb):
            left = rows_in_order(dt, order, j, gb, dt.shape[0])
            grad_ref[j * gb : (j + 1) * gb] = product(left, context[...]).astype(BF16)

    @pl.when(jnp.logical_and(pair == last, joined))
    def _():
        w = jnp.concatenate([wk[...], wv[...]], 1)
        give_ref[...] = product(kv[half:], w, NT).astype(BF16)
        own_ref[...] = product(kv[:half], w, NT)

    @pl.when(jnp.logical_and(pair == last, jnp.logical_not(joined)))
    def _():
        give_ref[...] = jnp.zeros_like(give_ref)
        own_ref[...] = jnp.zeros_like(own_ref)


def attend_back_far(info, order, q, k, v, c, lse, tables, d, d_other, wo, wk, wv, blocks, kb=1024, gb=256):
    rows, cols = q.shape
    count = k.shape[0]
    dim = wk.shape[0]
    half = d.shape[0]
    wide = pl.BlockSpec((rows, 128), lambda p, s, o: (0, p))
    table = pl.BlockSpec((count, 128), lambda p, s, o: (s[4], 0), pipeline_mode=ONCE)
    anywhere = pl.BlockSpec(memory_space=pl.ANY)
    out = shape_of((rows, cols), BF16)
    return pl.pallas_call(
        functools.partial(far_kernel, kb, gb),
        out_shape=(
            out,
            shape_of((rows, cols), F32),
            out,
            out,
            shape_of((half, dim), BF16),
            shape_of((half, dim), F32),
            shape_of((dim, cols), BF16),
        ),
        grid_spec=pltpu.PrefetchScalarGridSpec(
            num_scalar_prefetch=2,
            grid=(cols // 128,),
            in_specs=[wide] * 5
            + [table, table, fixed(d.shape), fixed(d.shape), fixed(wo.shape), anywhere, anywhere],
            out_specs=[fixed((rows, cols)), wide, wide, wide, fixed((half, dim)), fixed((half, dim)), fixed((dim, cols))],
            scratch_shapes=[
                pltpu.VMEM((count, 2 * cols), BF16),
                pltpu.VMEM((rows, cols), BF16),
                pltpu.VMEM(wk.shape, BF16),
                pltpu.VMEM(wv.shape, BF16),
                pltpu.VMEM((blocks, dim // blocks, rows), BF16),
                pltpu.SemaphoreType.DMA((2,)),
            ]
            + heads_scratch(count),
        ),
        compiler_params=limits(60),
        cost_estimate=cost(0),
        name="attend_back_far",
    )(info, order, q, k, v, c, lse, *tables, d, d_other, wo, wk, wv)


def own_kernel(kb, gb, info, order, q_ref, k_ref, v_ref, c_ref, lse_ref, g_ref, before_ref, cos_ref, sin_ref, *rest):
    hbm, (give_ref, own_ref, *rest) = rest[:9], rest[9:]
    grads, rest = rest[:2], rest[2:]
    vmem, (qkv, sems, nt, ft, *scratch) = rest[:9], rest[9:]
    n_ref, no_ref, f_ref, fo_ref, kf_ref, vf_ref, wq, wk, wv = vmem
    pair = pl.program_id(0)
    half = n_ref.shape[0]
    cols = wq.shape[1]

    @pl.when(pair == 0)
    def _():
        for c in copies(hbm, vmem, sems):
            c.start()

    bias = key_bias(info, k_ref.shape[0])
    dq = heads_back(q_ref[...], g_ref[...], k_ref, v_ref, c_ref[...], lse_ref[...], bias, scratch, kb)
    cos, sin = cos_ref[...], sin_ref[...]
    qkv[:, pair_lanes(pair)] = rotate(dq + before_ref[...], cos, sin, -1.0).astype(BF16)
    qkv[:, pair_lanes(pair, cols)] = rotate(scratch[3][...], cos, sin, -1.0).astype(BF16)
    qkv[:, pair_lanes(pair, 2 * cols)] = scratch[4][...].astype(BF16)

    @pl.when(pair == pl.num_programs(0) - 1)
    def _():
        for c in copies(hbm, vmem, sems):
            c.wait()
        w = jnp.concatenate([wq[...], wk[...], wv[...]], 1)
        give_ref[...] = product(qkv[half:], w, NT).astype(BF16)
        own_ref[...] = product(qkv[:half], w, NT)
        turn(nt, (n_ref, no_ref))
        turn(ft, (f_ref, fo_ref))
        blocks, each, _ = nt.shape
        dim = blocks * each
        for j in range(dim // gb):
            out, rows = place(grads, j, dim // gb, gb)
            both = product(rows_in_order(nt, order, j, gb), qkv[...])
            far = rows_in_order(ft, order, j, gb)
            out[rows, :cols] = both[:, :cols].astype(BF16)
            for i, other in ((1, kf_ref), (2, vf_ref)):
                columns = slice(i * cols, (i + 1) * cols)
                out[rows, columns] = (both[:, columns] + product(far, other[...])).astype(BF16)


def attend_back_own(info, order, q, k, v, c, lse, tables, g, before, lefts, far, weights, blocks, gb=256, kb=1024):
    rows, cols = q.shape
    count = k.shape[0]
    half, dim = lefts[0].shape
    wide = pl.BlockSpec((rows, 128), lambda p, s, o: (0, p))
    table = pl.BlockSpec((rows, 128), lambda p, s, o: (s[3], 0), pipeline_mode=ONCE)
    grads = shape_of((dim // 2, 3 * cols), BF16)
    turned = pltpu.VMEM((blocks, dim // blocks, rows), BF16)
    late = [*lefts, *far, *weights]
    return pl.pallas_call(
        functools.partial(own_kernel, kb, gb),
        out_shape=(shape_of((half, dim), BF16), shape_of((half, dim), F32), grads, grads),
        grid_spec=pltpu.PrefetchScalarGridSpec(
            num_scalar_prefetch=2,
            grid=(cols // 128,),
            in_specs=[wide] * 7 + [table, table] + [pl.BlockSpec(memory_space=pl.ANY)] * len(late),
            out_specs=[fixed((half, dim)), fixed((half, dim)), fixed(grads.shape), fixed(grads.shape)],
            scratch_shapes=[pltpu.VMEM(a.shape, BF16) for a in late]
            + [pltpu.VMEM((rows, 3 * cols), BF16), pltpu.SemaphoreType.DMA((len(late),)), turned, turned]
            + heads_scratch(count),
        ),
        compiler_params=limits(60),
        cost_estimate=cost(0),
        name="attend_back_own",
    )(info, order, q, k, v, c, lse, g, before, *tables, *late)


def gated_kernel(gb, rb, again, order, n_ref, no_ref, b_ref, bo_ref, wg_ref, wu_ref, wd_ref, *rest):
    if again:
        before_hbm, *rest, before, sem = rest
    hid_ref, own_ref, give_ref, *grads, down_ref, dg, du, acc, nt, bt = rest
    step = pl.program_id(0)
    half_rows, dim = n_ref.shape
    width = wg_ref.shape[1]

    @pl.when(step == 0)
    def _():
        if again:
            pltpu.make_async_copy(before_hbm, before, sem).start()
        turn(nt, (n_ref, no_ref))
        turn(bt, (b_ref, bo_ref))
        acc[...] = jnp.zeros_like(acc)

    for r in range(2 * half_rows // rb):
        rows_ref, d_ref = ((n_ref, b_ref), (no_ref, bo_ref))[r * rb // half_rows]
        inner = slice(r * rb % half_rows, r * rb % half_rows + rb)
        part = slice(r * rb, (r + 1) * rb)
        n = rows_ref[inner]
        gate = product(n, wg_ref[...])
        up = product(n, wu_ref[...])
        d_hidden = product(d_ref[inner], wd_ref[...], NT)
        s = 0.5 * jnp.tanh(0.5 * gate) + 0.5
        silu = gate * s
        hid_ref[part] = (silu * up).astype(BF16)
        d_gate = (d_hidden * up * (s * (1.0 + gate * (1.0 - s)))).astype(BF16)
        d_up = (d_hidden * silu).astype(BF16)
        dg[part] = d_gate
        du[part] = d_up
        acc[part] += product(
            jnp.concatenate([d_gate, d_up], 1), jnp.concatenate([wg_ref[...], wu_ref[...]], 1), NT
        )

    for j in range(dim // gb):
        left = rows_in_order(nt, order, j, gb)
        out, part = place(grads, j, dim // gb, gb)
        out[part, :width] = product(left, dg[...]).astype(BF16)
        out[part, width:] = product(left, du[...]).astype(BF16)
        left = rows_in_order(bt, order, j, gb, nt.shape[0])
        down_ref[j * gb : (j + 1) * gb] = product(left, hid_ref[...]).astype(BF16)

    @pl.when(step == pl.num_programs(0) - 1)
    def _():
        if again:
            pltpu.make_async_copy(before_hbm, before, sem).wait()
            own_ref[...] = acc[:half_rows] + before[...]
        else:
            own_ref[...] = acc[:half_rows]
        give_ref[...] = acc[half_rows:].astype(BF16)


def gated_units(order, rows_in, wg, wu, wd, blocks, first, last, before=(), width=WIDTH, gb=256, rb=512):
    half, dim = rows_in[0].shape
    rows = 2 * half
    steps = (last - first) // width
    at = first // width
    columns = pl.BlockSpec((dim, width), lambda s, o: (0, s + at))
    grads = shape_of((dim // 2, 2 * (last - first)), BF16)
    grad_spec = pl.BlockSpec((dim // 2, 2 * width), lambda s, o: (0, s))
    split = pl.BlockSpec((half, dim), lambda s, o: (0, 0))
    return pl.pallas_call(
        functools.partial(gated_kernel, gb, rb, bool(before)),
        out_shape=(shape_of((rows, last - first), BF16), shape_of((half, dim), F32), shape_of((half, dim), BF16))
        + (grads, grads, shape_of((dim, last - first), BF16)),
        grid_spec=pltpu.PrefetchScalarGridSpec(
            num_scalar_prefetch=1,
            grid=(steps,),
            in_specs=[fixed((half, dim))] * 4
            + [columns, columns, pl.BlockSpec((width, dim), lambda s, o: (s + at, 0))]
            + [pl.BlockSpec(memory_space=pl.ANY)] * len(before),
            out_specs=[pl.BlockSpec((rows, width), lambda s, o: (0, s)), split, split]
            + [grad_spec, grad_spec, pl.BlockSpec((dim, width), lambda s, o: (0, s))],
            scratch_shapes=[
                pltpu.VMEM((rows, width), BF16),
                pltpu.VMEM((rows, width), BF16),
                pltpu.VMEM((rows, dim), F32),
                pltpu.VMEM((blocks, dim // blocks, rows), BF16),
                pltpu.VMEM((blocks, dim // blocks, rows), BF16),
            ]
            + [pltpu.VMEM(a.shape, F32) for a in before]
            + [pltpu.SemaphoreType.DMA] * len(before),
        ),
        compiler_params=limits(60),
        cost_estimate=cost(0),
        name="gated_units",
    )(order, *rows_in, wg, wu, wd, *before)


def unpack_gated_kernel(first_ref, second_ref, turned_ref, gate_ref, up_ref, down_ref, project_ref):
    at = 0
    for ref in (first_ref, second_ref):
        for step in range(ref.shape[1] // (2 * WIDTH)):
            base = 2 * step * WIDTH
            cols = slice(at, at + WIDTH)
            gate_ref[:, cols] = ref[:, base : base + WIDTH].astype(F32)
            up_ref[:, cols] = ref[:, base + WIDTH : base + 2 * WIDTH].astype(F32)
            at += WIDTH
    down_ref[...] = turned_ref[:, :at].astype(F32)
    project_ref[...] = turned_ref[:, at:].astype(F32)


def unpack_gated(first, second, turned):
    rows, units = first.shape
    wide = shape_of((rows, units), F32)
    whole = pl.BlockSpec(memory_space=pltpu.VMEM)
    return pl.pallas_call(
        unpack_gated_kernel,
        out_shape=(wide, wide, wide, shape_of((rows, turned.shape[1] - units), F32)),
        in_specs=[whole] * 3,
        out_specs=[whole] * 4,
        compiler_params=limits(60),
        cost_estimate=cost(0),
        name="unpack_gated",
    )(first, second, turned)


def unpack_rest_kernel(ref, q_ref, k_ref, v_ref):
    cols = q_ref.shape[1]
    for i, out in enumerate((q_ref, k_ref, v_ref)):
        out[...] = ref[:, i * cols : (i + 1) * cols].astype(F32)


def unpack_rest(total):
    rows = total.shape[0]
    whole = pl.BlockSpec(memory_space=pltpu.VMEM)
    return pl.pallas_call(
        unpack_rest_kernel,
        out_shape=(shape_of((rows, total.shape[1] // 3), F32),) * 3,
        in_specs=[whole],
        out_specs=[whole] * 3,
        compiler_params=limits(60),
        cost_estimate=cost(0),
        name="unpack_rest",
    )(total)


def swap(value):
    return lax.ppermute(value, "mp", [(0, 1), (1, 0)])


def across(value, bit):
    return lax.ppermute(value, "dp", [(i, i ^ (1 << bit)) for i in range(lax.axis_size("dp"))])


def exchange(value, bits):
    size = lax.axis_size("dp")
    pairs = [(2 * i + c, 2 * (i ^ (1 << bit)) + c) for i in range(size) for c, bit in enumerate(bits)]
    return lax.ppermute(value, ("dp", "mp"), pairs)


def rounded_sum(parts):
    total = parts[0].astype(F32)
    for part in parts[1:]:
        total += part.astype(F32)
    return total.astype(BF16)


def first_half(parts):
    half = parts[0].shape[0] // 2
    return rounded_sum([p[:half] for p in parts])


def second_halves(parts):
    half = parts[0].shape[0] // 2
    return [p[half:] for p in parts]


def scatter_rest(quarters):
    size = lax.axis_size("dp")
    groups = [[b + 4 * k for k in range(size // 4)] for b in range(4)]
    return lax.psum_scatter(quarters, "dp", scatter_dimension=0, axis_index_groups=groups, tiled=True)


def later_bits():
    return range(2, lax.axis_size("dp").bit_length() - 1)


def after(value, done):
    return lax.optimization_barrier((value, done))[0]


def block_orders():
    size = lax.axis_size("dp")
    me = lax.axis_index("dp")
    first_core = lax.axis_index("mp") == 0
    count = size.bit_length() - 1
    places = np.arange(size)
    results = []
    for halved in (2, count):
        flows = []
        for outer, inner in ((0, 1), (1, 0)):
            flipped = np.zeros(size, np.int32)
            for position, bit in enumerate((outer, inner, *range(2, halved))):
                flipped |= (1 - ((places >> (count - 1 - position)) & 1)).astype(np.int32) << bit
            if halved == 2:
                plain = (places % (size // 4)).astype(np.int32) * 4
                flows.append((jnp.asarray(flipped) ^ (me & 3)) | jnp.asarray(plain))
            else:
                flows.append(jnp.asarray(flipped) ^ me)
        results.append(jnp.where(first_core, flows[0], flows[1]).astype(jnp.int32))
    within = places % 4
    swapped = (within % 2) * 2 + within // 2
    flipped = jnp.where(first_core, jnp.asarray(3 - swapped), jnp.asarray(3 - within)) ^ (me & 3)
    last = ((places // 4) * 4 + flipped).astype(jnp.int32)
    return jnp.concatenate([results[0], last]), results[1]


def rotary_tables(slot_rows):
    half_dim = HEAD_DIM // 2
    frequency = (10000.0 ** (-(np.arange(half_dim) * 2.0 / HEAD_DIM))).astype(np.float32)
    within = np.arange(slot_rows)
    tables = []
    for window_half in range(2):
        for shift in (0, slot_rows // 2):
            tables.append((within + shift) % slot_rows + window_half * slot_rows)
    angles = np.concatenate(tables).astype(np.float32)[:, None] * frequency[None, :]
    angles = np.tile(angles.astype(np.float64), (1, 4))
    return np.cos(angles).astype(np.float32), np.sin(angles).astype(np.float32)


def local(
    inputs,
    first_gain,
    first_shift,
    query_weight,
    key_weight,
    value_weight,
    output_weight,
    second_gain,
    second_shift,
    gate_weight,
    up_weight,
    down_weight,
    cotangent,
    species_weight,
    species_ids,
    slot_bucket,
    slot_length,
):
    half_rows = inputs.shape[0]
    slot_rows = 2 * half_rows
    blocks = lax.axis_size("dp")
    core = lax.axis_index("mp")
    parity = lax.axis_index("dp") % 2
    joined = slot_bucket[0]
    length = slot_length[0]
    start = core * half_rows
    own_table = 2 * parity * joined + core
    far_table = 2 * (1 - parity) * joined + core
    info = jnp.stack([joined, length, start, own_table, far_table]).astype(jnp.int32)
    order, order_all = block_orders()
    tables = rotary_tables(slot_rows)
    units = gate_weight.shape[1]

    cot_other = swap(cotangent)
    output_weight_other = swap(output_weight)
    n1_own = norm_rows(inputs, first_gain, first_shift)
    n1_far_own = across(n1_own, 0)
    n1_other = swap(n1_own)
    q, k, v = project(info[3:4], n1_own, n1_other, (query_weight, key_weight, value_weight), *tables)
    earlier = attend(True, info, q, k, v)

    n1_far_own = after(n1_far_own, earlier[2])
    n1_far_other = swap(n1_far_own)
    token_index = (jnp.arange(slot_rows, dtype=jnp.int32) + start) % slot_rows
    table_index = jnp.arange(species_weight.shape[0], dtype=jnp.int32)
    slot_weight = jnp.sum(jnp.where(table_index == species_ids[0], species_weight, 0.0))
    token_weight = jnp.where(token_index < length, slot_weight, 0.0)[:, None]
    late_cot, late_other = after((cotangent, cot_other), earlier[2])
    d_branch = [
        (c.astype(F32) * w).astype(BF16)
        for c, w in ((late_cot, token_weight[:half_rows]), (late_other, token_weight[half_rows:]))
    ]
    k_far, v_far = project(
        after(info[4:5], d_branch), n1_far_own, n1_far_other, (key_weight, value_weight), *tables
    )
    context, context_give, log_total = attend(False, info, q, k_far, v_far, tuple(earlier))
    middle, n2_own = middle_rows(
        context, swap(context_give), output_weight, output_weight_other, inputs, second_gain, second_shift
    )
    rows_in = (n2_own, swap(n2_own), *d_branch)

    gated = functools.partial(gated_units, order, rows_in, gate_weight, up_weight, down_weight, blocks)
    near, off = (0, 1), (1, 0)
    hidden_1, d_n2_1, give_1, sent, parts_1, down_1 = gated(0, units // 2)
    got_1 = exchange(sent, near)
    down_1 = scatter_rest(down_1)
    hidden_2, d_n2, give_2, sent, parts_2, down_2 = gated(units // 2, units, (d_n2_1,))
    got_2 = exchange(sent, near)
    down_2 = scatter_rest(down_2)
    d_middle, d_attended, second_sums = middle_back(
        info, slot_weight[None], (d_n2, swap(give_1), swap(give_2)), middle, cotangent, second_gain
    )
    d_attended_other = swap(d_attended)
    parts_1 = [parts_1, after(got_1, d_attended)]
    onward_1 = first_half(parts_1)
    again_1 = exchange(onward_1, off)

    d_context, dq_far, dk_far, dv_far, d_far_give, d_far, projected = attend_back_far(
        after(info, onward_1),
        order,
        q,
        k_far,
        v_far,
        context,
        log_total,
        tables,
        d_attended,
        d_attended_other,
        output_weight,
        key_weight,
        value_weight,
        blocks,
    )
    got_2, again_1 = after((got_2, again_1), dq_far)
    parts_2 = [parts_2, got_2]
    onward_2 = first_half(parts_2)
    again_2 = exchange(onward_2, off)
    kept_1 = rounded_sum([*second_halves(parts_1), again_1])
    gated_1 = scatter_rest(kept_1)
    d_far_got = after(swap(d_far_give), (kept_1, onward_2))
    d_far = rounded_sum([d_far, d_far_got])
    d_far_back = across(d_far, 0)
    projected = scatter_rest(after(projected, d_far))

    d_n1_give, d_n1, sent, parts_3 = attend_back_own(
        after(info, (kept_1, onward_2, d_far)),
        order_all,
        q,
        k,
        v,
        context,
        log_total,
        tables,
        d_context,
        dq_far,
        (n1_own, n1_other, n1_far_own, n1_far_other),
        (dk_far, dv_far),
        (query_weight, key_weight, value_weight),
        blocks,
    )
    got_3 = exchange(sent, near)
    again_2, d_far_back, gated_1, down_1, down_2 = after(
        (again_2, d_far_back, gated_1, down_1, down_2), parts_3
    )
    kept_2 = rounded_sum([*second_halves(parts_2), again_2])
    gated_2 = scatter_rest(kept_2)
    d_n1_got = after(swap(d_n1_give), kept_2)
    input_grad, first_sums = first_back(d_n1, d_n1_got, d_far_back, inputs, d_middle, first_gain)
    turned = [jnp.concatenate([down_1, down_2, after(projected, first_sums)], 1)]
    turned_send = first_half(turned)
    turned_got = exchange(turned_send, near)
    sums = jnp.concatenate([first_sums[:2], second_sums[:2]], 0)
    sums += after(swap(sums), turned_send)
    branch_give, branch = rows_times(
        after(order, (turned_send, sums)), ((hidden_1, down_weight, 0), (hidden_2, down_weight, 1)), NN
    )
    parts_3 = [parts_3, after(got_3, branch_give)]
    sent = first_half(parts_3)
    parts_3 = [*second_halves(parts_3), exchange(sent, off)]
    sums += after(across(sums, 0), sent)
    turned = [*second_halves(turned), after(turned_got, sent)]
    turned = [*second_halves(turned), exchange(first_half(turned), off)]
    parts_3 = after(parts_3, gated_2)
    *early, last_bit = later_bits()
    for bit in early:
        sent = first_half(parts_3)
        parts_3 = [*second_halves(parts_3), across(sent, bit)]
        sums += after(across(sums, bit - 1), sent)
    output = (middle + branch + swap(branch_give).astype(F32)).astype(BF16)
    gate_grad, up_grad, down_grad, project_grad = unpack_gated(gated_1, gated_2, rounded_sum(turned))
    parts_3 = after(parts_3, (output, gate_grad))
    sent = first_half(parts_3)
    parts_3 = [*second_halves(parts_3), across(sent, last_bit)]
    sums += after(across(sums, last_bit - 1), sent)
    norm_sums = sums + across(sums, last_bit)
    query_grad, key_grad, value_grad = unpack_rest(rounded_sum(parts_3))
    share = norm_sums.shape[1] // (2 * blocks)
    norm_sums = lax.dynamic_slice_in_dim(norm_sums, (2 * lax.axis_index("dp") + core) * share, share, 1)
    return (
        output,
        input_grad,
        norm_sums[0],
        norm_sums[1],
        query_grad,
        key_grad,
        value_grad,
        project_grad.T,
        norm_sums[2],
        norm_sums[3],
        gate_grad,
        up_grad,
        down_grad.T,
    )


def solution(mesh):
    rows = P(("dp", "mp"), None)
    in_specs = (
        rows,
        P(),
        P(),
        P(None, "mp"),
        P(None, "mp"),
        P(None, "mp"),
        P("mp", None),
        P(),
        P(),
        P(None, "mp"),
        P(None, "mp"),
        P("mp", None),
        rows,
        P(),
        P("dp"),
        P("dp"),
        P("dp"),
    )
    out_specs = (
        rows,
        rows,
        P(("dp", "mp")),
        P(("dp", "mp")),
        P("dp", "mp"),
        P("dp", "mp"),
        P("dp", "mp"),
        P("mp", "dp"),
        P(("dp", "mp")),
        P(("dp", "mp")),
        P("dp", "mp"),
        P("dp", "mp"),
        P("mp", "dp"),
    )
    return jax.shard_map(local, mesh=mesh, in_specs=in_specs, out_specs=out_specs, check_vma=False)
```

```python
import functools

import jax
import jax.numpy as jnp
import numpy as np
from jax import lax
from jax.experimental import pallas as pl
from jax.experimental.pallas import tpu as pltpu
from jax.sharding import PartitionSpec as P

HEAD_DIM = 64
EPS = 1e-05
NEG = -1e30
F32 = jnp.float32
BF16 = jnp.bfloat16
NT = (((1,), (1,)), ((), ()))
NN = (((1,), (0,)), ((), ()))
MIB = 1024 * 1024
ONES = 16
WIDTH = 512


def product(a, b, dims=NN):
    return lax.dot_general(a, b, dims, preferred_element_type=F32)


def lanes_of(shape):
    return lax.broadcasted_iota(jnp.int32, shape, 1)


def limits(mebibytes):
    return pltpu.CompilerParams(vmem_limit_bytes=mebibytes * MIB)


def cost(us):
    return pl.CostEstimate(flops=0, bytes_accessed=us * 3500000, transcendentals=0)


def shape_of(dims, kind):
    return jax.ShapeDtypeStruct(dims, kind)


ONCE = pl.Buffered(1)
SMALL = pl.BlockSpec(memory_space=pltpu.SMEM)


def fixed(dims, at=None):
    place = (0,) * len(dims) if at is None else at
    return pl.BlockSpec(dims, lambda *_: place, pipeline_mode=ONCE)


def normalize(v):
    centred = v - jnp.mean(v, -1, keepdims=True)
    inv_std = lax.rsqrt(jnp.mean(centred * centred, -1, keepdims=True) + EPS)
    return centred * inv_std, inv_std


def norm_back(upstream, x_hat, inv_std, gain):
    scaled = upstream * gain
    return inv_std * (
        scaled - jnp.mean(scaled, -1, keepdims=True) - x_hat * jnp.mean(scaled * x_hat, -1, keepdims=True)
    )


def norm_kernel(x_ref, gain_ref, shift_ref, n_ref):
    x_hat, _ = normalize(x_ref[...].astype(F32))
    n_ref[...] = (x_hat * gain_ref[...] + shift_ref[...]).astype(BF16)


def norm_rows(x, gain, shift, block=256):
    rows, dim = x.shape
    spec = pl.BlockSpec((block, dim), lambda i: (i, 0))
    return pl.pallas_call(
        norm_kernel,
        out_shape=shape_of((rows, dim), BF16),
        grid=(rows // block,),
        in_specs=[spec, fixed((1, dim)), fixed((1, dim))],
        out_specs=spec,
        compiler_params=limits(60),
        cost_estimate=cost(2),
        name="norm_rows",
    )(x, gain[None], shift[None])


def rotate(u, cos, sin, sign):
    lane = lanes_of(u.shape)
    half = HEAD_DIM // 2
    turned = jnp.where(lane % HEAD_DIM < half, -pltpu.roll(u, 128 - half, 1), pltpu.roll(u, half, 1))
    return u * cos + sign * turned * sin


def project_kernel(with_query, sel, own_ref, other_ref, *rest):
    if with_query:
        wq_ref, wk_ref, wv_ref, cos_ref, sin_ref, q_ref, k_ref, v_ref = rest
        todo = ((wq_ref, q_ref, HEAD_DIM**-0.5), (wk_ref, k_ref, 1.0))
    else:
        wk_ref, wv_ref, cos_ref, sin_ref, k_ref, v_ref = rest
        todo = ((wk_ref, k_ref, 1.0),)

    def work(n):
        cos, sin = cos_ref[...], sin_ref[...]
        for w_ref, out_ref, scale in todo:
            u = product(n, w_ref[...])
            for g in range(u.shape[1] // 128):
                cols = slice(g * 128, (g + 1) * 128)
                turned = rotate(u[:, cols], cos, sin, 1.0).astype(BF16)
                out_ref[:, cols] = (turned.astype(F32) * scale).astype(BF16)
        v_ref[...] = product(n, wv_ref[...]).astype(BF16)

    first = pl.program_id(0) < pl.num_programs(0) // 2
    work(jnp.where(first, own_ref[...], other_ref[...]))


def project(sel, own, other, weights, cos, sin, block=256):
    half, dim = own.shape
    cols = weights[0].shape[1]
    steps = 2 * half // block
    middle = steps // 2
    table = pl.BlockSpec((block, 128), lambda i, s: (s[0] * steps + i, 0))
    count = len(weights)
    return pl.pallas_call(
        functools.partial(project_kernel, count == 3),
        out_shape=(shape_of((2 * half, cols), BF16),) * count,
        grid_spec=pltpu.PrefetchScalarGridSpec(
            num_scalar_prefetch=1,
            grid=(steps,),
            in_specs=[
                pl.BlockSpec((block, dim), lambda i, s: (jnp.minimum(i, middle - 1), 0)),
                pl.BlockSpec((block, dim), lambda i, s: (jnp.maximum(i - middle, 0), 0)),
            ]
            + [fixed((dim, cols))] * count
            + [table, table],
            out_specs=[pl.BlockSpec((block, cols), lambda i, s: (i, 0))] * count,
        ),
        compiler_params=limits(60),
        cost_estimate=cost(0),
        name="project_rows",
    )(sel, own, other, *weights, cos, sin)


def middle_kernel(c_ref, co_ref, w_ref, wo_ref, x_ref, gain_ref, shift_ref, middle_ref, n_ref):
    middle = x_ref[...].astype(F32) + (product(c_ref[...], w_ref[...]) + product(co_ref[...], wo_ref[...]))
    middle_ref[...] = middle
    x_hat, _ = normalize(middle)
    n_ref[...] = (x_hat * gain_ref[...] + shift_ref[...]).astype(BF16)


def middle_rows(context, other, weight, weight_other, x, gain, shift, block=256):
    rows, dim = x.shape
    cols = context.shape[1]
    narrow = pl.BlockSpec((block, cols), lambda i: (i, 0))
    wide = pl.BlockSpec((block, dim), lambda i: (i, 0))
    return pl.pallas_call(
        middle_kernel,
        out_shape=(shape_of((rows, dim), F32), shape_of((rows, dim), BF16)),
        grid=(rows // block,),
        in_specs=[narrow, narrow, fixed((cols, dim)), fixed((cols, dim)), wide, fixed((1, dim)), fixed((1, dim))],
        out_specs=[wide, wide],
        compiler_params=limits(60),
        cost_estimate=cost(5),
        name="middle_rows",
    )(context, other, weight, weight_other, x, gain[None], shift[None])


def add_sums(sums_ref, upstream, x_hat):
    row = lax.broadcasted_iota(jnp.int32, sums_ref.shape, 0)
    new = jnp.where(
        row == 0,
        jnp.sum(upstream * x_hat, 0, keepdims=True),
        jnp.where(row == 1, jnp.sum(upstream, 0, keepdims=True), 0.0),
    )
    first = pl.program_id(0) == 0

    @pl.when(first)
    def _():
        sums_ref[...] = new

    @pl.when(jnp.logical_not(first))
    def _():
        sums_ref[...] += new


def middle_back_kernel(info, weight, d_ref, got1_ref, got2_ref, middle_ref, cot_ref, gain_ref, dm_ref, da_ref, sums_ref):
    upstream = d_ref[...] + (got1_ref[...].astype(F32) + got2_ref[...].astype(F32))
    x_hat, inv_std = normalize(middle_ref[...])
    block, dim = cot_ref.shape
    row = lax.broadcasted_iota(jnp.int32, (block, dim), 0) + (info[2] + pl.program_id(0) * block)
    cot = cot_ref[...].astype(F32) * jnp.where(row < info[1], weight[0], 0.0)
    d_middle = cot + norm_back(upstream, x_hat, inv_std, gain_ref[...])
    dm_ref[...] = d_middle
    da_ref[...] = d_middle.astype(BF16)
    add_sums(sums_ref, upstream, x_hat)


def middle_back(info, weight, parts, middle, cotangent, gain, block=128):
    rows, dim = middle.shape
    wide = pl.BlockSpec((block, dim), lambda i: (i, 0))
    return pl.pallas_call(
        middle_back_kernel,
        out_shape=(shape_of((rows, dim), F32), shape_of((rows, dim), BF16), shape_of((8, dim), F32)),
        grid=(rows // block,),
        in_specs=[SMALL, SMALL] + [wide] * 5 + [fixed((1, dim))],
        out_specs=[wide, wide, pl.BlockSpec((8, dim), lambda i: (0, 0))],
        compiler_params=limits(60),
        cost_estimate=cost(0),
        name="middle_back",
    )(info, weight, *parts, middle, cotangent, gain[None])


def first_back_kernel(d_ref, got_ref, far_ref, x_ref, dm_ref, gain_ref, out_ref, sums_ref):
    upstream = d_ref[...] + got_ref[...].astype(F32) + far_ref[...].astype(F32)
    x_hat, inv_std = normalize(x_ref[...].astype(F32))
    out_ref[...] = dm_ref[...] + norm_back(upstream, x_hat, inv_std, gain_ref[...])
    add_sums(sums_ref, upstream, x_hat)


def first_back(d_n1, got, far, x, d_middle, gain, block=128):
    rows, dim = x.shape
    wide = pl.BlockSpec((block, dim), lambda i: (i, 0))
    return pl.pallas_call(
        first_back_kernel,
        out_shape=(shape_of((rows, dim), F32), shape_of((8, dim), F32)),
        grid=(rows // block,),
        in_specs=[wide] * 5 + [fixed((1, dim))],
        out_specs=[wide, pl.BlockSpec((8, dim), lambda i: (0, 0))],
        compiler_params=limits(60),
        cost_estimate=cost(6),
        name="first_back",
    )(d_n1, got, far, x, d_middle, gain[None])


def rows_times_kernel(count, dims, mark, *refs):
    lefts, rights = refs[:count], refs[count : 2 * count]
    give_ref, own_ref = refs[2 * count :]
    total = product(
        jnp.concatenate([a[...] for a in lefts], 1),
        jnp.concatenate([a[...] for a in rights], 1 if dims is NT else 0),
        dims,
    )
    giving = pl.program_id(0) < pl.num_programs(0) // 2

    @pl.when(giving)
    def _():
        give_ref[...] = total.astype(BF16)

    @pl.when(jnp.logical_not(giving))
    def _():
        own_ref[...] = total


def rows_times(mark, terms, dims, block=256):
    rows = terms[0][0].shape[0]
    dim = terms[0][1].shape[0 if dims is NT else 1]
    steps = rows // block
    middle = steps // 2
    specs, rights = [], []
    for left, right, which in terms:
        depth = left.shape[1]
        specs.append(fixed((dim, depth), (0, which)) if dims is NT else fixed((depth, dim), (which, 0)))
    return pl.pallas_call(
        functools.partial(rows_times_kernel, len(terms), dims),
        out_shape=(shape_of((rows // 2, dim), BF16), shape_of((rows // 2, dim), F32)),
        grid=(steps,),
        in_specs=[SMALL]
        + [
            pl.BlockSpec((block, left.shape[1]), lambda i: ((i + middle) % steps, 0))
            for left, _, _ in terms
        ]
        + specs,
        out_specs=[
            pl.BlockSpec((block, dim), lambda i: (jnp.minimum(i, middle - 1), 0)),
            pl.BlockSpec((block, dim), lambda i: (jnp.maximum(i - middle, 0), 0)),
        ],
        compiler_params=limits(60),
        cost_estimate=cost(9),
        name="rows_times",
    )(mark, *[t[0] for t in terms], *[t[1] for t in terms])


def key_side(k, h, bias):
    lane = lanes_of(k.shape)
    pos = lane % HEAD_DIM
    extra = jnp.where(pos < 3, 1.0, jnp.where(pos == 3, bias, 0.0))
    return jnp.where(lane // HEAD_DIM == h, k.astype(F32), extra).astype(BF16)


def row_side(q, h, stat):
    lane = lanes_of(q.shape)
    pos = lane % HEAD_DIM
    high = stat.astype(BF16).astype(F32)
    left = stat - high
    mid = left.astype(BF16).astype(F32)
    low = left - mid
    extra = jnp.where(
        pos == 0, high, jnp.where(pos == 1, mid, jnp.where(pos == 2, low, jnp.where(pos == 3, 1.0, 0.0)))
    )
    return jnp.where(lane // HEAD_DIM == h, q.astype(F32), extra).astype(BF16)


def only_head(q, h):
    return jnp.where(lanes_of(q.shape) // HEAD_DIM == h, q, jnp.zeros_like(q))


def key_bias(info, rows):
    row = lax.broadcasted_iota(jnp.int32, (rows, 128), 0)
    return jnp.where(lax.rem(row + info[2], rows) < info[1], 0.0, NEG)


def attend_kernel(own, sub, kb, info, q_ref, k_ref, v_ref, *rest):
    if own:
        o_ref, l_ref, m_ref, keys, values_t = rest
    else:
        o1_ref, l1_ref, m1_ref, c_ref, give_ref, lse_ref, keys, values_t = rest
    count = k_ref.shape[0]
    rows = q_ref.shape[0]

    def scores(unit):
        h, r = unit
        q = q_ref[r * sub : (r + 1) * sub, :]
        qa = row_side(q, h, jnp.zeros(q.shape, F32))
        parts = [product(keys[h, b * kb : (b + 1) * kb], qa, NT) for b in range(count // kb)]
        top = jnp.max(parts[0], 0, keepdims=True)
        for s in parts[1:]:
            top = jnp.maximum(top, jnp.max(s, 0, keepdims=True))
        return parts, top

    def combine(unit, parts, top):
        h, _ = unit
        total = None
        for b, s in enumerate(parts):
            p = jnp.exp(s - top).astype(BF16)
            x = product(values_t[h, :, b * kb : (b + 1) * kb], p)
            total = x if total is None else total + x
        return total[:HEAD_DIM], total[HEAD_DIM : HEAD_DIM + 1], top

    def work():
        bias = key_bias(info, count) if own else 0.0
        for h in range(2):
            keys[h] = key_side(k_ref[...], h, bias)
        flipped = v_ref[...].T
        for h in range(2):
            values_t[h, :HEAD_DIM] = flipped[h * HEAD_DIM : (h + 1) * HEAD_DIM]
            values_t[h, HEAD_DIM:] = jnp.ones((ONES, count), BF16)
        units = [(h, r) for r in range(rows // sub) for h in range(2)]
        ready = scores(units[0])
        done = {}
        for i, unit in enumerate(units):
            following = scores(units[i + 1]) if i + 1 < len(units) else None
            done[unit] = combine(unit, *ready)
            ready = following
        gathered = []
        for part in range(3):
            strips = []
            for r in range(rows // sub):
                strips.append(
                    jnp.concatenate(
                        [jnp.broadcast_to(done[(h, r)][part], (HEAD_DIM, sub)) for h in range(2)], 0
                    )
                )
            gathered.append(jnp.concatenate(strips, 1))
        return gathered

    def finish(o, l, m):
        context = (o / l).T.astype(BF16)
        c_ref[...] = context
        give_ref[...] = context[rows // 2 :]
        lse_ref[...] = pltpu.roll((m + jnp.log(l)).T, HEAD_DIM, 1)

    if own:
        o, l, m = work()
        o_ref[...] = o
        l_ref[...] = l
        m_ref[...] = m
    else:

        @pl.when(info[0] == 1)
        def _():
            o, l, m = work()
            m1 = m1_ref[...]
            top = jnp.maximum(m, m1)
            a1 = jnp.exp(m1 - top)
            a2 = jnp.exp(m - top)
            finish(o1_ref[...] * a1 + o * a2, l1_ref[...] * a1 + l * a2, top)

        @pl.when(info[0] != 1)
        def _():
            finish(o1_ref[...], l1_ref[...], m1_ref[...])


def attend(own, info, q, k, v, earlier=(), sub=256, kb=256):
    rows, cols = q.shape
    count = k.shape[0]
    wide = pl.BlockSpec((rows, 128), lambda p, s: (0, p))
    tall = pl.BlockSpec((128, rows), lambda p, s: (p, 0))
    upright = jax.ShapeDtypeStruct((cols, rows), F32)
    if own:
        outs = (upright,) * 3
    else:
        outs = (
            jax.ShapeDtypeStruct((rows, cols), BF16),
            jax.ShapeDtypeStruct((rows // 2, cols), BF16),
            jax.ShapeDtypeStruct((rows, cols), F32),
        )
    return pl.pallas_call(
        functools.partial(attend_kernel, own, sub, kb),
        out_shape=outs,
        grid_spec=pltpu.PrefetchScalarGridSpec(
            num_scalar_prefetch=1,
            grid=(cols // 128,),
            in_specs=[wide, pl.BlockSpec((count, 128), lambda p, s: (0, p)), pl.BlockSpec((count, 128), lambda p, s: (0, p))]
            + [tall] * len(earlier),
            out_specs=[tall] * 3 if own else [wide, pl.BlockSpec((rows // 2, 128), lambda p, s: (0, p)), wide],
            scratch_shapes=[
                pltpu.VMEM((2, count, 128), BF16),
                pltpu.VMEM((2, HEAD_DIM + ONES, count), BF16),
            ],
        ),
        compiler_params=limits(60),
        cost_estimate=cost(0),
        name="attend_own" if own else "attend_far",
    )(info, q, k, v, *earlier)


def turn(out, parts):
    each = out.shape[1]
    size = 256
    unit = (lax.broadcasted_iota(jnp.int32, (size, size), 0) == lax.broadcasted_iota(jnp.int32, (size, size), 1)).astype(
        F32
    ).astype(BF16)
    at = 0
    for n_ref in parts:
        rows, dim = n_ref.shape
        for j in range(dim // size):
            flipped = product(unit, n_ref[:, j * size : (j + 1) * size], NT).astype(BF16)
            out[j * size // each : (j + 1) * size // each, :, at : at + rows] = flipped.reshape(
                size // each, each, rows
            )
        at += rows


def place(grads, j, count, gb):
    j, out = j % (count // 2), grads[j // (count // 2)]
    return out, slice(j * gb, (j + 1) * gb)


def rows_in_order(turned, order, j, gb, first=0):
    per = gb // turned.shape[1]
    return jnp.concatenate([turned[order[first + j * per + i]] for i in range(per)], 0)


def heads_back(q, g, k_ref, v_ref, c, lse, bias, scratch, kb):
    keys, values, keys_t, dk_sum, dv_sum = scratch
    count = k_ref.shape[0]
    for h in range(2):
        keys[h] = key_side(k_ref[...], h, bias)
        values[h] = key_side(v_ref[...], h, 0.0)
        keys_t[h] = only_head(k_ref[...], h).T
    lane = lanes_of(q.shape)
    overlap = g.astype(F32) * c.astype(F32)
    dq = None
    for h in range(2):
        qa = row_side(q, h, -lse)
        delta = jnp.sum(jnp.where(lane // HEAD_DIM == h, overlap, 0.0), -1, keepdims=True)
        ga = row_side(g, h, jnp.broadcast_to(-delta, q.shape))
        qm = only_head(q, h)
        gm = only_head(g, h)
        for b in range(count // kb):
            rows = slice(b * kb, (b + 1) * kb)
            p = jnp.exp(product(keys[h, rows], qa, NT))
            ds = (p * product(values[h, rows], ga, NT)).astype(BF16)
            dv = product(p.astype(BF16), gm)
            dk = product(ds, qm)
            if h == 0:
                dv_sum[rows] = dv
                dk_sum[rows] = dk
            else:
                dv_sum[rows] += dv
                dk_sum[rows] += dk
            part = product(keys_t[h, :, rows], ds)
            dq = part if dq is None else dq + part
    return dq.T * (HEAD_DIM**-0.5)


def heads_scratch(count):
    return [
        pltpu.VMEM((2, count, 128), BF16),
        pltpu.VMEM((2, count, 128), BF16),
        pltpu.VMEM((2, 128, count), BF16),
        pltpu.VMEM((count, 128), F32),
        pltpu.VMEM((count, 128), F32),
    ]


def pair_lanes(pair, first=0):
    return pl.ds(pl.multiple_of(first + pair * 128, 128), 128)


def copies(sources, targets, sems):
    return [pltpu.make_async_copy(a, b, sems.at[i]) for i, (a, b) in enumerate(zip(sources, targets))]


def far_kernel(kb, gb, info, order, q_ref, k_ref, v_ref, c_ref, lse_ref, cos_ref, sin_ref, d_ref, do_ref, *rest):
    wo_ref, wk_hbm, wv_hbm, g_hbm, dq_ref, dk_ref, dv_ref, give_ref, own_ref, grad_hbm, *rest = rest
    g_ref, grad_ref, kv, context, wk, wv, dt, sems, out_sems, *scratch = rest
    pair = pl.program_id(0)
    last = pl.num_programs(0) - 1
    half = d_ref.shape[0]
    cols = wk.shape[1]
    joined = info[0] == 1

    @pl.when(pair == 0)
    def _():
        for c in copies((wk_hbm, wv_hbm), (wk, wv), sems):
            c.start()
        g_ref[:half] = product(d_ref[...], wo_ref[...], NT).astype(BF16)
        g_ref[half:] = product(do_ref[...], wo_ref[...], NT).astype(BF16)
        pltpu.make_async_copy(g_ref, g_hbm, out_sems.at[0]).start()

    context[:, pair_lanes(pair)] = c_ref[...]

    @pl.when(joined)
    def _():
        g = g_ref[:, pair_lanes(pair)]
        dq_ref[...] = heads_back(q_ref[...], g, k_ref, v_ref, c_ref[...], lse_ref[...], 0.0, scratch, kb)
        dk = rotate(scratch[3][...], cos_ref[...], sin_ref[...], -1.0).astype(BF16)
        dv = scratch[4][...].astype(BF16)
        dk_ref[...] = dk
        dv_ref[...] = dv
        kv[:, pair_lanes(pair)] = dk
        kv[:, pair_lanes(pair, cols)] = dv

    @pl.when(jnp.logical_not(joined))
    def _():
        dq_ref[...] = jnp.zeros_like(dq_ref)
        dk_ref[...] = jnp.zeros_like(dk_ref)
        dv_ref[...] = jnp.zeros_like(dv_ref)

    @pl.when(pair == last)
    def _():
        for c in copies((wk_hbm, wv_hbm), (wk, wv), sems):
            c.wait()
        turn(dt, (d_ref, do_ref))
        for j in range(grad_ref.shape[0] // gb):
            left = rows_in_order(dt, order, j, gb)
            grad_ref[j * gb : (j + 1) * gb] = product(left, context[...]).astype(BF16)
        pltpu.make_async_copy(grad_ref, grad_hbm, out_sems.at[1]).start()

    @pl.when(jnp.logical_and(pair == last, joined))
    def _():
        w = jnp.concatenate([wk[...], wv[...]], 1)
        give_ref[...] = product(kv[half:], w, NT).astype(BF16)
        own_ref[...] = product(kv[:half], w, NT)

    @pl.when(jnp.logical_and(pair == last, jnp.logical_not(joined)))
    def _():
        give_ref[...] = jnp.zeros_like(give_ref)
        own_ref[...] = jnp.zeros_like(own_ref)

    @pl.when(pair == last)
    def _():
        pltpu.make_async_copy(g_ref, g_hbm, out_sems.at[0]).wait()
        pltpu.make_async_copy(grad_ref, grad_hbm, out_sems.at[1]).wait()


def attend_back_far(info, order, q, k, v, c, lse, tables, d, d_other, wo, wk, wv, blocks, kb=1024, gb=256):
    rows, cols = q.shape
    count = k.shape[0]
    dim = wk.shape[0]
    half = d.shape[0]
    wide = pl.BlockSpec((rows, 128), lambda p, s, o: (0, p))
    table = pl.BlockSpec((count, 128), lambda p, s, o: (s[4], 0), pipeline_mode=ONCE)
    anywhere = pl.BlockSpec(memory_space=pl.ANY)
    out = shape_of((rows, cols), BF16)
    return pl.pallas_call(
        functools.partial(far_kernel, kb, gb),
        out_shape=(
            out,
            shape_of((rows, cols), F32),
            out,
            out,
            shape_of((half, dim), BF16),
            shape_of((half, dim), F32),
            shape_of((dim, cols), BF16),
        ),
        grid_spec=pltpu.PrefetchScalarGridSpec(
            num_scalar_prefetch=2,
            grid=(cols // 128,),
            in_specs=[wide] * 5
            + [table, table, fixed(d.shape), fixed(d.shape), fixed(wo.shape), anywhere, anywhere],
            out_specs=[anywhere, wide, wide, wide, fixed((half, dim)), fixed((half, dim)), anywhere],
            scratch_shapes=[
                pltpu.VMEM((rows, cols), BF16),
                pltpu.VMEM((dim, cols), BF16),
                pltpu.VMEM((count, 2 * cols), BF16),
                pltpu.VMEM((rows, cols), BF16),
                pltpu.VMEM(wk.shape, BF16),
                pltpu.VMEM(wv.shape, BF16),
                pltpu.VMEM((blocks, dim // blocks, rows), BF16),
                pltpu.SemaphoreType.DMA((2,)),
                pltpu.SemaphoreType.DMA((2,)),
            ]
            + heads_scratch(count),
        ),
        compiler_params=limits(60),
        cost_estimate=cost(0),
        name="attend_back_far",
    )(info, order, q, k, v, c, lse, *tables, d, d_other, wo, wk, wv)


def own_kernel(kb, gb, info, order, q_ref, k_ref, v_ref, c_ref, lse_ref, g_ref, before_ref, cos_ref, sin_ref, *rest):
    hbm, results, rest = rest[:9], rest[9:13], rest[13:]
    vmem, (give_ref, own_ref, *rest) = rest[:9], rest[9:]
    grads, (qkv, sems, out_sems, nt, ft, *scratch) = rest[:2], rest[2:]
    n_ref, no_ref, f_ref, fo_ref, kf_ref, vf_ref, wq, wk, wv = vmem
    pair = pl.program_id(0)
    half = n_ref.shape[0]
    cols = wq.shape[1]

    @pl.when(pair == 0)
    def _():
        for c in copies(hbm, vmem, sems):
            c.start()

    bias = key_bias(info, k_ref.shape[0])
    dq = heads_back(q_ref[...], g_ref[...], k_ref, v_ref, c_ref[...], lse_ref[...], bias, scratch, kb)
    cos, sin = cos_ref[...], sin_ref[...]
    qkv[:, pair_lanes(pair)] = rotate(dq + before_ref[...], cos, sin, -1.0).astype(BF16)
    qkv[:, pair_lanes(pair, cols)] = rotate(scratch[3][...], cos, sin, -1.0).astype(BF16)
    qkv[:, pair_lanes(pair, 2 * cols)] = scratch[4][...].astype(BF16)

    @pl.when(pair == pl.num_programs(0) - 1)
    def _():
        for c in copies(hbm, vmem, sems):
            c.wait()
        w = jnp.concatenate([wq[...], wk[...], wv[...]], 1)
        leaving = copies((give_ref, own_ref, *grads), results, out_sems)
        give_ref[...] = product(qkv[half:], w, NT).astype(BF16)
        leaving[0].start()
        own_ref[...] = product(qkv[:half], w, NT)
        leaving[1].start()
        turn(nt, (n_ref, no_ref))
        turn(ft, (f_ref, fo_ref))
        blocks, each, _ = nt.shape
        dim = blocks * each
        for j in range(dim // gb):
            out, rows = place(grads, j, dim // gb, gb)
            both = product(rows_in_order(nt, order, j, gb), qkv[...])
            far = rows_in_order(ft, order, j, gb)
            out[rows, :cols] = both[:, :cols].astype(BF16)
            for i, other in ((1, kf_ref), (2, vf_ref)):
                columns = slice(i * cols, (i + 1) * cols)
                out[rows, columns] = (both[:, columns] + product(far, other[...])).astype(BF16)
            if j == dim // gb // 2 - 1:
                leaving[2].start()
        leaving[3].start()
        for c in leaving:
            c.wait()


def attend_back_own(info, order, q, k, v, c, lse, tables, g, before, lefts, far, weights, blocks, gb=256, kb=1024):
    rows, cols = q.shape
    count = k.shape[0]
    half, dim = lefts[0].shape
    wide = pl.BlockSpec((rows, 128), lambda p, s, o: (0, p))
    table = pl.BlockSpec((rows, 128), lambda p, s, o: (s[3], 0), pipeline_mode=ONCE)
    grads = shape_of((dim // 2, 3 * cols), BF16)
    turned = pltpu.VMEM((blocks, dim // blocks, rows), BF16)
    late = [*lefts, *far, *weights]
    return pl.pallas_call(
        functools.partial(own_kernel, kb, gb),
        out_shape=(shape_of((half, dim), BF16), shape_of((half, dim), F32), grads, grads),
        grid_spec=pltpu.PrefetchScalarGridSpec(
            num_scalar_prefetch=2,
            grid=(cols // 128,),
            in_specs=[wide] * 7 + [table, table] + [pl.BlockSpec(memory_space=pl.ANY)] * len(late),
            out_specs=[pl.BlockSpec(memory_space=pl.ANY)] * 4,
            scratch_shapes=[pltpu.VMEM(a.shape, BF16) for a in late]
            + [
                pltpu.VMEM((half, dim), BF16),
                pltpu.VMEM((half, dim), F32),
                pltpu.VMEM(grads.shape, BF16),
                pltpu.VMEM(grads.shape, BF16),
                pltpu.VMEM((rows, 3 * cols), BF16),
                pltpu.SemaphoreType.DMA((len(late),)),
                pltpu.SemaphoreType.DMA((4,)),
                turned,
                turned,
            ]
            + heads_scratch(count),
        ),
        compiler_params=limits(60),
        cost_estimate=cost(0),
        name="attend_back_own",
    )(info, order, q, k, v, c, lse, g, before, *tables, *late)


def gated_first_kernel(gb, rb, again, order, n_ref, no_ref, b_ref, bo_ref, wg_ref, wu_ref, wd_ref, *rest):
    if again:
        before_hbm, *rest, before, sem = rest
    hid_ref, own_ref, give_ref, *grads, down_ref, dg, du, acc, nt, bt = rest
    step = pl.program_id(0)
    half_rows, dim = n_ref.shape
    width = wg_ref.shape[1]

    @pl.when(step == 0)
    def _():
        if again:
            pltpu.make_async_copy(before_hbm, before, sem).start()
        turn(nt, (n_ref, no_ref))
        turn(bt, (b_ref, bo_ref))
        acc[...] = jnp.zeros_like(acc)

    for r in range(2 * half_rows // rb):
        rows_ref, d_ref = ((n_ref, b_ref), (no_ref, bo_ref))[r * rb // half_rows]
        inner = slice(r * rb % half_rows, r * rb % half_rows + rb)
        part = slice(r * rb, (r + 1) * rb)
        n = rows_ref[inner]
        gate = product(n, wg_ref[...])
        up = product(n, wu_ref[...])
        d_hidden = product(d_ref[inner], wd_ref[...], NT)
        s = 0.5 * jnp.tanh(0.5 * gate) + 0.5
        silu = gate * s
        hid_ref[part] = (silu * up).astype(BF16)
        d_gate = (d_hidden * up * (s * (1.0 + gate * (1.0 - s)))).astype(BF16)
        d_up = (d_hidden * silu).astype(BF16)
        dg[part] = d_gate
        du[part] = d_up
        acc[part] += product(
            jnp.concatenate([d_gate, d_up], 1), jnp.concatenate([wg_ref[...], wu_ref[...]], 1), NT
        )

    for j in range(dim // gb):
        left = rows_in_order(nt, order, j, gb)
        out, part = place(grads, j, dim // gb, gb)
        out[part, :width] = product(left, dg[...]).astype(BF16)
        out[part, width:] = product(left, du[...]).astype(BF16)
        left = rows_in_order(bt, order, j, gb, nt.shape[0])
        down_ref[j * gb : (j + 1) * gb] = product(left, hid_ref[...]).astype(BF16)

    @pl.when(step == pl.num_programs(0) - 1)
    def _():
        if again:
            pltpu.make_async_copy(before_hbm, before, sem).wait()
            own_ref[...] = acc[:half_rows] + before[...]
        else:
            own_ref[...] = acc[:half_rows]
        give_ref[...] = acc[half_rows:].astype(BF16)


def gated_first(order, rows_in, wg, wu, wd, blocks, first, last, before=(), width=WIDTH, gb=256, rb=512):
    half, dim = rows_in[0].shape
    rows = 2 * half
    steps = (last - first) // width
    at = first // width
    columns = pl.BlockSpec((dim, width), lambda s, o: (0, s + at))
    grads = shape_of((dim // 2, 2 * (last - first)), BF16)
    grad_spec = pl.BlockSpec((dim // 2, 2 * width), lambda s, o: (0, s))
    split = pl.BlockSpec((half, dim), lambda s, o: (0, 0))
    return pl.pallas_call(
        functools.partial(gated_first_kernel, gb, rb, bool(before)),
        out_shape=(shape_of((rows, last - first), BF16), shape_of((half, dim), F32), shape_of((half, dim), BF16))
        + (grads, grads, shape_of((dim, last - first), BF16)),
        grid_spec=pltpu.PrefetchScalarGridSpec(
            num_scalar_prefetch=1,
            grid=(steps,),
            in_specs=[fixed((half, dim))] * 4
            + [columns, columns, pl.BlockSpec((width, dim), lambda s, o: (s + at, 0))]
            + [pl.BlockSpec(memory_space=pl.ANY)] * len(before),
            out_specs=[pl.BlockSpec((rows, width), lambda s, o: (0, s)), split, split]
            + [grad_spec, grad_spec, pl.BlockSpec((dim, width), lambda s, o: (0, s))],
            scratch_shapes=[
                pltpu.VMEM((rows, width), BF16),
                pltpu.VMEM((rows, width), BF16),
                pltpu.VMEM((rows, dim), F32),
                pltpu.VMEM((blocks, dim // blocks, rows), BF16),
                pltpu.VMEM((blocks, dim // blocks, rows), BF16),
            ]
            + [pltpu.VMEM(a.shape, F32) for a in before]
            + [pltpu.SemaphoreType.DMA] * len(before),
        ),
        compiler_params=limits(60),
        cost_estimate=cost(0),
        name="gated_units",
    )(order, *rows_in, wg, wu, wd, *before)


def gated_kernel(width, gb, first, steps, again, order, *refs):
    ins, refs = refs[:7], refs[7:]
    if again:
        before_hbm, *refs = refs
    hid_hbm, own_hbm, give_hbm, sent_hbm, kept_hbm, down_hbm, *refs = refs
    nv, nov, bv, bov, wgv, wuv, wdv, *refs = refs
    if again:
        before, *refs = refs
    hid, give, acc, sent, kept, down, dg, du, nt, bt, sem_in, sem_out = refs
    n_hbm, no_hbm, b_hbm, bo_hbm, wg_hbm, wu_hbm, wd_hbm = ins
    half_rows, dim = nv.shape
    pending = []

    def fetch(source, target):
        copy = pltpu.make_async_copy(source, target, sem_in.at[len(pending)])
        pending.append(copy)
        copy.start()
        return copy

    def fetch_weights(s, between=()):
        units = pl.ds(first + s * width, width)
        pair = [fetch(wg_hbm.at[:, units], wgv.at[s]), fetch(wu_hbm.at[:, units], wuv.at[s])]
        return pair, [fetch(*b) for b in between] + [fetch(wd_hbm.at[units], wdv.at[s])]

    rows_in = [fetch(n_hbm, nv), fetch(no_hbm, nov)]
    weights = [fetch_weights(0, ((b_hbm, bv), (bo_hbm, bov)))]
    leaving = []

    def leave(source, target):
        copy = pltpu.make_async_copy(source, target, sem_out.at[len(leaving)])
        leaving.append(copy)
        copy.start()

    for copy in rows_in:
        copy.wait()
    turn(nt, (nv, nov))
    for s in range(steps):
        units = pl.ds(s * width, width)
        for copy in weights[s][0]:
            copy.wait()
        for r, (n_ref, b_ref) in enumerate(((nv, bv), (nov, bov))):
            part = slice(r * half_rows, (r + 1) * half_rows)
            n = n_ref[...]
            gate = product(n, wgv[s])
            up = product(n, wuv[s])
            if r == 0:
                for copy in weights[s][1]:
                    copy.wait()
                if s < steps - 1:
                    weights.append(fetch_weights(s + 1))
                elif again:
                    late = fetch(before_hbm, before)
            d_hidden = product(b_ref[...], wdv[s], NT)
            sig = 0.5 * jnp.tanh(0.5 * gate) + 0.5
            silu = gate * sig
            hid[s, part] = (silu * up).astype(BF16)
            d_gate = (d_hidden * up * (sig * (1.0 + gate * (1.0 - sig)))).astype(BF16)
            d_up = (d_hidden * silu).astype(BF16)
            dg[part] = d_gate
            du[part] = d_up
            back = product(jnp.concatenate([d_gate, d_up], 1), jnp.concatenate([wgv[s], wuv[s]], 1), NT)
            if s == 0:
                acc[part] = back
            else:
                acc[part] += back
        leave(hid.at[s], hid_hbm.at[:, units])
        if s == steps - 1:
            if again:
                late.wait()
                acc[:half_rows] += before[...]
            give[...] = acc[half_rows:].astype(BF16)
            leave(acc.at[pl.ds(0, half_rows)], own_hbm)
            leave(give, give_hbm)
        if s == 0:
            turn(bt, (bv, bov))
        for j in range(dim // gb):
            left = rows_in_order(bt, order, j, gb, nt.shape[0])
            down[s, j * gb : (j + 1) * gb] = product(left, hid[s]).astype(BF16)
        leave(down.at[s], down_hbm.at[:, units])
        both = pl.ds(s * 2 * width, 2 * width)
        for j in range(dim // gb):
            left = rows_in_order(nt, order, j, gb)
            out, part = place((sent, kept), j, dim // gb, gb)
            out[s, part, :width] = product(left, dg[...]).astype(BF16)
            out[s, part, width:] = product(left, du[...]).astype(BF16)
            if j == dim // gb // 2 - 1:
                leave(sent.at[s], sent_hbm.at[:, both])
        leave(kept.at[s], kept_hbm.at[:, both])
    for copy in leaving:
        copy.wait()


def gated_units(order, rows_in, wg, wu, wd, blocks, first, last, before=(), width=WIDTH, gb=256):
    half, dim = rows_in[0].shape
    rows = 2 * half
    count = last - first
    steps = count // width
    grads = shape_of((dim // 2, 2 * count), BF16)
    anywhere = pl.BlockSpec(memory_space=pl.ANY)
    vmem = pltpu.VMEM
    turned = vmem((blocks, dim // blocks, rows), BF16)
    return pl.pallas_call(
        functools.partial(gated_kernel, width, gb, first, steps, bool(before)),
        out_shape=(
            shape_of((rows, count), BF16),
            shape_of((half, dim), F32),
            shape_of((half, dim), BF16),
            grads,
            grads,
            shape_of((dim, count), BF16),
        ),
        in_specs=[SMALL] + [anywhere] * (7 + len(before)),
        out_specs=[anywhere] * 6,
        scratch_shapes=[vmem((half, dim), BF16)] * 4
        + [vmem((steps, dim, width), BF16)] * 2
        + [vmem((steps, width, dim), BF16)]
        + [vmem(a.shape, F32) for a in before]
        + [
            vmem((steps, rows, width), BF16),
            vmem((half, dim), BF16),
            vmem((rows, dim), F32),
            vmem((steps, dim // 2, 2 * width), BF16),
            vmem((steps, dim // 2, 2 * width), BF16),
            vmem((steps, dim, width), BF16),
            vmem((rows, width), BF16),
            vmem((rows, width), BF16),
            turned,
            turned,
            pltpu.SemaphoreType.DMA((4 + 3 * steps + len(before),)),
            pltpu.SemaphoreType.DMA((4 * steps + 2,)),
        ],
        compiler_params=limits(60),
        cost_estimate=cost(0),
        name="gated_units",
    )(order, *rows_in, wg, wu, wd, *before)


def unpack_gated_kernel(first_ref, second_ref, turned_ref, gate_ref, up_ref, down_ref, project_ref):
    at = 0
    for ref in (first_ref, second_ref):
        for step in range(first_ref.shape[1] // (2 * WIDTH)):
            base = 2 * step * WIDTH
            cols = slice(at, at + WIDTH)
            gate_ref[:, cols] = ref[:, base : base + WIDTH].astype(F32)
            up_ref[:, cols] = ref[:, base + WIDTH : base + 2 * WIDTH].astype(F32)
            at += WIDTH
    down_ref[...] = turned_ref[...].astype(F32)
    project_ref[...] = second_ref[:, first_ref.shape[1] :].astype(F32)


def unpack_gated(first, second, turned):
    rows, units = first.shape
    wide = shape_of((rows, units), F32)
    whole = pl.BlockSpec(memory_space=pltpu.VMEM)
    return pl.pallas_call(
        unpack_gated_kernel,
        out_shape=(wide, wide, wide, shape_of((rows, second.shape[1] - units), F32)),
        in_specs=[whole] * 3,
        out_specs=[whole] * 4,
        compiler_params=limits(60),
        cost_estimate=cost(0),
        name="unpack_gated",
    )(first, second, turned)


def unpack_rest_kernel(ref, q_ref, k_ref, v_ref):
    cols = q_ref.shape[1]
    for i, out in enumerate((q_ref, k_ref, v_ref)):
        out[...] = ref[:, i * cols : (i + 1) * cols].astype(F32)


def unpack_rest(total):
    rows = total.shape[0]
    whole = pl.BlockSpec(memory_space=pltpu.VMEM)
    return pl.pallas_call(
        unpack_rest_kernel,
        out_shape=(shape_of((rows, total.shape[1] // 3), F32),) * 3,
        in_specs=[whole],
        out_specs=[whole] * 3,
        compiler_params=limits(60),
        cost_estimate=cost(0),
        name="unpack_rest",
    )(total)


def swap(value):
    return lax.ppermute(value, "mp", [(0, 1), (1, 0)])


def across(value, bit):
    return lax.ppermute(value, "dp", [(i, i ^ (1 << bit)) for i in range(lax.axis_size("dp"))])


def exchange(value, bits):
    size = lax.axis_size("dp")
    pairs = [(2 * i + c, 2 * (i ^ (1 << bit)) + c) for i in range(size) for c, bit in enumerate(bits)]
    return lax.ppermute(value, ("dp", "mp"), pairs)


def rounded_sum(parts):
    total = parts[0].astype(F32)
    for part in parts[1:]:
        total += part.astype(F32)
    return total.astype(BF16)


def first_half(parts):
    half = parts[0].shape[0] // 2
    return rounded_sum([p[:half] for p in parts])


def second_halves(parts):
    half = parts[0].shape[0] // 2
    return [p[half:] for p in parts]


def scatter_rest(quarters):
    size = lax.axis_size("dp")
    groups = [[b + 4 * k for k in range(size // 4)] for b in range(4)]
    return lax.psum_scatter(quarters, "dp", scatter_dimension=0, axis_index_groups=groups, tiled=True)


def later_bits():
    return range(2, lax.axis_size("dp").bit_length() - 1)


def after(value, done):
    return lax.optimization_barrier((value, done))[0]


def block_orders():
    size = lax.axis_size("dp")
    me = lax.axis_index("dp")
    first_core = lax.axis_index("mp") == 0
    count = size.bit_length() - 1
    places = np.arange(size)
    results = []
    for halved in (2, count):
        flows = []
        for outer, inner in ((0, 1), (1, 0)):
            flipped = np.zeros(size, np.int32)
            for position, bit in enumerate((outer, inner, *range(2, halved))):
                flipped |= (1 - ((places >> (count - 1 - position)) & 1)).astype(np.int32) << bit
            if halved == 2:
                plain = (places % (size // 4)).astype(np.int32) * 4
                flows.append((jnp.asarray(flipped) ^ (me & 3)) | jnp.asarray(plain))
            else:
                flows.append(jnp.asarray(flipped) ^ me)
        results.append(jnp.where(first_core, flows[0], flows[1]).astype(jnp.int32))
    within = places % 4
    swapped = (within % 2) * 2 + within // 2
    flipped = jnp.where(first_core, jnp.asarray(3 - swapped), jnp.asarray(3 - within)) ^ (me & 3)
    last = ((places // 4) * 4 + flipped).astype(jnp.int32)
    return jnp.concatenate([results[0], last]), results[1]


def rotary_tables(slot_rows):
    half_dim = HEAD_DIM // 2
    frequency = (10000.0 ** (-(np.arange(half_dim) * 2.0 / HEAD_DIM))).astype(np.float32)
    within = np.arange(slot_rows)
    tables = []
    for window_half in range(2):
        for shift in (0, slot_rows // 2):
            tables.append((within + shift) % slot_rows + window_half * slot_rows)
    angles = np.concatenate(tables).astype(np.float32)[:, None] * frequency[None, :]
    angles = np.tile(angles.astype(np.float64), (1, 4))
    return np.cos(angles).astype(np.float32), np.sin(angles).astype(np.float32)


def local(
    inputs,
    first_gain,
    first_shift,
    query_weight,
    key_weight,
    value_weight,
    output_weight,
    second_gain,
    second_shift,
    gate_weight,
    up_weight,
    down_weight,
    cotangent,
    species_weight,
    species_ids,
    slot_bucket,
    slot_length,
):
    half_rows = inputs.shape[0]
    slot_rows = 2 * half_rows
    blocks = lax.axis_size("dp")
    core = lax.axis_index("mp")
    parity = lax.axis_index("dp") % 2
    joined = slot_bucket[0]
    length = slot_length[0]
    start = core * half_rows
    own_table = 2 * parity * joined + core
    far_table = 2 * (1 - parity) * joined + core
    info = jnp.stack([joined, length, start, own_table, far_table]).astype(jnp.int32)
    order, order_all = block_orders()
    tables = rotary_tables(slot_rows)
    units = gate_weight.shape[1]

    cot_other = swap(cotangent)
    output_weight_other = swap(output_weight)
    n1_own = norm_rows(inputs, first_gain, first_shift)
    n1_far_own = across(n1_own, 0)
    n1_other = swap(n1_own)
    q, k, v = project(info[3:4], n1_own, n1_other, (query_weight, key_weight, value_weight), *tables)
    earlier = attend(True, info, q, k, v)

    n1_far_own = after(n1_far_own, earlier[2])
    n1_far_other = swap(n1_far_own)
    token_index = (jnp.arange(slot_rows, dtype=jnp.int32) + start) % slot_rows
    table_index = jnp.arange(species_weight.shape[0], dtype=jnp.int32)
    slot_weight = jnp.sum(jnp.where(table_index == species_ids[0], species_weight, 0.0))
    token_weight = jnp.where(token_index < length, slot_weight, 0.0)[:, None]
    late_cot, late_other = after((cotangent, cot_other), earlier[2])
    d_branch = [
        (c.astype(F32) * w).astype(BF16)
        for c, w in ((late_cot, token_weight[:half_rows]), (late_other, token_weight[half_rows:]))
    ]
    k_far, v_far = project(
        after(info[4:5], d_branch), n1_far_own, n1_far_other, (key_weight, value_weight), *tables
    )
    context, context_give, log_total = attend(False, info, q, k_far, v_far, tuple(earlier))
    middle, n2_own = middle_rows(
        context, swap(context_give), output_weight, output_weight_other, inputs, second_gain, second_shift
    )
    rows_in = (n2_own, swap(n2_own), *d_branch)

    gated = (order, rows_in, gate_weight, up_weight, down_weight, blocks)
    near, off = (0, 1), (1, 0)
    hidden_1, d_n2_1, give_1, sent, parts_1, down_1 = gated_first(*gated, 0, units // 2)
    got_1 = exchange(sent, near)
    down_1 = scatter_rest(down_1)
    hidden_2, d_n2, give_2, sent, parts_2, down_2 = gated_units(*gated, units // 2, units, (d_n2_1,))
    got_2 = exchange(sent, near)
    down_2 = scatter_rest(down_2)
    d_middle, d_attended, second_sums = middle_back(
        info, slot_weight[None], (d_n2, swap(give_1), swap(give_2)), middle, cotangent, second_gain
    )
    d_attended_other = swap(d_attended)
    parts_1 = [parts_1, after(got_1, d_attended)]
    onward_1 = first_half(parts_1)
    again_1 = exchange(onward_1, off)

    d_context, dq_far, dk_far, dv_far, d_far_give, d_far, projected = attend_back_far(
        after(info, onward_1),
        order,
        q,
        k_far,
        v_far,
        context,
        log_total,
        tables,
        d_attended,
        d_attended_other,
        output_weight,
        key_weight,
        value_weight,
        blocks,
    )
    got_2, again_1 = after((got_2, again_1), dq_far)
    parts_2 = [parts_2, got_2]
    onward_2 = first_half(parts_2)
    again_2 = exchange(onward_2, off)
    kept_1 = rounded_sum([*second_halves(parts_1), again_1])
    gated_1 = scatter_rest(kept_1)
    d_far_got = after(swap(d_far_give), (kept_1, onward_2))
    d_far = rounded_sum([d_far, d_far_got])
    d_far_back = across(d_far, 0)
    parts_p = [projected[projected.shape[0] // 2 :]]
    got_p = exchange(after(projected[: projected.shape[0] // 2], d_far), near)

    d_n1_give, d_n1, sent, parts_3 = attend_back_own(
        after(info, (kept_1, onward_2, d_far)),
        order_all,
        q,
        k,
        v,
        context,
        log_total,
        tables,
        d_context,
        dq_far,
        (n1_own, n1_other, n1_far_own, n1_far_other),
        (dk_far, dv_far),
        (query_weight, key_weight, value_weight),
        blocks,
    )
    got_3 = exchange(sent, near)
    again_2, d_far_back, gated_1, down_1, down_2, got_p = after(
        (again_2, d_far_back, gated_1, down_1, down_2, got_p), parts_3
    )
    parts_p.append(got_p)
    onward_p = first_half(parts_p)
    again_p = exchange(onward_p, off)
    kept_2 = rounded_sum([*second_halves(parts_2), again_2])
    d_n1_got = after(swap(d_n1_give), (kept_2, onward_p))
    input_grad, first_sums = first_back(d_n1, d_n1_got, d_far_back, inputs, d_middle, first_gain)
    kept_p = rounded_sum([*second_halves(parts_p), after(again_p, first_sums)])
    gated_2 = scatter_rest(jnp.concatenate([kept_2, kept_p], 1))
    turned = [jnp.concatenate([down_1, after(down_2, first_sums)], 1)]
    turned_send = first_half(turned)
    turned_got = exchange(turned_send, near)
    sums = jnp.concatenate([first_sums[:2], second_sums[:2]], 0)
    sums += after(swap(sums), turned_send)
    branch_give, branch = rows_times(
        after(order, (turned_send, sums, kept_p)), ((hidden_1, down_weight, 0), (hidden_2, down_weight, 1)), NN
    )
    parts_3 = [parts_3, after(got_3, branch_give)]
    sent = first_half(parts_3)
    parts_3 = [*second_halves(parts_3), exchange(sent, off)]
    sums += after(across(sums, 0), sent)
    turned = [*second_halves(turned), after(turned_got, sent)]
    turned = [*second_halves(turned), exchange(first_half(turned), off)]
    parts_3 = after(parts_3, gated_2)
    *early, last_bit = later_bits()
    for bit in early:
        sent = first_half(parts_3)
        parts_3 = [*second_halves(parts_3), across(sent, bit)]
        sums += after(across(sums, bit - 1), sent)
    output = (middle + branch + swap(branch_give).astype(F32)).astype(BF16)
    gate_grad, up_grad, down_grad, project_grad = unpack_gated(gated_1, gated_2, rounded_sum(turned))
    parts_3 = after(parts_3, (output, gate_grad))
    sent = first_half(parts_3)
    parts_3 = [*second_halves(parts_3), across(sent, last_bit)]
    sums += after(across(sums, last_bit - 1), sent)
    norm_sums = sums + across(sums, last_bit)
    query_grad, key_grad, value_grad = unpack_rest(rounded_sum(parts_3))
    share = norm_sums.shape[1] // (2 * blocks)
    norm_sums = lax.dynamic_slice_in_dim(norm_sums, (2 * lax.axis_index("dp") + core) * share, share, 1)
    return (
        output,
        input_grad,
        norm_sums[0],
        norm_sums[1],
        query_grad,
        key_grad,
        value_grad,
        project_grad.T,
        norm_sums[2],
        norm_sums[3],
        gate_grad,
        up_grad,
        down_grad.T,
    )


def solution(mesh):
    rows = P(("dp", "mp"), None)
    in_specs = (
        rows,
        P(),
        P(),
        P(None, "mp"),
        P(None, "mp"),
        P(None, "mp"),
        P("mp", None),
        P(),
        P(),
        P(None, "mp"),
        P(None, "mp"),
        P("mp", None),
        rows,
        P(),
        P("dp"),
        P("dp"),
        P("dp"),
    )
    out_specs = (
        rows,
        rows,
        P(("dp", "mp")),
        P(("dp", "mp")),
        P("dp", "mp"),
        P("dp", "mp"),
        P("dp", "mp"),
        P("mp", "dp"),
        P(("dp", "mp")),
        P(("dp", "mp")),
        P("dp", "mp"),
        P("dp", "mp"),
        P("mp", "dp"),
    )
    return jax.shard_map(local, mesh=mesh, in_specs=in_specs, out_specs=out_specs, check_vma=False)
```
